32 devices in a mesh: blk: 4 (over y, x), batch: 8 (over z, core).
Axes of the slice: x: 2, y: 2, z: 4, core: 2. Of those that a mesh axis runs over, the one named last changes fastest.
Arguments:
- inputs: bfloat16 [32, 512, 768], P('batch', 'blk'), may hold values from -6 to 6
- lengths: int32 [32], P('batch'), may hold values from 64 to 512, as said below
- positions: int32 [32, 80], P('batch'), may hold values from 0 to 511, as said below
- counts: int32 [32], P('batch'), may hold values from 40 to 80, as said below
- token_ids: int32 [32, 80], P('batch'), may hold values from 0 to 15359
- table: bfloat16 [15360, 768], replicated, may hold values from -6 to 6
- w_query: bfloat16 [768, 768], replicated, may hold values from -0.3125 to 0.3125
- b_query: bfloat16 [768], replicated, may hold values from -1.75 to 1.75
- w_key: bfloat16 [768, 768], replicated, may hold values from -0.21875 to 0.21875
- w_value: bfloat16 [768, 768], replicated, may hold values from -0.21875 to 0.21875
- b_value: bfloat16 [768], replicated, may hold values from -0.625 to 0.625
- w_out: bfloat16 [768, 768], replicated, may hold values from -1.75 to 1.75
- b_out: bfloat16 [768], replicated, may hold values from -3 to 3
- gain_one: bfloat16 [768], replicated, may hold values from 0.5 to 1.5
- shift_one: bfloat16 [768], replicated, may hold values from -1.75 to 1.75
- w_up: bfloat16 [768, 3072], replicated, may hold values from -0.21875 to 0.21875
- b_up: bfloat16 [3072], replicated, may hold values from -3 to 3
- w_down: bfloat16 [3072, 768], replicated, may hold values from -0.109375 to 0.109375
- b_down: bfloat16 [768], replicated, may hold values from -3 to 3
- gain_two: bfloat16 [768], replicated, may hold values from 0.5 to 1.5
- shift_two: bfloat16 [768], replicated, may hold values from -1.75 to 1.75
- cotangent: bfloat16 [32, 512, 768], P('batch', 'blk'), may hold values from -8 to 8
Outputs:
- outputs: bfloat16 [32, 512, 768], P('batch', 'blk')
- d_inputs: bfloat16 [32, 512, 768], P('batch', 'blk')
- grad_query: float32 [768, 768], P('batch')
- grad_query_bias: float32 [768], P('batch')
- grad_key: float32 [768, 768], P('batch')
- grad_value: float32 [768, 768], P('batch')
- grad_value_bias: float32 [768], P('batch')
- grad_out: float32 [768, 768], P('batch')
- grad_out_bias: float32 [768], P('batch')
- grad_gain_one: float32 [768], P('batch')
- grad_shift_one: float32 [768], P('batch')
- grad_up: float32 [768, 3072], P('batch')
- grad_up_bias: float32 [3072], P('batch')
- grad_down: float32 [3072, 768], P('batch')
- grad_down_bias: float32 [768], P('batch')
- grad_gain_two: float32 [768], P('batch')
- grad_shift_two: float32 [768], P('batch')
The draws below stay inside these ranges and needn't reach their ends.
Inputs may be any that keep to these rules, and one draw needn't show every extreme that they name: `lengths`: in each group of 4 pages that one index of batch holds, at least one page has length 512. The 80 positions listed for a page are distinct; entries at or past the page's count are present but unused. `counts`: some page has exactly 80 masked positions.
All inputs are finite; a program needn't handle non-finite values.
Results may differ from the reference program's by a relative error of at most 0.02.
Values may be sent and summed in bfloat16 or wider, within the bound.
No kernel may reach another device: no remote copies, remote signals or barrier semaphores. Data moves between devices by JAX's collectives and lax.ppermute only.
A program may use at most 192 MiB of HBM per device.

```python
import jax
import jax.numpy as jnp
from jax import lax

D = 768
HEADS = 12
HD = 64
FF = 3072
VOCAB = 15360
PAGE = 512
MASKS = 80
PAGES_DEV = 4
PAGES = 32
N_BATCH = 8


def draw_lengths(key, part):
    key = jax.random.fold_in(key, 11)
    first_key, second_key = jax.random.split(key)
    base = jax.random.randint(first_key, (PAGES,), PAGE // 8, PAGE + 1, dtype=jnp.int32)
    chosen = jax.random.randint(second_key, (PAGES // PAGES_DEV,), 0, PAGES_DEV, dtype=jnp.int32)
    slot_index = jnp.arange(PAGES, dtype=jnp.int32) % PAGES_DEV
    full_page = jnp.repeat(chosen, PAGES_DEV, total_repeat_length=PAGES) == slot_index
    return jnp.where(full_page, PAGE, base).astype(jnp.int32)


def draw_positions(key, part):
    key = jax.random.fold_in(key, 23)
    page_keys = jax.random.split(key, PAGES)

    def one_page(page_key):
        return jax.random.permutation(page_key, PAGE)[:MASKS]
    return jax.vmap(one_page)(page_keys).astype(jnp.int32)


def draw_counts(key, part):
    key = jax.random.fold_in(key, 37)
    first_key, second_key = jax.random.split(key)
    base = jax.random.randint(first_key, (PAGES,), MASKS // 2, MASKS + 1, dtype=jnp.int32)
    chosen = jax.random.randint(second_key, (), 0, PAGES, dtype=jnp.int32)
    return jnp.where(jnp.arange(PAGES, dtype=jnp.int32) == chosen, MASKS, base).astype(jnp.int32)


def set_ends(values, rng, low, largest):
    shape = values.shape
    index_at = [jax.random.randint(jax.random.fold_in(rng, axis), (), 0, shape[axis]) for axis in range(len(shape))]
    values = values.at[tuple(index_at)].set(low)
    longest = shape.index(max(shape))
    index_at[longest] = (index_at[longest] + 1) % shape[longest]
    return values.at[tuple(index_at)].set(largest)


def raised(values, rng, source, target, shards_of, factor):
    def block_of(position):
        return (jnp.arange(values.shape[position]) // (values.shape[position] // shards_of)).reshape((-1,) + (1,) * (values.ndim - 1 - position))

    near = jax.random.permutation(rng, shards_of)[block_of(target)]
    second = (block_of(target) + shards_of // 2) % shards_of
    return jnp.where((block_of(source) == near) | (block_of(source) == second), factor * values, values)


def level_of(rng, dims, cuts, low, high):
    level, own = 1.0, jax.random.fold_in(rng, 6)
    for dim, shards_of in cuts:
        steps = jnp.exp(jax.random.uniform(jax.random.fold_in(own, dim), (shards_of,), jnp.float32, low / len(cuts), high / len(cuts)))
        level = level * jnp.repeat(steps, dims[dim] // shards_of).reshape([-1 if axis == dim else 1 for axis in range(len(dims))])
    return level


def noise(rng, dims, scale, most, shards=(), kind=jnp.bfloat16):
    factor_of = level_of(rng, dims, shards, -0.22, 0.18) if shards else 1.0
    values = jax.random.normal(rng, dims, jnp.float32) * scale * factor_of
    return jnp.minimum(jnp.maximum(values, -most), most).astype(kind)


def gaussian_with(key, dims, scale, bound, cuts, heavy, kind=jnp.bfloat16):
    drawn = scale * jax.random.normal(key, dims, jnp.float32)
    if cuts:
        drawn = drawn * level_of(key, dims, cuts, -0.22, 0.18)
    return jnp.clip(raised(drawn, jax.random.fold_in(key, 3), *heavy), -bound, bound).astype(kind)


def setup_inputs(seed: int = 0) -> dict:
    keys = jax.random.split(jax.random.key(seed), 23)
    return {
        "inputs": noise(keys[0], (PAGES, PAGE, D), 1.0, 6.0, ((0, 8), (1, 4))),
        "lengths": draw_lengths(jax.random.fold_in(keys[22], 71), 0),
        "positions": draw_positions(jax.random.fold_in(keys[22], 71), 0),
        "counts": draw_counts(jax.random.fold_in(keys[22], 71), 0),
        "token_ids": set_ends(jax.random.randint(keys[4], (PAGES, MASKS), 0, VOCAB), jax.random.fold_in(keys[4], 1), 0, VOCAB - 1).astype(jnp.int32),
        "table": noise(keys[5], (VOCAB, D), 1.0, 6.0),
        "w_query": noise(keys[6], (D, D), (D // 2) ** -0.5, 0.3125),
        "b_query": noise(keys[7], (D,), 0.3, 1.75),
        "w_key": noise(keys[8], (D, D), D ** -0.5, 0.21875),
        "w_value": noise(keys[9], (D, D), D ** -0.5, 0.21875),
        "b_value": noise(keys[10], (D,), 0.1, 0.625),
        "w_out": noise(keys[11], (D, D), (D // 64) ** -0.5, 1.75),
        "b_out": noise(keys[12], (D,), 0.5, 3.0),
        "gain_one": jnp.clip(1.0 + 0.1 * jax.random.normal(keys[13], (D,), jnp.float32), 0.5, 1.5).astype(jnp.bfloat16),
        "shift_one": noise(keys[14], (D,), 0.3, 1.75),
        "w_up": noise(keys[15], (D, FF), D ** -0.5, 0.21875),
        "b_up": noise(keys[16], (FF,), 0.5, 3.0),
        "w_down": noise(keys[17], (FF, D), FF ** -0.5, 0.109375),
        "b_down": noise(keys[18], (D,), 0.5, 3.0),
        "gain_two": jnp.clip(1.0 + 0.1 * jax.random.normal(keys[19], (D,), jnp.float32), 0.5, 1.5).astype(jnp.bfloat16),
        "shift_two": noise(keys[20], (D,), 0.3, 1.75),
        "cotangent": gaussian_with(keys[21], (PAGES, PAGE, D), 1.0, 8.0, ((0, 8), (1, 4)), (0, 2, 8, 2.0)),
    }


SCALE = 0.125
NEGATIVE = -1e+30
EPSILON = 1e-12
HIGHEST = lax.Precision.HIGHEST

@jax.custom_vjp
def low(v):
    return lax.optimization_barrier(v.astype(jnp.bfloat16)).astype(jnp.float32)

@jax.custom_vjp
def low_back(v):
    return v

def low_keep(v):
    return (low(v), None)

def low_pass(kept, grad):
    return (grad,)

def back_keep(v):
    return (v, None)

def back_low(kept, grad):
    return (low(grad),)
low.defvjp(low_keep, low_pass)
low_back.defvjp(back_keep, back_low)

def product(matrix_a, matrix_b):
    return jnp.dot(matrix_a, matrix_b, precision=HIGHEST, preferred_element_type=jnp.float32)

def normed(values, gain, shift):
    centre = lax.optimization_barrier(jnp.mean(values, axis=-1, keepdims=True))
    centred = values - centre
    spread = lax.optimization_barrier(jnp.mean(centred * centred, axis=-1, keepdims=True))
    return centred * lax.rsqrt(spread + EPSILON) * gain + shift

def attend(queries, keys_all, values_all, key_live):
    raw = low_back(jnp.einsum('gshd,gthd->ghst', queries, keys_all, precision=HIGHEST) * SCALE)
    masked = jnp.where(key_live[:, None, None, :], raw, NEGATIVE)
    row_max = lax.optimization_barrier(jnp.max(masked, axis=-1, keepdims=True))
    weights = jnp.exp(masked - row_max)
    weight_sum = lax.optimization_barrier(jnp.sum(weights, axis=-1))
    summed = low_back(jnp.einsum('ghst,gthd->ghsd', low(weights), values_all, precision=HIGHEST))
    return summed / weight_sum[..., None]

def layer(start_rows, key_live, params):
    w_query, b_query, w_key, w_value, b_value, w_out, b_out, gain_one, shift_one, w_up, b_up, w_down, b_down, gain_two, shift_two = params
    group_pages = start_rows.shape[0]
    flat_rows = start_rows.reshape(group_pages * PAGE, D)
    heads_shape = (group_pages, PAGE, HEADS, HD)
    queries = low_back(low(product(flat_rows, w_query) + b_query)).reshape(heads_shape)
    keys_all = low_back(low(product(flat_rows, w_key))).reshape(heads_shape)
    values_all = low_back(low(product(flat_rows, w_value) + b_value)).reshape(heads_shape)
    mixed_heads = attend(queries, keys_all, values_all, key_live)
    attended = low(mixed_heads.transpose(0, 2, 1, 3).reshape(group_pages * PAGE, D))
    branch = low_back(product(attended, w_out) + b_out)
    normed_one = normed(flat_rows + branch, gain_one, shift_one)
    hidden = low_back(product(low(normed_one), w_up) + b_up)
    active = low(jax.nn.gelu(hidden, approximate=False))
    down_out = low_back(product(active, w_down) + b_down)
    return normed(normed_one + down_out, gain_two, shift_two).reshape(start_rows.shape)

def replace_rows(rows_in, spots_in, used_counts, names, table):
    slot_numbers = jnp.arange(MASKS, dtype=jnp.int32)
    slot_live = slot_numbers[None, :] < used_counts[:, None]
    slot_hits = (spots_in[:, :, None] == jnp.arange(PAGE, dtype=jnp.int32)[None, None, :]) & slot_live[:, :, None]
    slot_of = lax.optimization_barrier(jnp.sum(slot_hits.astype(jnp.int32) * (slot_numbers + 1)[None, :, None], axis=1)).astype(jnp.int32) - 1
    replaced = slot_of >= 0
    ids_at = jnp.take_along_axis(names, jnp.maximum(slot_of, 0).astype(jnp.int32), axis=1)
    placed = jnp.take(table, ids_at, axis=0).astype(jnp.float32)
    return (jnp.where(replaced[..., None], placed, rows_in.astype(jnp.float32)), replaced)

def reference(inputs, lengths, positions, counts, token_ids, table, w_query, b_query, w_key, w_value, b_value, w_out, b_out, gain_one, shift_one, w_up, b_up, w_down, b_down, gain_two, shift_two, cotangent):
    params = tuple((weight.astype(jnp.float32) for weight in (w_query, b_query, w_key, w_value, b_value, w_out, b_out, gain_one, shift_one, w_up, b_up, w_down, b_down, gain_two, shift_two)))

    def grouped(array):
        return array.reshape((N_BATCH, PAGES_DEV) + array.shape[1:])

    def group_step(grad_sums, pieces):
        rows_in, sizes_in, spots_in, used_counts, names, back_in = pieces
        start_rows, replaced = replace_rows(rows_in, spots_in, used_counts, names, table)
        key_live = jnp.arange(PAGE, dtype=jnp.int32)[None, :] < sizes_in[:, None]

        def apply_layer(rows_now, weights_now):
            return layer(rows_now, key_live, weights_now)
        result, pull = jax.vjp(apply_layer, start_rows, params)
        d_rows, d_params = pull(back_in.astype(jnp.float32))
        d_start = jnp.where(replaced[..., None], 0.0, d_rows)
        grad_sums = tuple((total + part for total, part in zip(grad_sums, d_params)))
        return (grad_sums, (result.astype(jnp.bfloat16), d_start.astype(jnp.bfloat16)))
    zeros = tuple((jnp.zeros(weight.shape, jnp.float32) for weight in params))
    grad_sums, (outputs, d_inputs) = lax.scan(group_step, zeros, (grouped(inputs), grouped(lengths), grouped(positions), grouped(counts), grouped(token_ids), grouped(cotangent)))
    grad_query, grad_query_bias, grad_key, grad_value, grad_value_bias, grad_out, grad_out_bias, grad_gain_one, grad_shift_one, grad_up, grad_up_bias, grad_down, grad_down_bias, grad_gain_two, grad_shift_two = grad_sums
    return (outputs.reshape(inputs.shape), d_inputs.reshape(inputs.shape), grad_query, grad_query_bias, grad_key, grad_value, grad_value_bias, grad_out, grad_out_bias, grad_gain_one, grad_shift_one, grad_up, grad_up_bias, grad_down, grad_down_bias, grad_gain_two, grad_shift_two)
```

```python
import functools

import jax
import jax.numpy as jnp
from jax import lax
from jax.experimental import pallas as pl
from jax.experimental.pallas import tpu as pltpu
from jax.sharding import PartitionSpec as P

HEADS = 12
HD = 64
SCALE = 0.125
NEGATIVE = -1e30
EPSILON = 1e-12
BF = jnp.bfloat16
F32 = jnp.float32
MIB = 1024 * 1024


def nn(a, b):
    return lax.dot_general(a, b, (((1,), (0,)), ((), ())), preferred_element_type=F32)


def nt(a, b):
    return lax.dot_general(a, b, (((1,), (1,)), ((), ())), preferred_element_type=F32)


def tn(a, b):
    return lax.dot_general(a, b, (((0,), (0,)), ((), ())), preferred_element_type=F32)


def head_lanes(shape, which):
    lane = lax.broadcasted_iota(jnp.int32, shape, 1)
    return (lane >= HD) if which else (lane < HD)


def hits_of(pos_ref, count, rows, slots):
    spot = lax.broadcasted_iota(jnp.int32, (rows, slots), 0)
    slot = lax.broadcasted_iota(jnp.int32, (rows, slots), 1)
    return (pos_ref[...] == spot) & (slot < count)


def norm_parts(v):
    width = v.shape[-1]
    centre = jnp.sum(v, axis=-1, keepdims=True) * (1.0 / width)
    centred = v - centre
    spread = jnp.sum(centred * centred, axis=-1, keepdims=True) * (1.0 / width)
    rstd = lax.rsqrt(spread + EPSILON)
    return centred * rstd, rstd


def norm_back(c2, n, rstd):
    width = c2.shape[-1]
    a = jnp.sum(c2, axis=-1, keepdims=True) * (1.0 / width)
    b = jnp.sum(c2 * n, axis=-1, keepdims=True) * (1.0 / width)
    return (c2 - a - n * b) * rstd


def colsum(v):
    return jnp.sum(v, axis=0, keepdims=True)


def attend_kernel(
    info_ref, own_ref, p1_ref, p2_ref, p3_ref, pos_ref, fetched_ref,
    wq_ref, bq_ref, wk_ref, wv_ref, bv_ref, wo_ref, bo_ref,
    x_ref, q_ref, k_ref, v_ref, att_ref, max_ref, sum_ref, n_ref, rstd_ref,
    work_ref, att_rows,
):
    length, count, me = info_ref[0], info_ref[1], info_ref[2]
    rows, width = x_ref.shape
    span = own_ref.shape[0]
    for step, piece in enumerate((own_ref, p1_ref, p2_ref, p3_ref)):
        at = pl.multiple_of((me ^ step) * span, span)
        work_ref[pl.ds(at, span), :] = piece[...]
    hits = hits_of(pos_ref, count, rows, pos_ref.shape[1])
    onehot = hits.astype(F32)
    replaced = jnp.sum(onehot, axis=1, keepdims=True) > 0.5
    placed = nn(onehot.astype(BF), fetched_ref[...]).astype(BF)
    x = jnp.where(replaced, placed, work_ref[...])
    x_ref[...] = x
    q_ref[...] = ((nn(x, wq_ref[...]) + bq_ref[...]).astype(BF).astype(F32) * SCALE).astype(BF)
    k_ref[...] = nn(x, wk_ref[...]).astype(BF)
    v_ref[...] = (nn(x, wv_ref[...]) + bv_ref[...]).astype(BF)
    dead = jnp.where(lax.broadcasted_iota(jnp.int32, (rows, 1), 0) < length, 0.0, NEGATIVE)

    def pair(i, carry):
        lanes = pl.ds(pl.multiple_of(i * 2 * HD, 2 * HD), 2 * HD)
        q2, k2 = q_ref[:, lanes], k_ref[:, lanes]
        v2t = v_ref[:, lanes].T
        for h in range(2):
            qm = jnp.where(head_lanes(q2.shape, h), q2, jnp.zeros_like(q2))
            s = nt(k2, qm) + dead
            top = jnp.max(s, axis=0, keepdims=True)
            p = jnp.exp(s - top)
            total = jnp.sum(p, axis=0, keepdims=True)
            o = nn(v2t[h * HD:(h + 1) * HD], p.astype(BF)) / total
            max_ref[2 * i + h] = top
            sum_ref[2 * i + h] = total
            att_ref[pl.ds(pl.multiple_of(i * 2 * HD + h * HD, HD), HD), :] = o.astype(BF)
        att_rows[:, lanes] = att_ref[pl.ds(pl.multiple_of(i * 2 * HD, 2 * HD), 2 * HD), :].T
        return carry

    lax.fori_loop(0, HEADS // 2, pair, 0)
    branch = nn(att_rows[...], wo_ref[...]) + bo_ref[...]
    n, rstd = norm_parts(x_ref[...].astype(F32) + branch)
    n_ref[...] = n
    rstd_ref[...] = jnp.broadcast_to(rstd, rstd_ref.shape)


def gelu_both(v):
    e = jnp.exp(v * v * -0.5)
    t = 1.0 / (1.0 + 0.3275911 * 0.7071067811865476 * jnp.abs(v))
    poly = t * (0.5 * 0.254829592 + t * (0.5 * -0.284496736 + t * (0.5 * 1.421413741 + t * (0.5 * -1.453152027 + t * (0.5 * 1.061405429)))))
    tail = poly * e
    phi = jnp.where(v >= 0, 1.0 - tail, tail)
    return v * phi, phi + v * (e * 0.3989422804014327)


def ff_kernel(
    packed, shares, info_ref, n_ref, rstd_ref, att_ref, sum_ref,
    c0_ref, c1_ref, c2_ref, c3_ref,
    wu_ref, bu_ref, wd_ref, bd_ref, wo_ref, g1_ref, s1_ref, g2_ref, s2_ref,
    out_ref, gdu_ref, go_ref, dr_ref, dst_ref, delta_ref,
    bd_out, bu_out, bo_out, gg1_ref, gs1_ref, gg2_ref, gs2_ref,
    act, slope, dh, cot, nlow, nlow_t, dd, dfirst,
):
    rows, width = n_ref.shape
    ff = wu_ref.shape[1]
    step = 512
    span = c0_ref.shape[0]
    me, core = info_ref[2], info_ref[3]
    for hop, piece in enumerate((c0_ref, c1_ref, c2_ref, c3_ref)):
        at = pl.multiple_of((me ^ hop) * span, span)
        cot[pl.ds(at, span), :] = piece[...]
    normed = n_ref[...] * g1_ref[...] + s1_ref[...]
    nlow[...] = normed.astype(BF)
    nlow_t[...] = nlow[...].T

    def up(i, carry):
        lanes = pl.ds(pl.multiple_of(i * step, step), step)
        h = nn(nlow[...], wu_ref[:, lanes]) + bu_ref[:, lanes]
        a, b = gelu_both(h)
        act[:, lanes] = a.astype(BF)
        slope[:, lanes] = b.astype(BF)
        return carry

    lax.fori_loop(0, ff // step, up, 0)
    resid = n_ref[...] * g1_ref[...] + s1_ref[...] + nn(act[...], wd_ref[...]) + bd_ref[...]
    n2, rstd2 = norm_parts(resid)
    out_ref[...] = (n2 * g2_ref[...] + s2_ref[...]).astype(BF)
    c = cot[...].astype(F32)
    gg2_ref[...] = colsum(c * n2)
    gs2_ref[...] = colsum(c)
    d_r2 = norm_back(c * g2_ref[...], n2, rstd2)
    dfirst[...] = d_r2
    dd[...] = d_r2.astype(BF)
    bd_out[...] = colsum(dd[...].astype(F32))

    def back(i, carry):
        lanes = pl.ds(pl.multiple_of(i * width, width), width)
        g_down = tn(act[:, lanes], dd[...]).astype(BF)
        dhc = (nt(dd[...], wd_ref[lanes, :]) * slope[:, lanes].astype(F32)).astype(BF)
        dh[:, lanes] = dhc
        bu_out[:, lanes] = colsum(dhc.astype(F32))
        g_up = nn(nlow_t[...], dhc).astype(BF)
        if packed:
            unit = width // shares
            for c in range(2):
                for p in range(4):
                    at = (c * 4 + p) * unit
                    gdu_ref[c ^ core, p, i, 0] = g_down[at:at + unit]
                for z in range(shares // 2):
                    at = (2 * z + c) * unit
                    gdu_ref[c ^ core, i, z, 1] = g_up[at:at + unit]
        else:
            gdu_ref[0, lanes, :] = g_down
            gdu_ref[1, lanes, :] = g_up
        return carry

    lax.fori_loop(0, ff // width, back, 0)
    d_f = dfirst[...] + nt(dh[...], wu_ref[...])
    n1 = n_ref[...]
    gg1_ref[...] = colsum(d_f * n1)
    gs1_ref[...] = colsum(d_f)
    d_r1 = norm_back(d_f * g1_ref[...], n1, rstd_ref[:, 0:1])
    dr_ref[...] = d_r1
    db = d_r1.astype(BF)
    dd[...] = db
    bo_out[...] = colsum(db.astype(F32))
    go_ref[...] = nn(att_ref[...], dd[...]).astype(BF)
    for i in range(HEADS):
        at = slice(i * HD, (i + 1) * HD)
        dm = nt(wo_ref[at, :], dd[...])
        inv = 1.0 / sum_ref[i]
        delta_ref[i] = colsum(dm * att_ref[at, :].astype(F32)) * inv
        dst_ref[at, :] = (dm * inv).astype(BF)


def back_kernel(
    packed, shares, info_ref, pos_ref, x_ref, q_ref, k_ref, v_ref, dst_ref, delta_ref, max_ref, dr_ref, go_ref,
    wq_ref, wk_ref, wv_ref,
    ga_ref, bq_out, bv_out, din_ref,
    x_t, dq, dk, dv,
):
    length, count = info_ref[0], info_ref[1]
    rows, width = x_ref.shape
    x_t[...] = x_ref[...].T
    dead = jnp.where(lax.broadcasted_iota(jnp.int32, (rows, 1), 0) < length, 0.0, NEGATIVE)

    def pair(i, carry):
        at = pl.multiple_of(i * 2 * HD, 2 * HD)
        lanes = pl.ds(at, 2 * HD)
        q2, k2, v2 = q_ref[:, lanes], k_ref[:, lanes], v_ref[:, lanes]
        dst = dst_ref[pl.ds(at, 2 * HD), :]
        ds2 = dst.T
        k2t = k2.T
        dv2 = jnp.zeros((rows, 2 * HD), F32)
        dk2 = jnp.zeros((rows, 2 * HD), F32)
        dqs = []
        for h in range(2):
            live = head_lanes(q2.shape, h)
            zero = jnp.zeros_like(q2)
            qm = jnp.where(live, q2, zero)
            s = nt(k2, qm) + dead
            p = jnp.exp(s - max_ref[2 * i + h])
            dp = nn(jnp.where(live, v2, zero), dst)
            dsc = (p * (dp - delta_ref[2 * i + h])).astype(BF)
            dv2 = dv2 + nn(p.astype(BF), jnp.where(live, ds2, zero))
            dk2 = dk2 + nn(dsc, qm)
            dqs.append(nn(k2t[h * HD:(h + 1) * HD], dsc))
        dq[:, lanes] = (jnp.concatenate(dqs, axis=0) * SCALE).astype(BF).T
        dk[:, lanes] = dk2.astype(BF)
        dv[:, lanes] = dv2.astype(BF)
        return carry

    lax.fori_loop(0, HEADS // 2, pair, 0)
    bq_out[...] = colsum(dq[...].astype(F32))
    bv_out[...] = colsum(dv[...].astype(F32))
    core = info_ref[3]
    for i, part in enumerate((dq, dk, dv, None)):
        g = go_ref[...] if part is None else nn(x_t[...], part[...]).astype(BF)
        if packed:
            unit = width // shares
            for b in range(shares):
                ga_ref[(b % 2) ^ core, i, b // 2] = g[b * unit:(b + 1) * unit]
        else:
            ga_ref[i] = g
    total = dr_ref[...] + nt(dq[...], wq_ref[...]) + nt(dk[...], wk_ref[...]) + nt(dv[...], wv_ref[...])
    hits = hits_of(pos_ref, count, rows, pos_ref.shape[1]).astype(F32)
    replaced = jnp.sum(hits, axis=1, keepdims=True) > 0.5
    din_ref[...] = jnp.where(replaced, 0.0, total).astype(BF)


VM = pl.BlockSpec(memory_space=pltpu.VMEM)
SM = pl.BlockSpec(memory_space=pltpu.SMEM)


def call(kernel, args, outs, scratch, flops):
    moved = sum(a.size * a.dtype.itemsize for a in args)
    return pl.pallas_call(
        kernel,
        out_shape=[jax.ShapeDtypeStruct(s, d) for s, d in outs],
        in_specs=[SM] + [VM] * (len(args) - 1),
        out_specs=[VM] * len(outs),
        scratch_shapes=[pltpu.VMEM(s, d) for s, d in scratch],
        compiler_params=pltpu.CompilerParams(vmem_limit_bytes=60 * MIB),
        cost_estimate=pl.CostEstimate(flops=flops, bytes_accessed=moved, transcendentals=0),
    )(*args)


def attend(info, pieces, pos, fetched, wq, bq, wk, wv, bv, wo, bo):
    span, width = pieces[0].shape
    rows = 4 * span
    args = (info, *pieces, pos, fetched, wq, bq, wk, wv, bv, wo, bo)
    outs = [((rows, width), BF)] * 4 + [((width, rows), BF), ((HEADS, 1, rows), F32), ((HEADS, 1, rows), F32), ((rows, width), F32), ((rows, 128), F32)]
    flops = 8 * rows * width * width + 4 * rows * rows * width * 4
    return call(attend_kernel, args, outs, [((rows, width), BF)] * 2, flops)


def feed(packed, shares, info, n, rstd, att, sums, pieces, wu, bu, wd, bd, wo, g1, s1, g2, s2):
    rows, width = n.shape
    ff = wu.shape[1]
    args = (info, n, rstd, att, sums, *pieces, wu, bu, wd, bd, wo, g1, s1, g2, s2)
    gdu = (2, 4, shares // 2, 2, width // shares, width) if packed else (2, ff, width)
    outs = [((rows, width), BF), (gdu, BF), ((width, width), BF), ((rows, width), F32), ((width, rows), BF), ((HEADS, 1, rows), F32)]
    outs += [((1, width), F32), ((1, ff), F32)] + [((1, width), F32)] * 5
    scratch = [((rows, ff), BF)] * 3 + [((rows, width), BF)] * 2 + [((width, rows), BF), ((rows, width), BF), ((rows, width), F32)]
    flops = 12 * rows * width * ff + 4 * rows * width * width
    return call(functools.partial(ff_kernel, packed, shares), args, outs, scratch, flops)


def back(packed, shares, info, pos, x, q, k, v, dst, delta, tops, dr, go, wq, wk, wv):
    rows, width = x.shape
    args = (info, pos, x, q, k, v, dst, delta, tops, dr, go, wq, wk, wv)
    ga = (2, 4, shares // 2, width // shares, width) if packed else (4, width, width)
    outs = [(ga, BF)] + [((1, width), F32)] * 2 + [((rows, width), BF)]
    scratch = [((width, rows), BF)] + [((rows, width), BF)] * 3
    flops = 12 * rows * width * width + 10 * rows * rows * width * 4
    return call(functools.partial(back_kernel, packed, shares), args, outs, scratch, flops)


def pick(array, index):
    return lax.dynamic_index_in_dim(array, index, 0, keepdims=False)


def swap(array, bit):
    return lax.ppermute(array, "blk", [(i, i ^ bit) for i in range(lax.axis_size("blk"))])


def swap_first(array, first):
    blks, shares = lax.axis_size("blk"), lax.axis_size("batch")
    perm = []
    for b in range(blks):
        for s in range(shares):
            bit = 1 if (s % 2 == 0) == first else 2
            perm.append((b * shares + s, (b ^ bit) * shares + s))
    return lax.ppermute(array, ("blk", "batch"), perm)


def swap_batch(array, bit):
    return lax.ppermute(array, "batch", [(i, i ^ bit) for i in range(lax.axis_size("batch"))])


def added(a, b):
    return (a.astype(F32) + b.astype(F32)).astype(BF)


def halve(data, mine, move):
    return added(pick(data, mine), move(pick(data, 1 - mine)))


def joined(own, other, mine):
    return jnp.where(mine == 0, jnp.stack([own, other]), jnp.stack([other, own]))


def reduce_all(packed, where):
    blk, share, core = where
    shares = lax.axis_size("batch")
    x_bit, y_bit = blk % 2, blk // 2
    hi = jnp.where(core == 0, x_bit, y_bit)
    lo = jnp.where(core == 0, y_bit, x_bit)
    data = added(packed[0], swap_batch(packed[1], 1))
    data = halve(data.reshape((2, 2) + data.shape[1:]), hi, lambda v: swap_first(v, True))
    data = halve(data, lo, lambda v: swap_first(v, False))
    bit = 2
    while bit < shares:
        data = data.reshape((data.shape[0] // 2, 2) + data.shape[1:])
        mine = (share // bit) % 2
        data = added(
            lax.dynamic_index_in_dim(data, mine, 1, keepdims=False),
            swap_batch(lax.dynamic_index_in_dim(data, 1 - mine, 1, keepdims=False), bit),
        )
        bit *= 2
    data = data[0]
    data = joined(data, swap_first(data, False), lo)
    data = joined(data, swap_first(data, True), hi)
    return data.reshape((4,) + data.shape[2:])


def body(
    inputs, lengths, positions, counts, token_ids, table,
    w_query, b_query, w_key, w_value, b_value, w_out, b_out, gain_one, shift_one,
    w_up, b_up, w_down, b_down, gain_two, shift_two, cotangent,
):
    blk, share = lax.axis_index("blk"), lax.axis_index("batch")
    shares = lax.axis_size("batch")
    core = share % 2
    where = (blk, share, core)
    pages, span, width = inputs.shape
    ff = w_up.shape[1]
    unit = width // shares
    packed = shares == 8
    info = jnp.stack([pick(lengths, blk), pick(counts, blk), blk, core]).astype(jnp.int32)
    rows_in = [pick(inputs, blk)] + [swap(pick(inputs, blk ^ i), i) for i in range(1, pages)]
    back_in = [pick(cotangent, blk)] + [swap(pick(cotangent, blk ^ i), i) for i in range(1, pages)]
    slots = positions.shape[1]
    pos = jnp.pad(pick(positions, blk), (0, 128 - slots), constant_values=-1).reshape(1, 128)
    fetched = jnp.take(table, jnp.pad(pick(token_ids, blk), (0, 128 - slots)), axis=0)

    def row(v):
        return v.astype(F32).reshape(1, -1)

    x, q, k, v, att, tops, sums, n1, rstd = attend(
        info, rows_in, pos, fetched, w_query, row(b_query), w_key, w_value, row(b_value), w_out, row(b_out)
    )
    (out_page, gdu, g_out, d_r1, dst, delta, v_down, v_up, v_out, v_gain1, v_shift1, v_gain2, v_shift2) = feed(
        packed, shares, info, n1, rstd, att, sums, back_in, w_up, row(b_up), w_down, row(b_down), w_out,
        row(gain_one), row(shift_one), row(gain_two), row(shift_two),
    )
    ga, v_query, v_value, d_page = back(
        packed, shares, info, pos, x, q, k, v, dst, delta, tops, d_r1, g_out, w_query, w_key, w_value
    )

    def to_pages(page):
        parts = page.reshape(pages, span, width)
        result = jnp.zeros_like(parts)
        for i in range(pages):
            part = pick(parts, blk ^ i)
            part = part if i == 0 else swap(part, i)
            result = lax.dynamic_update_index_in_dim(result, part, blk ^ i, 0)
        return result

    outputs = to_pages(out_page)
    d_inputs = to_pages(d_page)
    if not packed:
        down = gdu[0].reshape(shares // 2, 2, 4, unit, width).transpose(1, 2, 0, 3, 4)
        up = gdu[1].reshape(4, shares // 2, 2, unit, width).transpose(2, 0, 1, 3, 4)
        gdu = jnp.stack([down, up], axis=3)
        ga = ga.reshape(4, shares // 2, 2, unit, width).transpose(2, 0, 1, 3, 4)
        gdu = jnp.where(core == 0, gdu, gdu[::-1])
        ga = jnp.where(core == 0, ga, ga[::-1])
    du = reduce_all(gdu, where).astype(F32)
    grads = reduce_all(ga, where).astype(F32)
    grad_down = du[:, 0].reshape(ff // shares, width)
    grad_up = du[:, 1].transpose(1, 0, 2).reshape(unit, ff)
    grad_query, grad_key, grad_value, grad_out = (grads[i] for i in range(4))
    vectors = [v_query, v_value, v_out, v_gain1, v_shift1, v_up, v_down, v_gain2, v_shift2]
    stacked = jnp.concatenate([u.reshape(shares, -1) for u in vectors], axis=1)
    mine = pick(lax.psum(stacked, ("blk", "batch")), share)
    sizes = [u.size // shares for u in vectors]
    cuts = [sum(sizes[:i]) for i in range(len(sizes) + 1)]
    r = [mine[cuts[i]:cuts[i + 1]] for i in range(len(sizes))]
    return (
        outputs, d_inputs, grad_query, r[0], grad_key, grad_value, r[1], grad_out, r[2],
        r[3], r[4], grad_up, r[5], grad_down, r[6], r[7], r[8],
    )


def solution(mesh):
    split, whole = P("batch", "blk", None), P()
    rows, vec = P("batch", None), P("batch")
    in_specs = (split, vec, rows, vec, rows) + (whole,) * 16 + (split,)
    out_specs = (split, split, rows, vec, rows, rows, vec, rows, vec, vec, vec, rows, vec, rows, vec, vec, vec)
    return jax.shard_map(body, mesh=mesh, in_specs=in_specs, out_specs=out_specs, check_vma=False)
```

```python
import functools

import jax
import jax.numpy as jnp
from jax import lax
from jax.experimental import pallas as pl
from jax.experimental.pallas import tpu as pltpu
from jax.sharding import PartitionSpec as P

HEADS = 12
HD = 64
SCALE = 0.125
NEGATIVE = -1e30
EPSILON = 1e-12
BF = jnp.bfloat16
F32 = jnp.float32
MIB = 1024 * 1024
GROUP = 16
PARTS = 8
B_QUERY, B_VALUE, B_OUT, B_DOWN, GAIN_ONE, SHIFT_ONE, GAIN_TWO, SHIFT_TWO, B_UP = range(9)


def nn(a, b):
    return lax.dot_general(a, b, (((1,), (0,)), ((), ())), preferred_element_type=F32)


def nt(a, b):
    return lax.dot_general(a, b, (((1,), (1,)), ((), ())), preferred_element_type=F32)


def tn(a, b):
    return lax.dot_general(a, b, (((0,), (0,)), ((), ())), preferred_element_type=F32)


def head_lanes(shape, which):
    lane = lax.broadcasted_iota(jnp.int32, shape, 1)
    return (lane >= HD) if which else (lane < HD)


def norm_parts(v):
    width = v.shape[-1]
    centre = jnp.sum(v, axis=-1, keepdims=True) * (1.0 / width)
    centred = v - centre
    spread = jnp.sum(centred * centred, axis=-1, keepdims=True) * (1.0 / width)
    rstd = lax.rsqrt(spread + EPSILON)
    return centred * rstd, rstd


def norm_back(c2, n, rstd):
    width = c2.shape[-1]
    a = jnp.sum(c2, axis=-1, keepdims=True) * (1.0 / width)
    b = jnp.sum(c2 * n, axis=-1, keepdims=True) * (1.0 / width)
    return (c2 - a - n * b) * rstd


def colsum(v):
    return jnp.sum(v, axis=0, keepdims=True)


def wide_row(ref):
    return ref[...].astype(F32).reshape(1, ref.shape[0])


def block(i, size):
    return pl.ds(pl.multiple_of(i * size, size), size)


def own_blk():
    return lax.axis_index("blk")


def own_core():
    return lax.rem(lax.axis_index("batch"), 2)


def first_bit():
    return jnp.where(own_core() == 0, lax.rem(own_blk(), 2), lax.div(own_blk(), 2))


def second_bit():
    return jnp.where(own_core() == 0, lax.div(own_blk(), 2), lax.rem(own_blk(), 2))


def z_bits():
    z = lax.div(lax.axis_index("batch"), 2)
    return lax.rem(z, 2), lax.div(z, 2)


def fetch_kernel(ids_ref, counts_ref, spots_ref, table_ref, placed_ref, hit_ref, rows_ref, wide_ref, sel_ref, sem):
    slots = ids_ref.shape[1]
    me = own_blk()

    def start(j, carry):
        group = pl.multiple_of((ids_ref[me, j] // GROUP) * GROUP, GROUP)
        pltpu.make_async_copy(table_ref.at[pl.ds(group, GROUP), :], rows_ref.at[block(j, GROUP), :], sem).start()
        return carry

    lax.fori_loop(0, slots, start, 0, unroll=8)
    total = placed_ref.shape[0]
    spot = lax.broadcasted_iota(jnp.int32, (total, slots), 0)
    slot = lax.broadcasted_iota(jnp.int32, (total, slots), 1)
    hits = ((spots_ref[pl.ds(me, 1), :] == spot) & (slot < counts_ref[me])).astype(F32)
    hit_ref[...] = jnp.broadcast_to(jnp.sum(hits, axis=1, keepdims=True), hit_ref.shape)
    pltpu.make_async_copy(table_ref.at[pl.ds(0, slots * GROUP), :], rows_ref, sem).wait()
    wide_ref[...] = rows_ref[...].astype(F32)
    for j in range(slots):
        at = j * GROUP + lax.rem(ids_ref[me, j], GROUP)
        sel_ref[pl.ds(j, 1), :] = wide_ref[pl.ds(at, 1), :]
    placed_ref[...] = nn(hits.astype(BF), sel_ref[...].astype(BF)).astype(BF)


def attend_kernel(
    lengths_ref, inputs_ref, p1_ref, p2_ref, p3_ref, placed_ref, hit_ref, bq_ref, bv_ref, bo_ref,
    wq_ref, wk_ref, wv_ref, wo_ref,
    x_ref, q_ref, k_ref, v_ref, att_ref, max_ref, sum_ref, n_ref, rstd_ref,
    att_rows,
):
    me = own_blk()
    length = lengths_ref[me]
    rows, width = x_ref.shape
    span = p1_ref.shape[0]
    for step, piece in enumerate((inputs_ref[me], p1_ref[...], p2_ref[...], p3_ref[...])):
        at = block(me ^ step, span)
        x_ref[at, :] = jnp.where(hit_ref[at, 0:1] > 0.5, placed_ref[at, :], piece)
    q = (nn(x_ref[...], wq_ref[...]) + wide_row(bq_ref)).astype(BF)
    q_ref[...] = (q.astype(F32) * SCALE).astype(BF)
    k_ref[...] = nn(x_ref[...], wk_ref[...]).astype(BF)
    v_ref[...] = (nn(x_ref[...], wv_ref[...]) + wide_row(bv_ref)).astype(BF)
    dead = jnp.where(lax.broadcasted_iota(jnp.int32, (rows, 1), 0) < length, 0.0, NEGATIVE)

    def pair(i, carry):
        lanes = block(i, 2 * HD)
        q2, k2 = q_ref[:, lanes], k_ref[:, lanes]
        v2t = v_ref[:, lanes].T
        for h in range(2):
            qm = jnp.where(head_lanes(q2.shape, h), q2, jnp.zeros_like(q2))
            s = nt(k2, qm) + dead
            top = jnp.max(s, axis=0, keepdims=True)
            p = jnp.exp(s - top)
            total = jnp.sum(p, axis=0, keepdims=True)
            o = nn(v2t[h * HD:(h + 1) * HD], p.astype(BF)) / total
            max_ref[2 * i + h] = top
            sum_ref[2 * i + h] = total
            att_ref[block(2 * i + h, HD), :] = o.astype(BF)
        att_rows[:, lanes] = att_ref[lanes, :].T
        return carry

    lax.fori_loop(0, HEADS // 2, pair, 0)
    branch = nn(att_rows[...], wo_ref[...]) + wide_row(bo_ref)
    n, rstd = norm_parts(x_ref[...].astype(F32) + branch)
    n_ref[...] = n
    rstd_ref[...] = jnp.broadcast_to(rstd, rstd_ref.shape)


def gelu_both(v):
    e = jnp.exp(v * v * -0.5)
    t = 1.0 / (1.0 + (0.3275911 * 0.7071067811865476) * jnp.abs(v))
    poly = t * (0.5 * 0.254829592 + t * (0.5 * -0.284496736 + t * (0.5 * 1.421413741 + t * (0.5 * -1.453152027 + t * (0.5 * 1.061405429)))))
    tail = poly * e
    phi = jnp.where(v >= 0, 1.0 - tail, tail)
    return v * phi, phi + v * (e * 0.3989422804014327)


def by_core(core, keep, send, parity, index, value):
    @pl.when(core == parity)
    def _():
        keep[index] = value

    @pl.when(core != parity)
    def _():
        send[index] = value


def ff_kernel(
    n_ref, rstd_ref, att_ref, sum_ref,
    cot_ref, c1_ref, c2_ref, c3_ref,
    bu_ref, bd_ref, g1_ref, s1_ref, g2_ref, s2_ref,
    wu_ref, wd_ref, wo_ref,
    out_ref, dkeep, dsend, ukeep, usend, dr_ref, dst_ref, delta_ref, vsum_ref,
    act, slope, cot, nlow, nlow_t, dd, dfirst,
):
    rows, width = n_ref.shape
    ff = wu_ref.shape[1]
    parts = ff // width
    shares = 2 * dkeep.shape[1]
    unit = width // shares
    span = c1_ref.shape[0]
    me, core = own_blk(), own_core()
    for hop, piece in enumerate((cot_ref[me], c1_ref[...], c2_ref[...], c3_ref[...])):
        cot[block(me ^ hop, span), :] = piece
    normed = n_ref[...] * wide_row(g1_ref) + wide_row(s1_ref)
    nlow[...] = normed.astype(BF)
    nlow_t[...] = nlow[...].T
    for i in range(parts):
        lanes = slice(i * width, (i + 1) * width)
        a, b = gelu_both(nn(nlow[...], wu_ref[:, lanes]) + wide_row(bu_ref)[:, lanes])
        act[:, lanes] = a.astype(BF)
        slope[:, lanes] = b.astype(BF)
    normed = n_ref[...] * wide_row(g1_ref) + wide_row(s1_ref)
    resid = normed + nn(act[...], wd_ref[...]) + wide_row(bd_ref)
    n2, rstd2 = norm_parts(resid)
    out_ref[...] = (n2 * wide_row(g2_ref) + wide_row(s2_ref)).astype(BF)
    c = cot[...].astype(F32)
    vsum_ref[...] = jnp.zeros_like(vsum_ref)
    vsum_ref[GAIN_TWO:GAIN_TWO + 1] = colsum(c * n2)
    vsum_ref[SHIFT_TWO:SHIFT_TWO + 1] = colsum(c)
    d_r2 = norm_back(c * wide_row(g2_ref), n2, rstd2)
    dfirst[...] = d_r2
    dd[...] = d_r2.astype(BF)
    vsum_ref[B_DOWN:B_DOWN + 1] = colsum(dd[...].astype(F32))

    def back(i, carry):
        lanes = block(i, width)
        g_down = tn(act[:, lanes], dd[...]).astype(BF)
        for c in range(2):
            for p in range(4):
                at = (c * 4 + p) * unit
                by_core(core, dkeep, dsend, c, (p, i), g_down[at:at + unit])
        dhc = (nt(dd[...], wd_ref[lanes, :]) * slope[:, lanes].astype(F32)).astype(BF)
        act[:, lanes] = dhc
        vsum_ref[pl.ds(B_UP + i, 1)] = colsum(dhc.astype(F32))
        g_up = nn(nlow_t[...], dhc).astype(BF)
        for c in range(2):
            for z in range(shares // 2):
                at = (2 * z + c) * unit
                by_core(core, ukeep, usend, c, (i, z, slice(0, unit)), g_up[at:at + unit])
        return carry

    lax.fori_loop(0, parts, back, 0)
    d_f = dfirst[...] + nt(act[...], wu_ref[...])
    n1 = n_ref[...]
    vsum_ref[GAIN_ONE:GAIN_ONE + 1] = colsum(d_f * n1)
    vsum_ref[SHIFT_ONE:SHIFT_ONE + 1] = colsum(d_f)
    d_r1 = norm_back(d_f * wide_row(g1_ref), n1, rstd_ref[:, 0:1])
    dr_ref[...] = d_r1
    db = d_r1.astype(BF)
    dd[...] = db
    vsum_ref[B_OUT:B_OUT + 1] = colsum(db.astype(F32))
    g_out = nn(att_ref[...], dd[...]).astype(BF)
    for b in range(shares):
        for g in range(unit // GROUP):
            p, at = (g // 2, g % 2) if g < 4 else (g - 2, 0)
            index = (p, b // 2, slice(unit + at * GROUP, unit + (at + 1) * GROUP))
            by_core(core, ukeep, usend, b % 2, index, g_out[b * unit + g * GROUP:b * unit + (g + 1) * GROUP])
    for p in (2, 3):
        for z in range(shares // 2):
            for ref in (ukeep, usend):
                ref[p, z, unit + GROUP:unit + 2 * GROUP] = jnp.zeros((GROUP, width), BF)
    for i in range(HEADS):
        at = slice(i * HD, (i + 1) * HD)
        dm = nt(wo_ref[at, :], dd[...])
        inv = 1.0 / sum_ref[i]
        delta_ref[i] = colsum(dm * att_ref[at, :].astype(F32)) * inv
        dst_ref[at, :] = (dm * inv).astype(BF)


def heads_kernel(first, lengths_ref, q_ref, k_ref, v_ref, dst_ref, delta_ref, max_ref, dq, dk, dv):
    length = lengths_ref[own_blk()]
    rows = q_ref.shape[0]
    dead = jnp.where(lax.broadcasted_iota(jnp.int32, (rows, 1), 0) < length, 0.0, NEGATIVE)

    def pair(i, carry):
        lanes, own = block(first + i, 2 * HD), block(i, 2 * HD)
        q2, k2, v2 = q_ref[:, lanes], k_ref[:, lanes], v_ref[:, lanes]
        dst = dst_ref[lanes, :]
        ds2 = dst.T
        k2t = k2.T
        dv2 = jnp.zeros((rows, 2 * HD), F32)
        dk2 = jnp.zeros((rows, 2 * HD), F32)
        dqs = []
        for h in range(2):
            live = head_lanes(q2.shape, h)
            zero = jnp.zeros_like(q2)
            qm = jnp.where(live, q2, zero)
            s = nt(k2, qm) + dead
            head = 2 * (first + i) + h
            p = jnp.exp(s - max_ref[head])
            dp = nn(jnp.where(live, v2, zero), dst)
            dsc = (p * (dp - delta_ref[head])).astype(BF)
            dv2 = dv2 + nn(p.astype(BF), jnp.where(live, ds2, zero))
            dk2 = dk2 + nn(dsc, qm)
            dqs.append(nn(k2t[h * HD:(h + 1) * HD], dsc))
        dq[:, own] = (jnp.concatenate(dqs, axis=0) * SCALE).astype(BF).T
        dk[:, own] = dk2.astype(BF)
        dv[:, own] = dv2.astype(BF)
        return carry

    lax.fori_loop(0, dq.shape[1] // (2 * HD), pair, 0)


def grads_kernel(groups, x_ref, vin_ref, *refs):
    parts = [refs[3 * g:3 * g + 3] for g in range(groups)]
    keep, send_low, send_high, x_t = refs[3 * groups:]
    core = own_core()
    rows, width = x_ref.shape
    x_t[...] = x_ref[...].T
    shares = 2 * keep.shape[1]
    unit = width // shares
    tall = keep.shape[2]
    bias = []
    for i in range(3):
        at_lane = 0
        sums = []
        for part in parts:
            wide = part[i].shape[1]
            lanes = slice(at_lane, at_lane + wide)
            at_lane += wide
            g = nn(x_t[...], part[i][...]).astype(BF)
            sums.append(colsum(part[i][...].astype(F32)))
            for b in range(shares):
                for j in range(unit // GROUP):
                    at = i * unit + j * GROUP
                    p, value = at // tall, g[b * unit + j * GROUP:b * unit + (j + 1) * GROUP]
                    index = (b // 2, slice(at % tall, at % tall + GROUP), lanes)

                    @pl.when(core == b % 2)
                    def _():
                        keep[(p,) + index] = value

                    @pl.when(core != b % 2)
                    def _():
                        (send_low, send_high)[p // 2][(p % 2,) + index] = value

        bias.append(jnp.concatenate(sums, axis=1))
    vsum = vin_ref[...]
    row = lax.broadcasted_iota(jnp.int32, vsum.shape, 0)
    vsum = vsum + jnp.where(row == B_QUERY, bias[0], 0.0) + jnp.where(row == B_VALUE, bias[2], 0.0)
    high = vsum.astype(BF)
    low = (vsum - high.astype(F32)).astype(BF)
    for ref, p in ((keep, 3), (send_high, 1)):
        for z in range(shares // 2):
            ref[p, z, tall - 2 * GROUP:tall - GROUP] = high
            ref[p, z, tall - GROUP:tall] = low


def inputs_kernel(groups, hit_ref, dr_ref, wq_ref, wk_ref, wv_ref, *refs):
    parts = [refs[3 * g:3 * g + 3] for g in range(groups)]
    din_ref = refs[3 * groups]
    total = dr_ref[...]
    for i, w in enumerate((wq_ref, wk_ref, wv_ref)):
        at = 0
        for part in parts:
            wide = part[i].shape[1]
            total = total + nt(part[i][...], w[:, at:at + wide])
            at += wide
    din_ref[...] = jnp.where(hit_ref[:, 0:1] > 0.5, 0.0, total).astype(BF)


def added(a, b):
    return (a.astype(F32) + b.astype(F32)).astype(BF)


def pair_halves_kernel(bit, own, low, high, *outs):
    mine = bit()
    after = own.shape[2]
    for flip, out in zip((1, 0), outs):
        half = 1 - mine if flip else mine
        for which, came in enumerate((low, high)):

            @pl.when(half == which)
            def _():
                def one(j, carry):
                    out[j] = added(own[0, which, j], came[0, 0, j])
                    return carry

                lax.fori_loop(0, after, one, 0)


def halves_kernel(bit, which, own, came, *outs):
    mine = bit()
    for flip, out in zip(which, outs):
        half = 1 - mine if flip else mine

        def one(j, carry):
            out[j] = added(own[half, j], came[half, j])
            return carry

        lax.fori_loop(0, own.shape[1], one, 0)


def z_halves_kernel(which, own, came, *outs):
    low, high = z_bits()
    core = own_core()
    depth = own.shape[1]
    if depth == 4:
        mine = jnp.where(core == 0, low, high)
        by_half, by_rest = jnp.where(core == 0, 1, 2), jnp.where(core == 0, 2, 1)
    else:
        mine = jnp.where(core == 0, high, low)
        by_half, by_rest = 1, 0
    rest = depth // 2
    for flip, out in zip(which, outs):
        half = 1 - mine if flip else mine

        def one(j, carry):
            p, r = lax.div(j, rest), lax.rem(j, rest)
            z = half * by_half + r * by_rest
            out[p, r] = added(own[p, z], came[p, z])
            return carry

        lax.fori_loop(0, own.shape[0] * rest, one, 0)


def sum_kernel(own, came, out):
    out[...] = added(own[...], came[...]).reshape(out.shape)


def pair_kernel(own, came, out):
    lo = second_bit()
    out[lo] = own[...]
    out[1 - lo] = came[...]


def last_kernel(place, own, came, *outs):
    mine = first_bit()
    for half in range(2):
        @pl.when(mine == half)
        def _():
            for j in range(2):
                place(2 * half + j, own, j, *outs)
                place(2 * (1 - half) + j, came, j, *outs)


def place_down(p, ref, j, down):
    unit = ref.shape[1]
    down[p * unit:(p + 1) * unit] = ref[j].astype(F32)


def place_up(p, ref, j, up, out):
    unit, width = out.shape
    up[:, p * width:(p + 1) * width] = ref[j, 0:unit].astype(F32)
    tall, at = (2 * GROUP, p * 2 * GROUP) if p < 2 else (GROUP, (p + 2) * GROUP)
    out[at:at + tall] = ref[j, unit:unit + tall].astype(F32)


def place_rows(p, ref, j, query, key, value, vectors):
    unit = query.shape[0]
    tall = ref.shape[1]
    for g in range(tall // GROUP):
        at = p * tall + g * GROUP
        part = ref[j, g * GROUP:(g + 1) * GROUP].astype(F32)
        if at < 3 * unit:
            (query, key, value)[at // unit][at % unit:at % unit + GROUP] = part
        elif at == 3 * unit:
            vectors[...] = part + ref[j, (g + 1) * GROUP:(g + 2) * GROUP].astype(F32)


VM = pl.BlockSpec(memory_space=pltpu.VMEM)
SM = pl.BlockSpec(memory_space=pltpu.SMEM)
HB = pl.BlockSpec(memory_space=pl.ANY)


def call(kernel, args, places, outs, scratch, limit):
    return pl.pallas_call(
        kernel,
        out_shape=[jax.ShapeDtypeStruct(s, d) for s, d in outs],
        in_specs=places,
        out_specs=[VM] * len(outs),
        scratch_shapes=[s if not isinstance(s, tuple) else pltpu.VMEM(*s) for s in scratch],
        compiler_params=pltpu.CompilerParams(vmem_limit_bytes=limit * MIB),
        cost_estimate=pl.CostEstimate(flops=1024, bytes_accessed=1024, transcendentals=0),
    )(*args)


def fetch(ids, counts, spots, table, rows):
    width = table.shape[1]
    slots = ids.shape[1]
    return call(
        fetch_kernel, (ids, counts, spots, table), [SM, SM, VM, HB], [((rows, width), BF), ((rows, 128), F32)],
        [((slots * GROUP, width), BF), ((slots * GROUP, width), F32), ((slots, width), F32), pltpu.SemaphoreType.DMA], LIMITS[0],
    )


LIMITS = [44, 24, 40, 12, 16, 12, 8]


def attend(lengths, inputs, pieces, placed, hit, biases, wq, wk, wv, wo):
    span, width = pieces[0].shape
    rows = 4 * span
    args = (lengths, inputs, *pieces, placed, hit, *biases, wq, wk, wv, wo)
    outs = [((rows, width), BF)] * 4 + [((width, rows), BF), ((HEADS, 1, rows), F32), ((HEADS, 1, rows), F32), ((rows, width), F32), ((rows, 128), F32)]
    return call(attend_kernel, args, [SM] + [VM] * 13, outs, [((rows, width), BF)], LIMITS[1])


def feed(n, rstd, att, sums, cotangent, pieces, vecs, wu, wd, wo):
    rows, width = n.shape
    ff = wu.shape[1]
    unit = width // PARTS
    args = (n, rstd, att, sums, cotangent, *pieces, *vecs, wu, wd, wo)
    half = (4, PARTS // 2)
    outs = [((rows, width), BF)] + [(half + (unit, width), BF)] * 2 + [(half + (unit + 2 * GROUP, width), BF)] * 2
    outs += [((rows, width), F32), ((width, rows), BF), ((HEADS, 1, rows), F32), ((16, width), F32)]
    scratch = [((rows, ff), BF)] * 2 + [((rows, width), BF)] * 2 + [((width, rows), BF), ((rows, width), BF), ((rows, width), F32)]
    return call(ff_kernel, args, [VM] * len(args), outs, scratch, LIMITS[2])


def heads(first, count, lengths, q, k, v, dst, delta, tops):
    rows = q.shape[0]
    args = (lengths, q, k, v, dst, delta, tops)
    outs = [((rows, count * HD), BF)] * 3
    return call(functools.partial(heads_kernel, first // 2), args, [SM] + [VM] * 6, outs, [], LIMITS[3])


def grads(x, vsum, parts):
    rows, width = x.shape
    tall = (3 * (width // PARTS) + 2 * GROUP) // 4
    ga = (4, PARTS // 2, tall, width)
    args = (x, vsum) + tuple(t for part in parts for t in part)
    return call(functools.partial(grads_kernel, len(parts)), args, [VM] * len(args), [(ga, BF)] + [((2,) + ga[1:], BF)] * 2, [((width, rows), BF)], LIMITS[4])


def inputs_grad(hit, dr, wq, wk, wv, parts):
    args = (hit, dr, wq, wk, wv) + tuple(t for part in parts for t in part)
    return call(functools.partial(inputs_kernel, len(parts)), args, [VM] * len(args), [(dr.shape, BF)], [], LIMITS[5])[0]


def pick(array, index, axis=0):
    return lax.dynamic_index_in_dim(array, index, axis, keepdims=False)


def swap(array, bit):
    return lax.ppermute(array, "blk", [(i, i ^ bit) for i in range(lax.axis_size("blk"))])


def swap_first(array, first):
    blks, shares = lax.axis_size("blk"), lax.axis_size("batch")
    perm = []
    for b in range(blks):
        for s in range(shares):
            bit = 1 if (s % 2 == 0) == first else 2
            perm.append((b * shares + s, (b ^ bit) * shares + s))
    return lax.ppermute(array, ("blk", "batch"), perm)


def swap_batch(array, bit):
    return lax.ppermute(array, "batch", [(i, i ^ bit) for i in range(lax.axis_size("batch"))])


def swap_z(array, first):
    shares = lax.axis_size("batch")
    return lax.ppermute(array, "batch", [(i, i ^ (2 if (i % 2 == 0) == first else 4)) for i in range(shares)])


class Cell:
    def __init__(self, *values):
        self.values = values


class Order:
    def __init__(self):
        self.last = Cell()

    def enter(self, *arrays):
        tied = lax.optimization_barrier((*arrays, *self.last.values))
        self.last.values = tied[len(arrays):]
        return tied[:len(arrays)]

    def leave(self, cell):
        self.last = cell


class Chain:
    def __init__(self, order, cell, send):
        self.order = order
        self.own, self.came = cell, tuple(swap_batch(s, 1) for s in send)

    def halve(self, axis, bit, move, apart=False):
        own, *came = self.order.enter(self.own.values[0], *self.came)
        shape = own.shape
        after = shape[:axis] + (shape[axis] // 2,) + shape[axis + 1:]
        half = after if axis == 1 else (shape[0] * shape[1] // 2,) + shape[2:]

        def add(which, own, *came):
            if len(came) == 2:
                view = (1, 2, shape[0] * shape[1] // 2) + shape[2:]
                args = (own.reshape(view),) + tuple(c.reshape((1, 1) + view[2:]) for c in came)
                kernel = functools.partial(pair_halves_kernel, bit)
            else:
                view = shape if axis == 1 else (2, shape[0] * shape[1] // 2) + shape[2:]
                args = (own.reshape(view), came[0].reshape(view))
                kernel = functools.partial(z_halves_kernel, which) if axis == 1 else functools.partial(halves_kernel, bit, which)
            outs = call(kernel, args, [VM] * len(args), [(half, BF)] * len(which), [], LIMITS[6])
            return [out.reshape(after) for out in outs]

        if apart:
            out, = add((1,), own, *came)
            own, came[0], out = lax.optimization_barrier((own, came[0], out))
            self.came = (move(out),)
            keep, = add((0,), own, *came)
        else:
            out, keep = add((1, 0), own, *came)
            self.came = (move(out),)
        self.own = Cell(keep)
        self.order.leave(self.own)

    def first(self, apart=False):
        self.halve(0, first_bit, lambda v: swap_first(v, True), apart)

    def second(self):
        self.halve(0, second_bit, lambda v: swap_first(v, False))

    def z_first(self, apart=False):
        self.halve(1, None, lambda v: swap_z(v, True), apart)

    def z_second(self):
        self.halve(1, None, lambda v: swap_z(v, False))

    def gather_second(self):
        own, came = self.order.enter(self.own.values[0], *self.came)
        out, = call(sum_kernel, (own, came), [VM] * 2, [(own.shape[2:], BF)], [], LIMITS[6])
        self.own = Cell(out)
        self.came = (swap_first(out, False),)
        self.order.leave(self.own)

    def gather_first(self):
        own, came = self.order.enter(self.own.values[0], *self.came)
        out, = call(pair_kernel, (own, came), [VM] * 2, [((2,) + own.shape, BF)], [], LIMITS[6])
        self.own = Cell(out)
        self.came = (swap_first(out, True),)
        self.order.leave(self.own)

    def result(self, place, shapes):
        own, came = self.order.enter(self.own.values[0], *self.came)
        return call(functools.partial(last_kernel, place), (own, came), [VM] * 2, [(s, F32) for s in shapes], [], LIMITS[6])


def own_vectors(vec, share, shares):
    width = vec.shape[-1]
    n = width // shares
    cut = lax.dynamic_slice_in_dim(vec, share * n, n, 1)
    flat = vec[B_UP:B_UP + 4].reshape(-1)
    return [cut[i] for i in range(B_UP)] + [lax.dynamic_slice_in_dim(flat, share * 4 * n, 4 * n, 0)]


def body(
    inputs, lengths, positions, counts, token_ids, table,
    w_query, b_query, w_key, w_value, b_value, w_out, b_out, gain_one, shift_one,
    w_up, b_up, w_down, b_down, gain_two, shift_two, cotangent,
):
    blk, share = lax.axis_index("blk"), lax.axis_index("batch")
    shares = lax.axis_size("batch")
    core = share % 2
    pages, span, width = inputs.shape
    ff = w_up.shape[1]
    unit = width // PARTS
    rows_in = [swap(pick(inputs, blk ^ i), i) for i in range(1, pages)]
    back_in = [swap(pick(cotangent, blk ^ i), i) for i in range(1, pages)]
    placed, hit = fetch(token_ids, counts, positions, table, pages * span)
    x, q, k, v, att, tops, sums, n1, rstd = attend(
        lengths, inputs, rows_in, placed, hit, (b_query, b_value, b_out), w_query, w_key, w_value, w_out
    )
    out_page, d_keep, d_send, u_keep, u_send, d_r1, dst, delta, vsum = feed(
        n1, rstd, att, sums, cotangent, back_in, (b_up, b_down, gain_one, shift_one, gain_two, shift_two), w_up, w_down, w_out
    )
    order = Order()

    def attention_back(first, count):
        delta_now, = order.enter(delta)
        part = Cell(*heads(first, count, lengths, q, k, v, dst, delta_now, tops))
        order.leave(part)
        return part

    def to_pages(page, *others):
        pages_out = jnp.stack([page, *others]).reshape(1 + len(others), pages, span, width)
        result = jnp.zeros_like(pages_out)
        for i in range(pages):
            part = pick(pages_out, blk ^ i, 1)
            part = part if i == 0 else swap(part, i)
            result = lax.dynamic_update_index_in_dim(result, part, blk ^ i, 1)
        return result

    if shares == PARTS and lax.axis_size("blk") == 4:
        d = Chain(order, Cell(d_keep), [d_send])
        u = Chain(order, Cell(u_keep), [u_send])
        parts = [attention_back(0, 4)]
        d.z_first(True)
        parts.append(attention_back(4, 4))
        u.first(True)
        parts.append(attention_back(8, 4))
        x_now, = order.enter(x)
        a_keep, *a_send = grads(x_now, vsum, [p.values for p in parts])
        a_cell = Cell(a_keep)
        order.leave(a_cell)
        a = Chain(order, a_cell, a_send)
        u.second()
        d.z_second()
        a.first()
        hit_now, = order.enter(hit)
        d_cell = Cell(inputs_grad(hit_now, d_r1, w_query, w_key, w_value, [p.values for p in parts]))
        order.leave(d_cell)
        a.second()
        u.z_first()
        a.z_first()
        d.first()
        u.z_second()
        a.z_second()
        outputs, d_inputs = to_pages(out_page, *d_cell.values)
        d.second()
        u.gather_second()
        a.gather_second()
        d.gather_second()
        u.gather_first()
        a.gather_first()
        d.gather_first()
        grad_up, grad_out = u.result(place_up, [(unit, ff), (unit, width)])
        grad_query, grad_key, grad_value, vectors = a.result(place_rows, [(unit, width)] * 3 + [(GROUP, width)])
        grad_down, = d.result(place_down, [(ff // PARTS, width)])
    else:
        part = attention_back(0, HEADS)
        a_keep, *a_send = grads(x, vsum, [part.values])
        a_send = jnp.concatenate(a_send)
        d_page = inputs_grad(hit, d_r1, w_query, w_key, w_value, [part.values])
        outputs, d_inputs = to_pages(out_page, d_page)

        def parity(keep, send):
            packed = jnp.where(core == 0, jnp.stack([keep, send]), jnp.stack([send, keep]))
            return packed.transpose(1, 2, 0, 3, 4)

        def over(grad):
            part = lax.psum_scatter(grad.astype(F32), "batch", scatter_dimension=0, tiled=True)
            return lax.psum(part.astype(BF), "blk").astype(F32)

        down = parity(d_keep, d_send).transpose(1, 2, 0, 3, 4).reshape(ff, width)
        packed = parity(u_keep, u_send)
        up = packed[..., :unit, :].transpose(1, 2, 3, 0, 4).reshape(width, ff)
        rest = packed[..., unit:, :]
        out = jnp.concatenate([rest[0], rest[1], rest[2][..., :GROUP, :], rest[3][..., :GROUP, :]], axis=-2)
        out = out.reshape(width, width)
        rows = parity(a_keep, a_send).transpose(1, 2, 0, 3, 4).reshape(PARTS, -1, width)
        mats = [rows[:, i * unit:(i + 1) * unit].reshape(width, width) for i in range(3)]
        vectors = rows[0, 3 * unit:3 * unit + GROUP].astype(F32) + rows[0, 3 * unit + GROUP:].astype(F32)
        vectors = lax.psum(vectors, ("blk", "batch"))
        grad_down, grad_up, grad_out = over(down), over(up), over(out)
        grad_query, grad_key, grad_value = (over(m) for m in mats)
    r = own_vectors(vectors, share, shares)
    return (
        outputs, d_inputs, grad_query, r[B_QUERY], grad_key, grad_value, r[B_VALUE], grad_out, r[B_OUT],
        r[GAIN_ONE], r[SHIFT_ONE], grad_up, r[B_UP], grad_down, r[B_DOWN], r[GAIN_TWO], r[SHIFT_TWO],
    )


def solution(mesh):
    split, whole = P("batch", "blk", None), P()
    rows, vec = P("batch", None), P("batch")
    in_specs = (split, vec, rows, vec, rows) + (whole,) * 16 + (split,)
    out_specs = (split, split, rows, vec, rows, rows, vec, rows, vec, vec, vec, rows, vec, rows, vec, vec, vec)
    return jax.shard_map(body, mesh=mesh, in_specs=in_specs, out_specs=out_specs, check_vma=False)
```

```python
import functools

import jax
import jax.numpy as jnp
from jax import lax
from jax.experimental import pallas as pl
from jax.experimental.pallas import tpu as pltpu
from jax.sharding import PartitionSpec as P

HEADS = 12
HD = 64
SCALE = 0.125
NEGATIVE = -1e30
EPSILON = 1e-12
BF = jnp.bfloat16
F32 = jnp.float32
MIB = 1024 * 1024
GROUP = 16
PARTS = 8
B_QUERY, B_VALUE, B_OUT, B_DOWN, GAIN_ONE, SHIFT_ONE, GAIN_TWO, SHIFT_TWO, B_UP = range(9)


def nn(a, b):
    return lax.dot_general(a, b, (((1,), (0,)), ((), ())), preferred_element_type=F32)


def nt(a, b):
    return lax.dot_general(a, b, (((1,), (1,)), ((), ())), preferred_element_type=F32)


def tn(a, b):
    return lax.dot_general(a, b, (((0,), (0,)), ((), ())), preferred_element_type=F32)


def head_lanes(shape, which):
    lane = lax.broadcasted_iota(jnp.int32, shape, 1)
    return (lane >= HD) if which else (lane < HD)


def norm_parts(v):
    width = v.shape[-1]
    centre = jnp.sum(v, axis=-1, keepdims=True) * (1.0 / width)
    centred = v - centre
    spread = jnp.sum(centred * centred, axis=-1, keepdims=True) * (1.0 / width)
    rstd = lax.rsqrt(spread + EPSILON)
    return centred * rstd, rstd


def norm_back(c2, n, rstd):
    width = c2.shape[-1]
    a = jnp.sum(c2, axis=-1, keepdims=True) * (1.0 / width)
    b = jnp.sum(c2 * n, axis=-1, keepdims=True) * (1.0 / width)
    return (c2 - a - n * b) * rstd


def colsum(v):
    return jnp.sum(v, axis=0, keepdims=True)


def wide_row(ref):
    return ref[...].astype(F32).reshape(1, ref.shape[0])


def block(i, size):
    return pl.ds(pl.multiple_of(i * size, size), size)


def own_blk():
    return lax.axis_index("blk")


def own_core():
    return lax.rem(lax.axis_index("batch"), 2)


def first_bit():
    return jnp.where(own_core() == 0, lax.rem(own_blk(), 2), lax.div(own_blk(), 2))


def second_bit():
    return jnp.where(own_core() == 0, lax.div(own_blk(), 2), lax.rem(own_blk(), 2))


def z_bits():
    z = lax.div(lax.axis_index("batch"), 2)
    return lax.rem(z, 2), lax.div(z, 2)


def fetch_kernel(ids_ref, counts_ref, spots_ref, table_ref, placed_ref, hit_ref, rows_ref, wide_ref, sel_ref, sem):
    slots = ids_ref.shape[1]
    me = own_blk()

    def start(j, carry):
        group = pl.multiple_of((ids_ref[me, j] // GROUP) * GROUP, GROUP)
        pltpu.make_async_copy(table_ref.at[pl.ds(group, GROUP), :], rows_ref.at[block(j, GROUP), :], sem).start()
        return carry

    lax.fori_loop(0, slots, start, 0, unroll=8)
    total = placed_ref.shape[0]
    spot = lax.broadcasted_iota(jnp.int32, (total, slots), 0)
    slot = lax.broadcasted_iota(jnp.int32, (total, slots), 1)
    hits = ((spots_ref[pl.ds(me, 1), :] == spot) & (slot < counts_ref[me])).astype(F32)
    hit_ref[...] = jnp.broadcast_to(jnp.sum(hits, axis=1, keepdims=True), hit_ref.shape)
    pltpu.make_async_copy(table_ref.at[pl.ds(0, slots * GROUP), :], rows_ref, sem).wait()
    wide_ref[...] = rows_ref[...].astype(F32)
    for j in range(slots):
        at = j * GROUP + lax.rem(ids_ref[me, j], GROUP)
        sel_ref[pl.ds(j, 1), :] = wide_ref[pl.ds(at, 1), :]
    placed_ref[...] = nn(hits.astype(BF), sel_ref[...].astype(BF)).astype(BF)


def attend_kernel(
    lengths_ref, inputs_ref, p1_ref, p2_ref, p3_ref, placed_ref, hit_ref, bq_ref, bv_ref, bo_ref,
    wq_ref, wk_ref, wv_ref, wo_ref,
    x_t_ref, q_ref, k_ref, v_ref, att_ref, max_ref, sum_ref, n_ref, rstd_ref,
    x_ref, att_rows,
):
    me = own_blk()
    length = lengths_ref[me]
    rows, width = x_ref.shape
    span = p1_ref.shape[0]
    for step, piece in enumerate((inputs_ref[me], p1_ref[...], p2_ref[...], p3_ref[...])):
        at = block(me ^ step, span)
        x_ref[at, :] = jnp.where(hit_ref[at, 0:1] > 0.5, placed_ref[at, :], piece)
    x_t_ref[...] = x_ref[...].T
    q = (nn(x_ref[...], wq_ref[...]) + wide_row(bq_ref)).astype(BF)
    q_ref[...] = (q.astype(F32) * SCALE).astype(BF)
    k_ref[...] = nn(x_ref[...], wk_ref[...]).astype(BF)
    v_ref[...] = (nn(x_ref[...], wv_ref[...]) + wide_row(bv_ref)).astype(BF)
    dead = jnp.where(lax.broadcasted_iota(jnp.int32, (rows, 1), 0) < length, 0.0, NEGATIVE)

    def pair(i, carry):
        lanes = block(i, 2 * HD)
        q2, k2 = q_ref[:, lanes], k_ref[:, lanes]
        v2t = v_ref[:, lanes].T
        for h in range(2):
            qm = jnp.where(head_lanes(q2.shape, h), q2, jnp.zeros_like(q2))
            s = nt(k2, qm) + dead
            top = jnp.max(s, axis=0, keepdims=True)
            p = jnp.exp(s - top)
            total = jnp.sum(p, axis=0, keepdims=True)
            o = nn(v2t[h * HD:(h + 1) * HD], p.astype(BF)) / total
            max_ref[2 * i + h] = top
            sum_ref[2 * i + h] = total
            att_ref[block(2 * i + h, HD), :] = o.astype(BF)
        att_rows[:, lanes] = att_ref[lanes, :].T
        return carry

    lax.fori_loop(0, HEADS // 2, pair, 0)
    branch = nn(att_rows[...], wo_ref[...]) + wide_row(bo_ref)
    n, rstd = norm_parts(x_ref[...].astype(F32) + branch)
    n_ref[...] = n
    rstd_ref[...] = jnp.broadcast_to(rstd, rstd_ref.shape)


def gelu_both(v):
    e = jnp.exp(v * v * -0.5)
    t = 1.0 / (1.0 + (0.3275911 * 0.7071067811865476) * jnp.abs(v))
    poly = t * (0.5 * 0.254829592 + t * (0.5 * -0.284496736 + t * (0.5 * 1.421413741 + t * (0.5 * -1.453152027 + t * (0.5 * 1.061405429)))))
    tail = poly * e
    phi = jnp.where(v >= 0, 1.0 - tail, tail)
    return v * phi, phi + v * (e * 0.3989422804014327)


def by_core(core, deal, keep, send):
    for c in range(2):

        @pl.when(core == c)
        def _():
            deal(c, *keep)
            deal(1 - c, *send)


OUT_GROUPS = [(0, 0), (0, 1), (1, 0), (1, 1), (2, 0), (3, 0)]


def ff_kernel(
    n_ref, cot_ref, c1_ref, c2_ref, c3_ref,
    bu_ref, bd_ref, g1_ref, s1_ref, g2_ref, s2_ref, wu_ref, wd_ref,
    out_ref, dkeep, dsend, ukeep, usend, dh_ref, dfirst_ref, vsum_ref,
    act, slope, cot, nlow, nlow_t, dd, g_down, g_up,
):
    width = n_ref.shape[1]
    ff = wu_ref.shape[1]
    parts = ff // width
    shares = 2 * dkeep.shape[1]
    unit = width // shares
    span = c1_ref.shape[0]
    me, core = own_blk(), own_core()
    for hop, piece in enumerate((cot_ref[me], c1_ref[...], c2_ref[...], c3_ref[...])):
        cot[block(me ^ hop, span), :] = piece
    normed = n_ref[...] * wide_row(g1_ref) + wide_row(s1_ref)
    nlow[...] = normed.astype(BF)
    nlow_t[...] = nlow[...].T
    for i in range(parts):
        lanes = slice(i * width, (i + 1) * width)
        a, b = gelu_both(nn(nlow[...], wu_ref[:, lanes]) + wide_row(bu_ref)[:, lanes])
        act[:, lanes] = a.astype(BF)
        slope[:, lanes] = b.astype(BF)
    normed = n_ref[...] * wide_row(g1_ref) + wide_row(s1_ref)
    resid = normed + nn(act[...], wd_ref[...]) + wide_row(bd_ref)
    n2, rstd2 = norm_parts(resid)
    out_ref[...] = (n2 * wide_row(g2_ref) + wide_row(s2_ref)).astype(BF)
    c = cot[...].astype(F32)
    vsum_ref[...] = jnp.zeros_like(vsum_ref)
    vsum_ref[GAIN_TWO:GAIN_TWO + 1] = colsum(c * n2)
    vsum_ref[SHIFT_TWO:SHIFT_TWO + 1] = colsum(c)
    d_r2 = norm_back(c * wide_row(g2_ref), n2, rstd2)
    dfirst_ref[...] = d_r2
    dd[...] = d_r2.astype(BF)
    vsum_ref[B_DOWN:B_DOWN + 1] = colsum(dd[...].astype(F32))

    def back(i, carry):
        lanes = block(i, width)
        g_down[...] = tn(act[:, lanes], dd[...]).astype(BF)
        dhc = (nt(dd[...], wd_ref[lanes, :]) * slope[:, lanes].astype(F32)).astype(BF)
        dh_ref[:, lanes] = dhc
        vsum_ref[pl.ds(B_UP + i, 1)] = colsum(dhc.astype(F32))
        g_up[...] = nn(nlow_t[...], dhc).astype(BF)

        def deal(c, down, up):
            for p in range(4):
                at = (c * 4 + p) * unit
                down[p, i] = g_down[at:at + unit]
            for z in range(shares // 2):
                at = (2 * z + c) * unit
                up[i, z] = g_up[at:at + unit]

        by_core(core, deal, (dkeep, ukeep), (dsend, usend))
        return carry

    lax.fori_loop(0, parts, back, 0)


def mixed_kernel(
    n_ref, rstd_ref, att_ref, sum_ref, dh_ref, dfirst_ref, vin_ref, g1_ref, wu_ref, wo_ref,
    okeep, osend, dr_ref, dst_ref, delta_ref, vsum_ref,
    dd, g_out, dm_ref,
):
    width = n_ref.shape[1]
    shares = 2 * okeep.shape[1]
    unit = width // shares
    d_f = dfirst_ref[...] + nt(dh_ref[...], wu_ref[...])
    n1 = n_ref[...]
    vsum_ref[...] = vin_ref[...]
    vsum_ref[GAIN_ONE:GAIN_ONE + 1] = colsum(d_f * n1)
    vsum_ref[SHIFT_ONE:SHIFT_ONE + 1] = colsum(d_f)
    d_r1 = norm_back(d_f * wide_row(g1_ref), n1, rstd_ref[:, 0:1])
    dr_ref[...] = d_r1
    db = d_r1.astype(BF)
    dd[...] = db
    vsum_ref[B_OUT:B_OUT + 1] = colsum(db.astype(F32))
    g_out[...] = nn(att_ref[...], dd[...]).astype(BF)
    dm_ref[...] = nt(wo_ref[...], dd[...])

    def deal(c, out):
        for z in range(shares // 2):
            for g in range(unit // GROUP):
                p, at = OUT_GROUPS[g]
                src = (2 * z + c) * unit + g * GROUP
                out[p, z, at * GROUP:(at + 1) * GROUP] = g_out[src:src + GROUP]
            for p in (2, 3):
                out[p, z, GROUP:2 * GROUP] = jnp.zeros((GROUP, width), BF)

    by_core(own_core(), deal, (okeep,), (osend,))
    for i in range(HEADS):
        at = slice(i * HD, (i + 1) * HD)
        inv = 1.0 / sum_ref[i]
        delta_ref[i] = colsum(dm_ref[at, :] * att_ref[at, :].astype(F32)) * inv
        dst_ref[at, :] = (dm_ref[at, :] * inv).astype(BF)


def heads_kernel(first, lengths_ref, x_t_ref, vin_ref, q_ref, k_ref, v_ref, dst_ref, delta_ref, max_ref, dq, dk, dv, keep, send, g_ref):
    length = lengths_ref[own_blk()]
    rows = q_ref.shape[0]
    dead = jnp.where(lax.broadcasted_iota(jnp.int32, (rows, 1), 0) < length, 0.0, NEGATIVE)

    def pair(i, carry):
        lanes, own = block(first + i, 2 * HD), block(i, 2 * HD)
        q2, k2, v2 = q_ref[:, lanes], k_ref[:, lanes], v_ref[:, lanes]
        dst = dst_ref[lanes, :]
        ds2 = dst.T
        k2t = k2.T
        dv2 = jnp.zeros((rows, 2 * HD), F32)
        dk2 = jnp.zeros((rows, 2 * HD), F32)
        dqs = []
        for h in range(2):
            live = head_lanes(q2.shape, h)
            zero = jnp.zeros_like(q2)
            qm = jnp.where(live, q2, zero)
            s = nt(k2, qm) + dead
            head = 2 * (first + i) + h
            p = jnp.exp(s - max_ref[head])
            dp = nn(jnp.where(live, v2, zero), dst)
            dsc = (p * (dp - delta_ref[head])).astype(BF)
            dv2 = dv2 + nn(p.astype(BF), jnp.where(live, ds2, zero))
            dk2 = dk2 + nn(dsc, qm)
            dqs.append(nn(k2t[h * HD:(h + 1) * HD], dsc))
        dq[:, own] = (jnp.concatenate(dqs, axis=0) * SCALE).astype(BF).T
        dk[:, own] = dk2.astype(BF)
        dv[:, own] = dv2.astype(BF)
        return carry

    lax.fori_loop(0, dq.shape[1] // (2 * HD), pair, 0)
    for i, part in enumerate((dq, dk, dv)):
        g_ref[i] = nn(x_t_ref[...], part[...]).astype(BF)
    vsum = vin_ref[:, first * 2 * HD:first * 2 * HD + dq.shape[1]]
    row = lax.broadcasted_iota(jnp.int32, vsum.shape, 0)
    vsum = vsum + jnp.where(row == B_QUERY, colsum(dq[...].astype(F32)), 0.0) + jnp.where(row == B_VALUE, colsum(dv[...].astype(F32)), 0.0)
    high = vsum.astype(BF)
    low = (vsum - high.astype(F32)).astype(BF)
    shares = 2 * keep.shape[1]
    unit = x_t_ref.shape[0] // shares
    tall = keep.shape[2]

    def deal(c, pieces):
        for z in range(shares // 2):
            for i in range(3):
                for j in range(unit // GROUP):
                    at, src = i * unit + j * GROUP, (2 * z + c) * unit + j * GROUP
                    pieces[at // tall, z, at % tall:at % tall + GROUP] = g_ref[i, src:src + GROUP]
            pieces[3, z, tall - 2 * GROUP:tall - GROUP] = high
            pieces[3, z, tall - GROUP:tall] = low

    by_core(own_core(), deal, (keep,), (send,))


def inputs_kernel(groups, hit_ref, dr_ref, wq_ref, wk_ref, wv_ref, *refs):
    parts = [refs[3 * g:3 * g + 3] for g in range(groups)]
    din_ref = refs[3 * groups]
    total = dr_ref[...]
    for i, w in enumerate((wq_ref, wk_ref, wv_ref)):
        at = 0
        for part in parts:
            wide = part[i].shape[1]
            total = total + nt(part[i][...], w[:, at:at + wide])
            at += wide
    din_ref[...] = jnp.where(hit_ref[:, 0:1] > 0.5, 0.0, total).astype(BF)


def added(a, b):
    return (a.astype(F32) + b.astype(F32)).astype(BF)


def halves_kernel(bit, came_parts, own, *refs):
    came, (*sends, keep) = refs[:came_parts], refs[came_parts:]
    rest = own.shape[1]
    per_came, per_send = 2 * rest // came_parts, rest // len(sends)
    mine = bit()
    for half in range(2):
        for keeps in (False, True):

            @pl.when((mine == half) == keeps)
            def _():
                for r in range(rest):
                    flat = half * rest + r
                    value = added(own[half, r], came[flat // per_came][flat % per_came])
                    if keeps:
                        keep[r] = value
                    else:
                        sends[r // per_send][r % per_send] = value


def joined_halves_kernel(bit, axis, groups, *refs):
    owns, cames, (send, keep) = refs[:groups], refs[groups:2 * groups], refs[2 * groups:]
    mine = bit()
    for half in range(2):
        for keeps, out in ((False, send), (True, keep)):

            @pl.when((mine == half) == keeps)
            def _():
                for r in range(out.shape[0]):
                    at = 0
                    for own, came in zip(owns, cames):
                        size = own.shape[1 + axis]
                        cut = slice(at, at + size)
                        index = (r, cut) if axis == 1 else (r, slice(None), cut)
                        out[index] = added(own[half, r], came[half, r])
                        at += size


def z_halves_kernel(came_parts, own, *refs):
    came, (*sends, keep) = refs[:came_parts], refs[came_parts:]
    pieces, depth = own.shape[:2]
    rest = depth // 2
    per_came, per_send = pieces * depth // came_parts, pieces * rest // len(sends)
    low, high = z_bits()
    core = own_core()
    for c in range(2):
        mine = low if (c == 0) == (depth == 4) else high
        for half in range(2):

            @pl.when((core == c) & (mine == half))
            def _():
                for p in range(pieces):
                    for r in range(rest):
                        for keeps in (False, True):
                            h = half if keeps else 1 - half
                            z = h if depth == 2 else 2 * r + h if c == 0 else 2 * h + r
                            flat = p * depth + z
                            value = added(own[p, z], came[flat // per_came][flat % per_came])
                            out = p * rest + r
                            if keeps:
                                keep[out] = value
                            else:
                                sends[out // per_send][out % per_send] = value


def sum_kernel(own, came, out):
    out[...] = added(own[...].reshape(out.shape), came[...].reshape(out.shape))


def pair_kernel(own, came, out):
    lo = second_bit()
    out[lo] = own[...]
    out[1 - lo] = came[...]


def last_kernel(place, own, came, *refs):
    mine = first_bit()
    for half in range(2):
        @pl.when(mine == half)
        def _():
            for j in range(2):
                place(2 * half + j, own, j, *refs)
                place(2 * (1 - half) + j, came, j, *refs)


def place_up(p, ref, j, up, out):
    unit, width = out.shape
    up[:, p * width:(p + 1) * width] = ref[j, 0:unit].astype(F32)
    for g, (piece, at) in enumerate(OUT_GROUPS):
        if piece == p:
            out[g * GROUP:(g + 1) * GROUP] = ref[j, unit + at * GROUP:unit + (at + 1) * GROUP].astype(F32)


def place_down(p, ref, j, down):
    unit = down.shape[0] // 4
    down[p * unit:(p + 1) * unit] = ref[j].astype(F32)


def place_rows(p, ref, j, query, key, value, vectors):
    unit = query.shape[0]
    tall = ref.shape[1]
    for g in range(tall // GROUP):
        at = p * tall + g * GROUP
        part = ref[j, g * GROUP:(g + 1) * GROUP].astype(F32)
        if at < 3 * unit:
            (query, key, value)[at // unit][at % unit:at % unit + GROUP] = part
        elif at == 3 * unit:
            vectors[...] = part + ref[j, (g + 1) * GROUP:(g + 2) * GROUP].astype(F32)


def page_parts_kernel(out_page, d_page, *outs):
    span = outs[0].shape[1]
    for i, out in enumerate(outs):
        rows = block(own_blk() ^ (i + 1), span)
        out[0] = out_page[rows, :]
        out[1] = d_page[rows, :]


def page_rows_kernel(out_page, d_page, *refs):
    *came, out_rows, d_rows = refs
    span = out_rows.shape[1]
    me = own_blk()
    for which, (page, out) in enumerate(((out_page, out_rows), (d_page, d_rows))):
        out[me] = page[block(me, span), :]
        for i, part in enumerate(came):
            out[me ^ (i + 1)] = part[which]


VM = pl.BlockSpec(memory_space=pltpu.VMEM)
SM = pl.BlockSpec(memory_space=pltpu.SMEM)
HB = pl.BlockSpec(memory_space=pl.ANY)


def call(kernel, args, places, outs, scratch, limit):
    return pl.pallas_call(
        kernel,
        out_shape=[jax.ShapeDtypeStruct(s, d) for s, d in outs],
        in_specs=places,
        out_specs=[VM] * len(outs),
        scratch_shapes=[s if not isinstance(s, tuple) else pltpu.VMEM(*s) for s in scratch],
        compiler_params=pltpu.CompilerParams(vmem_limit_bytes=limit * MIB),
        cost_estimate=pl.CostEstimate(flops=1024, bytes_accessed=1024, transcendentals=0),
    )(*args)


def fetch(ids, counts, spots, table, rows):
    width = table.shape[1]
    slots = ids.shape[1]
    return call(
        fetch_kernel, (ids, counts, spots, table), [SM, SM, VM, HB], [((rows, width), BF), ((rows, 128), F32)],
        [((slots * GROUP, width), BF), ((slots * GROUP, width), F32), ((slots, width), F32), pltpu.SemaphoreType.DMA], LIMITS[0],
    )


LIMITS = [44, 24, 36, 16, 16, 16, 8]


def attend(lengths, inputs, pieces, placed, hit, biases, wq, wk, wv, wo):
    span, width = pieces[0].shape
    rows = 4 * span
    args = (lengths, inputs, *pieces, placed, hit, *biases, wq, wk, wv, wo)
    outs = [((width, rows), BF)] + [((rows, width), BF)] * 3 + [((width, rows), BF), ((HEADS, 1, rows), F32), ((HEADS, 1, rows), F32), ((rows, width), F32), ((rows, 128), F32)]
    return call(attend_kernel, args, [SM] + [VM] * 13, outs, [((rows, width), BF)] * 2, LIMITS[1])


def feed(n, cotangent, pieces, vecs, wu, wd):
    rows, width = n.shape
    ff = wu.shape[1]
    args = (n, cotangent, *pieces, *vecs, wu, wd)
    group = ((4, PARTS // 2, width // PARTS, width), BF)
    outs = [((rows, width), BF)] + [group] * 4 + [((rows, ff), BF), ((rows, width), F32), ((16, width), F32)]
    scratch = [((rows, ff), BF)] * 2 + [((rows, width), BF)] * 2 + [((width, rows), BF), ((rows, width), BF)] + [((width, width), BF)] * 2
    return call(ff_kernel, args, [VM] * len(args), outs, scratch, LIMITS[2])


def mixed_back(n, rstd, att, sums, dh, dfirst, vsum, gain, wu, wo):
    rows, width = n.shape
    args = (n, rstd, att, sums, dh, dfirst, vsum, gain, wu, wo)
    group = ((4, PARTS // 2, 2 * GROUP, width), BF)
    outs = [group] * 2 + [((rows, width), F32), ((width, rows), BF), ((HEADS, 1, rows), F32), (vsum.shape, F32)]
    scratch = [((rows, width), BF), ((width, width), BF), ((width, rows), F32)]
    return call(mixed_kernel, args, [VM] * len(args), outs, scratch, LIMITS[5])


def heads(first, count, lengths, x_t, vsum, q, k, v, dst, delta, tops):
    width, rows = x_t.shape
    wide = count * HD
    tall = (3 * (width // PARTS) + 2 * GROUP) // 4
    args = (lengths, x_t, vsum, q, k, v, dst, delta, tops)
    outs = [((rows, wide), BF)] * 3 + [((4, PARTS // 2, tall, wide), BF)] * 2
    return call(functools.partial(heads_kernel, first // 2), args, [SM] + [VM] * 8, outs, [((3, width, wide), BF)], LIMITS[3])


def inputs_grad(hit, dr, wq, wk, wv, parts):
    args = (hit, dr, wq, wk, wv) + tuple(t for part in parts for t in part)
    return call(functools.partial(inputs_kernel, len(parts)), args, [VM] * len(args), [(dr.shape, BF)], [], LIMITS[5])[0]


def pick(array, index, axis=0):
    return lax.dynamic_index_in_dim(array, index, axis, keepdims=False)


def swap(array, bit):
    return lax.ppermute(array, "blk", [(i, i ^ bit) for i in range(lax.axis_size("blk"))])


def swap_first(array, first):
    blks, shares = lax.axis_size("blk"), lax.axis_size("batch")
    perm = []
    for b in range(blks):
        for s in range(shares):
            bit = 1 if (s % 2 == 0) == first else 2
            perm.append((b * shares + s, (b ^ bit) * shares + s))
    return lax.ppermute(array, ("blk", "batch"), perm)


def swap_batch(array, bit):
    return lax.ppermute(array, "batch", [(i, i ^ bit) for i in range(lax.axis_size("batch"))])


def swap_z(array, first):
    shares = lax.axis_size("batch")
    return lax.ppermute(array, "batch", [(i, i ^ (2 if (i % 2 == 0) == first else 4)) for i in range(shares)])


class Cell:
    def __init__(self, *values):
        self.values = values


class Order:
    def __init__(self):
        self.last = Cell()

    def enter(self, *arrays):
        tied = lax.optimization_barrier((*arrays, *self.last.values))
        self.last.values = tied[len(arrays):]
        return tied[:len(arrays)]

    def leave(self, cell):
        self.last = cell


class Chain:
    def __init__(self, order, cell, send):
        self.order = order
        self.own, self.came = cell, tuple(swap_batch(s, 1) for s in send)

    @classmethod
    def joined(cls, order, axis, cells, cames):
        chain = cls(order, None, ())
        tied = order.enter(*(c.values[0] for c in cells), *cames)
        groups = len(cells)
        shape = tied[0].shape
        flat = [shape[0] * shape[1] // 2, shape[2], shape[3]]
        flat[axis] = sum(t.shape[axis + 1] for t in tied[:groups])
        args = [t.reshape((2, flat[0]) + t.shape[2:]) for t in tied]
        kernel = functools.partial(joined_halves_kernel, first_bit, axis, groups)
        send, keep = call(kernel, args, [VM] * len(args), [(tuple(flat), BF)] * 2, [], LIMITS[6])
        chain.came = [swap_first(send, True)]
        chain.own = Cell(keep.reshape((shape[0] // 2, shape[1], flat[1], flat[2])))
        order.leave(chain.own)
        return chain

    def halve(self, axis, bit, move, cuts):
        own, *came = self.order.enter(self.own.values[0], *self.came)
        shape = own.shape
        after = shape[:axis] + (shape[axis] // 2,) + shape[axis + 1:]
        flat = (after[0] * after[1],) + shape[2:]
        if axis == 0:
            own = own.reshape((2,) + flat)
            kernel = functools.partial(halves_kernel, bit, len(came))
        else:
            kernel = functools.partial(z_halves_kernel, len(came))
        came = [c.reshape((-1,) + shape[2:]) for c in came]
        outs = [((flat[0] // cuts,) + shape[2:], BF)] * cuts + [(flat, BF)]
        *sends, keep = call(kernel, (own, *came), [VM] * (1 + len(came)), outs, [], LIMITS[6])
        self.came = [move(send) for send in sends]
        self.own = Cell(keep.reshape(after))
        self.order.leave(self.own)

    def first(self, cuts=1):
        self.halve(0, first_bit, lambda v: swap_first(v, True), cuts)

    def second(self, cuts=1):
        self.halve(0, second_bit, lambda v: swap_first(v, False), cuts)

    def z_first(self, cuts=1):
        self.halve(1, None, lambda v: swap_z(v, True), cuts)

    def z_second(self, cuts=1):
        self.halve(1, None, lambda v: swap_z(v, False), cuts)

    def gather_second(self):
        own, came = self.order.enter(self.own.values[0], *self.came)
        out, = call(sum_kernel, (own, came), [VM] * 2, [(own.shape[2:], BF)], [], LIMITS[6])
        self.own = Cell(out)
        self.came = (swap_first(out, False),)
        self.order.leave(self.own)

    def gather_first(self):
        own, came = self.order.enter(self.own.values[0], *self.came)
        out, = call(pair_kernel, (own, came), [VM] * 2, [((2,) + own.shape, BF)], [], LIMITS[6])
        self.own = Cell(out)
        self.came = (swap_first(out, True),)
        self.order.leave(self.own)

    def result(self, place, shapes, *others):
        own, came = self.order.enter(self.own.values[0], *self.came)
        args = (own, came, *others)
        return call(functools.partial(last_kernel, place), args, [VM] * len(args), [(s, F32) for s in shapes], [], LIMITS[6])


def own_vectors(vec, share, shares):
    width = vec.shape[-1]
    n = width // shares
    cut = lax.dynamic_slice_in_dim(vec, share * n, n, 1)
    flat = vec[B_UP:B_UP + 4].reshape(-1)
    return [cut[i] for i in range(B_UP)] + [lax.dynamic_slice_in_dim(flat, share * 4 * n, 4 * n, 0)]


def body(
    inputs, lengths, positions, counts, token_ids, table,
    w_query, b_query, w_key, w_value, b_value, w_out, b_out, gain_one, shift_one,
    w_up, b_up, w_down, b_down, gain_two, shift_two, cotangent,
):
    blk, share = lax.axis_index("blk"), lax.axis_index("batch")
    shares = lax.axis_size("batch")
    core = share % 2
    pages, span, width = inputs.shape
    ff = w_up.shape[1]
    unit = width // PARTS
    rows_in = [swap(pick(inputs, blk ^ i), i) for i in range(1, pages)]
    back_in = [swap(pick(cotangent, blk ^ i), i) for i in range(1, pages)]
    placed, hit = fetch(token_ids, counts, positions, table, pages * span)
    x_t, q, k, v, att, tops, sums, n1, rstd = attend(
        lengths, inputs, rows_in, placed, hit, (b_query, b_value, b_out), w_query, w_key, w_value, w_out
    )
    out_page, d_keep, d_send, u_keep, u_send, dh, dfirst, vsum = feed(
        n1, cotangent, back_in, (b_up, b_down, gain_one, shift_one, gain_two, shift_two), w_up, w_down
    )

    def to_mixed(n1, vsum):
        return mixed_back(n1, rstd, att, sums, dh, dfirst, vsum, gain_one, w_up, w_out)

    order = Order()

    def attention_back(first, count, vsum, dst, delta):
        delta, = order.enter(delta)
        *parts, keep, send = heads(first, count, lengths, x_t, vsum, q, k, v, dst, delta, tops)
        grads = Cell(keep)
        order.leave(grads)
        return parts, grads, send

    def page_parts(out_page, d_page):
        return call(page_parts_kernel, (out_page, d_page), [VM] * 2, [((2, span, width), BF)] * (pages - 1), [], LIMITS[6])

    def page_rows(out_page, d_page, came):
        return call(page_rows_kernel, (out_page, d_page, *came), [VM] * (pages + 1), [(inputs.shape, BF)] * 2, [], LIMITS[6])

    if shares == PARTS and lax.axis_size("blk") == 4:
        d = Chain(order, Cell(d_keep), [d_send])
        u_came = swap_batch(u_send, 1)
        n_now, = order.enter(n1)
        o_keep, o_send, d_r1, dst, delta, vsum = to_mixed(n_now, vsum)
        o_cell = Cell(o_keep)
        order.leave(o_cell)
        o_came = swap_batch(o_send, 1)
        d.z_first()
        groups = [attention_back(0, 4, vsum, dst, delta)]
        u = Chain.joined(order, 1, [Cell(u_keep), o_cell], [u_came, o_came])
        groups.append(attention_back(4, 4, vsum, dst, delta))
        groups.append(attention_back(8, 4, vsum, dst, delta))
        parts = [g[0] for g in groups]
        a = Chain.joined(order, 2, [g[1] for g in groups], [swap_batch(g[2], 1) for g in groups])
        d.z_second()
        u.second()
        hit_now, = order.enter(hit)
        d_cell = Cell(inputs_grad(hit_now, d_r1, w_query, w_key, w_value, parts))
        order.leave(d_cell)
        a.second()
        u.z_first()
        d.first()
        a.z_first()
        out_now, = order.enter(out_page)
        d_page, = d_cell.values
        rows_cell = Cell(*page_parts(out_now, d_page))
        order.leave(rows_cell)
        came = [swap(part, i + 1) for i, part in enumerate(rows_cell.values)]
        u.z_second()
        d.second()
        a.z_second()
        d_page, *came = order.enter(d_page, *came)
        rows_cell = Cell(*page_rows(out_page, d_page, came))
        order.leave(rows_cell)
        u.gather_second()
        d.gather_second()
        a.gather_second()
        a.gather_first()
        u.gather_first()
        d.gather_first()
        grad_query, grad_key, grad_value, vectors = a.result(place_rows, [(unit, width)] * 3 + [(GROUP, width)])
        grad_up, grad_out = u.result(place_up, [(unit, ff), (unit, width)])
        grad_down, = d.result(place_down, [(ff // PARTS, width)])
        outputs, d_inputs = rows_cell.values
    else:
        o_keep, o_send, d_r1, dst, delta, vsum = to_mixed(n1, vsum)
        parts, a_keep, a_send = attention_back(0, HEADS, vsum, dst, delta)
        a_keep, = a_keep.values
        d_page = inputs_grad(hit, d_r1, w_query, w_key, w_value, [parts])
        came = [swap(part, i + 1) for i, part in enumerate(page_parts(out_page, d_page))]
        outputs, d_inputs = page_rows(out_page, d_page, came)

        def parity(keep, send):
            packed = jnp.where(core == 0, jnp.stack([keep, send]), jnp.stack([send, keep]))
            return packed.transpose(1, 2, 0, 3, 4)

        def over(grad):
            part = lax.psum_scatter(grad.astype(F32), "batch", scatter_dimension=0, tiled=True)
            return lax.psum(part.astype(BF), "blk").astype(F32)

        out = parity(o_keep, o_send)
        out = jnp.concatenate([out[p][..., at * GROUP:(at + 1) * GROUP, :] for p, at in OUT_GROUPS], axis=-2)
        out = out.reshape(width, width)
        down = parity(d_keep, d_send).transpose(1, 2, 0, 3, 4).reshape(ff, width)
        up = parity(u_keep, u_send).transpose(1, 2, 3, 0, 4).reshape(width, ff)
        rows = parity(a_keep, a_send).transpose(1, 2, 0, 3, 4).reshape(PARTS, -1, width)
        mats = [rows[:, i * unit:(i + 1) * unit].reshape(width, width) for i in range(3)]
        vectors = rows[0, 3 * unit:3 * unit + GROUP].astype(F32) + rows[0, 3 * unit + GROUP:].astype(F32)
        vectors = lax.psum(vectors, ("blk", "batch"))
        grad_down, grad_up, grad_out = over(down), over(up), over(out)
        grad_query, grad_key, grad_value = (over(m) for m in mats)
    r = own_vectors(vectors, share, shares)
    return (
        outputs, d_inputs, grad_query, r[B_QUERY], grad_key, grad_value, r[B_VALUE], grad_out, r[B_OUT],
        r[GAIN_ONE], r[SHIFT_ONE], grad_up, r[B_UP], grad_down, r[B_DOWN], r[GAIN_TWO], r[SHIFT_TWO],
    )


def solution(mesh):
    split, whole = P("batch", "blk", None), P()
    rows, vec = P("batch", None), P("batch")
    in_specs = (split, vec, rows, vec, rows) + (whole,) * 16 + (split,)
    out_specs = (split, split, rows, vec, rows, rows, vec, rows, vec, vec, vec, rows, vec, rows, vec, vec, vec)
    return jax.shard_map(body, mesh=mesh, in_specs=in_specs, out_specs=out_specs, check_vma=False)
```

```python
import functools

import jax
import jax.numpy as jnp
from jax import lax
from jax.experimental import pallas as pl
from jax.experimental.pallas import tpu as pltpu
from jax.sharding import PartitionSpec as P

HEADS = 12
HD = 64
SCALE = 0.125
NEGATIVE = -1e30
EPSILON = 1e-12
BF = jnp.bfloat16
F32 = jnp.float32
MIB = 1024 * 1024
GROUP = 16
PARTS = 8
B_QUERY, B_VALUE, B_OUT, B_DOWN, GAIN_ONE, SHIFT_ONE, GAIN_TWO, SHIFT_TWO, B_UP = range(9)


def nn(a, b):
    return lax.dot_general(a, b, (((1,), (0,)), ((), ())), preferred_element_type=F32)


def nt(a, b):
    return lax.dot_general(a, b, (((1,), (1,)), ((), ())), preferred_element_type=F32)


def tn(a, b):
    return lax.dot_general(a, b, (((0,), (0,)), ((), ())), preferred_element_type=F32)


def head_lanes(shape, which):
    lane = lax.broadcasted_iota(jnp.int32, shape, 1)
    return (lane >= HD) if which else (lane < HD)


def norm_parts(v):
    width = v.shape[-1]
    centre = jnp.sum(v, axis=-1, keepdims=True) * (1.0 / width)
    centred = v - centre
    spread = jnp.sum(centred * centred, axis=-1, keepdims=True) * (1.0 / width)
    rstd = lax.rsqrt(spread + EPSILON)
    return centred * rstd, rstd


def norm_back(c2, n, rstd):
    width = c2.shape[-1]
    a = jnp.sum(c2, axis=-1, keepdims=True) * (1.0 / width)
    b = jnp.sum(c2 * n, axis=-1, keepdims=True) * (1.0 / width)
    return (c2 - a - n * b) * rstd


def colsum(v):
    return jnp.sum(v, axis=0, keepdims=True)


def wide_row(ref):
    return ref[...].astype(F32).reshape(1, ref.shape[0])


def block(i, size):
    return pl.ds(pl.multiple_of(i * size, size), size)


def own_blk():
    return lax.axis_index("blk")


def own_core():
    return lax.rem(lax.axis_index("batch"), 2)


def first_bit():
    return jnp.where(own_core() == 0, lax.rem(own_blk(), 2), lax.div(own_blk(), 2))


def second_bit():
    return jnp.where(own_core() == 0, lax.div(own_blk(), 2), lax.rem(own_blk(), 2))


def z_bits():
    z = lax.div(lax.axis_index("batch"), 2)
    return lax.rem(z, 2), lax.div(z, 2)


def fetch_kernel(ids_ref, counts_ref, spots_ref, table_ref, placed_ref, hit_ref, rows_ref, wide_ref, sel_ref, sem):
    slots = ids_ref.shape[1]
    me = own_blk()

    def start(j, carry):
        group = pl.multiple_of((ids_ref[me, j] // GROUP) * GROUP, GROUP)
        pltpu.make_async_copy(table_ref.at[pl.ds(group, GROUP), :], rows_ref.at[block(j, GROUP), :], sem).start()
        return carry

    lax.fori_loop(0, slots, start, 0, unroll=8)
    total = placed_ref.shape[0]
    spot = lax.broadcasted_iota(jnp.int32, (total, slots), 0)
    slot = lax.broadcasted_iota(jnp.int32, (total, slots), 1)
    hits = ((spots_ref[pl.ds(me, 1), :] == spot) & (slot < counts_ref[me])).astype(F32)
    hit_ref[...] = jnp.broadcast_to(jnp.sum(hits, axis=1, keepdims=True), hit_ref.shape)
    pltpu.make_async_copy(table_ref.at[pl.ds(0, slots * GROUP), :], rows_ref, sem).wait()
    wide_ref[...] = rows_ref[...].astype(F32)
    for j in range(slots):
        at = j * GROUP + lax.rem(ids_ref[me, j], GROUP)
        sel_ref[pl.ds(j, 1), :] = wide_ref[pl.ds(at, 1), :]
    placed_ref[...] = nn(hits.astype(BF), sel_ref[...].astype(BF)).astype(BF)


def attend_kernel(
    lengths_ref, inputs_ref, p1_ref, p2_ref, p3_ref, placed_ref, hit_ref, bq_ref, bv_ref, bo_ref,
    wq_ref, wk_ref, wv_ref, wo_ref,
    x_t_ref, q_ref, k_ref, v_ref, att_ref, max_ref, sum_ref, n_ref, rstd_ref,
    x_ref, att_rows,
):
    me = own_blk()
    length = lengths_ref[me]
    rows, width = x_ref.shape
    span = p1_ref.shape[0]
    for step, piece in enumerate((inputs_ref[me], p1_ref[...], p2_ref[...], p3_ref[...])):
        at = block(me ^ step, span)
        x_ref[at, :] = jnp.where(hit_ref[at, 0:1] > 0.5, placed_ref[at, :], piece)
    x_t_ref[...] = x_ref[...].T
    q = (nn(x_ref[...], wq_ref[...]) + wide_row(bq_ref)).astype(BF)
    q_ref[...] = (q.astype(F32) * SCALE).astype(BF)
    k_ref[...] = nn(x_ref[...], wk_ref[...]).astype(BF)
    v_ref[...] = (nn(x_ref[...], wv_ref[...]) + wide_row(bv_ref)).astype(BF)
    dead = jnp.where(lax.broadcasted_iota(jnp.int32, (rows, 1), 0) < length, 0.0, NEGATIVE)

    def pair(i, carry):
        lanes = block(i, 2 * HD)
        q2, k2 = q_ref[:, lanes], k_ref[:, lanes]
        v2t = v_ref[:, lanes].T
        for h in range(2):
            qm = jnp.where(head_lanes(q2.shape, h), q2, jnp.zeros_like(q2))
            s = nt(k2, qm) + dead
            top = jnp.max(s, axis=0, keepdims=True)
            p = jnp.exp(s - top)
            total = jnp.sum(p, axis=0, keepdims=True)
            o = nn(v2t[h * HD:(h + 1) * HD], p.astype(BF)) / total
            max_ref[2 * i + h] = top
            sum_ref[2 * i + h] = total
            att_ref[block(2 * i + h, HD), :] = o.astype(BF)
        att_rows[:, lanes] = att_ref[lanes, :].T
        return carry

    lax.fori_loop(0, HEADS // 2, pair, 0)
    branch = nn(att_rows[...], wo_ref[...]) + wide_row(bo_ref)
    n, rstd = norm_parts(x_ref[...].astype(F32) + branch)
    n_ref[...] = n
    rstd_ref[...] = jnp.broadcast_to(rstd, rstd_ref.shape)


def gelu_both(v):
    e = jnp.exp(v * v * -0.5)
    t = 1.0 / (1.0 + (0.3275911 * 0.7071067811865476) * jnp.abs(v))
    poly = t * (0.5 * 0.254829592 + t * (0.5 * -0.284496736 + t * (0.5 * 1.421413741 + t * (0.5 * -1.453152027 + t * (0.5 * 1.061405429)))))
    tail = poly * e
    phi = jnp.where(v >= 0, 1.0 - tail, tail)
    return v * phi, phi + v * (e * 0.3989422804014327)


def by_core(core, deal, keep, send):
    for c in range(2):

        @pl.when(core == c)
        def _():
            deal(c, *keep)
            deal(1 - c, *send)


OUT_GROUPS = [(0, 0), (0, 1), (1, 0), (1, 1), (2, 0), (3, 0)]


def ff_kernel(
    n_ref, cot_ref, c1_ref, c2_ref, c3_ref,
    bu_ref, bd_ref, g1_ref, s1_ref, g2_ref, s2_ref, wu_ref, wd_ref,
    out_ref, dkeep, dsend, ukeep, usend, dh_ref, dfirst_ref, vsum_ref,
    act, cot, nlow, nlow_t, dd, g_down, g_up,
):
    width = n_ref.shape[1]
    ff = wu_ref.shape[1]
    parts = ff // width
    shares = 2 * dkeep.shape[1]
    unit = width // shares
    span = c1_ref.shape[0]
    me, core = own_blk(), own_core()
    for hop, piece in enumerate((cot_ref[me], c1_ref[...], c2_ref[...], c3_ref[...])):
        cot[block(me ^ hop, span), :] = piece
    normed = n_ref[...] * wide_row(g1_ref) + wide_row(s1_ref)
    nlow[...] = normed.astype(BF)
    nlow_t[...] = nlow[...].T
    for i in range(parts):
        lanes = slice(i * width, (i + 1) * width)
        a, b = gelu_both(nn(nlow[...], wu_ref[:, lanes]) + wide_row(bu_ref)[:, lanes])
        act[:, lanes] = a.astype(BF)
        dh_ref[:, lanes] = b.astype(BF)
    normed = n_ref[...] * wide_row(g1_ref) + wide_row(s1_ref)
    resid = normed + nn(act[...], wd_ref[...]) + wide_row(bd_ref)
    n2, rstd2 = norm_parts(resid)
    out_ref[...] = (n2 * wide_row(g2_ref) + wide_row(s2_ref)).astype(BF)
    c = cot[...].astype(F32)
    vsum_ref[...] = jnp.zeros_like(vsum_ref)
    vsum_ref[GAIN_TWO:GAIN_TWO + 1] = colsum(c * n2)
    vsum_ref[SHIFT_TWO:SHIFT_TWO + 1] = colsum(c)
    d_r2 = norm_back(c * wide_row(g2_ref), n2, rstd2)
    dfirst_ref[...] = d_r2
    dd[...] = d_r2.astype(BF)
    vsum_ref[B_DOWN:B_DOWN + 1] = colsum(dd[...].astype(F32))

    def back(i, carry):
        lanes = block(i, width)
        g_down[...] = tn(act[:, lanes], dd[...]).astype(BF)
        dhc = (nt(dd[...], wd_ref[lanes, :]) * dh_ref[:, lanes].astype(F32)).astype(BF)
        dh_ref[:, lanes] = dhc
        vsum_ref[pl.ds(B_UP + i, 1)] = colsum(dhc.astype(F32))
        g_up[...] = nn(nlow_t[...], dhc).astype(BF)

        def deal(c, down, up):
            for p in range(4):
                at = (c * 4 + p) * unit
                down[p, i] = g_down[at:at + unit]
            for z in range(shares // 2):
                at = (2 * z + c) * unit
                up[i, z] = g_up[at:at + unit]

        by_core(core, deal, (dkeep, ukeep), (dsend, usend))
        return carry

    lax.fori_loop(0, parts, back, 0)


def mixed_kernel(
    n_ref, rstd_ref, att_ref, dh_ref, dfirst_ref, vin_ref, g1_ref, wu_ref,
    okeep, osend, dr_ref, dd, vsum_ref,
    g_out,
):
    width = n_ref.shape[1]
    shares = 2 * okeep.shape[1]
    unit = width // shares
    d_f = dfirst_ref[...] + nt(dh_ref[...], wu_ref[...])
    n1 = n_ref[...]
    vsum_ref[...] = vin_ref[...]
    vsum_ref[GAIN_ONE:GAIN_ONE + 1] = colsum(d_f * n1)
    vsum_ref[SHIFT_ONE:SHIFT_ONE + 1] = colsum(d_f)
    d_r1 = norm_back(d_f * wide_row(g1_ref), n1, rstd_ref[:, 0:1])
    dr_ref[...] = d_r1
    db = d_r1.astype(BF)
    dd[...] = db
    vsum_ref[B_OUT:B_OUT + 1] = colsum(db.astype(F32))
    g_out[...] = nn(att_ref[...], dd[...]).astype(BF)

    def deal(c, out):
        for z in range(shares // 2):
            for g in range(unit // GROUP):
                p, at = OUT_GROUPS[g]
                src = (2 * z + c) * unit + g * GROUP
                out[p, z, at * GROUP:(at + 1) * GROUP] = g_out[src:src + GROUP]
            for p in (2, 3):
                out[p, z, GROUP:2 * GROUP] = jnp.zeros((GROUP, width), BF)

    by_core(own_core(), deal, (okeep,), (osend,))


def attended_kernel(att_ref, sum_ref, dd_ref, wo_ref, dst_ref, delta_ref, dm_ref):
    dm_ref[...] = nt(wo_ref[...], dd_ref[...])
    for i in range(HEADS):
        at = slice(i * HD, (i + 1) * HD)
        inv = 1.0 / sum_ref[i]
        delta_ref[i] = colsum(dm_ref[at, :] * att_ref[at, :].astype(F32)) * inv
        dst_ref[at, :] = (dm_ref[at, :] * inv).astype(BF)


def heads_kernel(first, lengths_ref, x_t_ref, vin_ref, q_ref, k_ref, v_ref, dst_ref, delta_ref, max_ref, dq, dk, dv, keep, *sends):
    *sends, g_ref = sends
    length = lengths_ref[own_blk()]
    rows = q_ref.shape[0]
    dead = jnp.where(lax.broadcasted_iota(jnp.int32, (rows, 1), 0) < length, 0.0, NEGATIVE)

    def pair(i, carry):
        lanes, own = block(first + i, 2 * HD), block(i, 2 * HD)
        q2, k2, v2 = q_ref[:, lanes], k_ref[:, lanes], v_ref[:, lanes]
        dst = dst_ref[lanes, :]
        ds2 = dst.T
        k2t = k2.T
        dv2 = jnp.zeros((rows, 2 * HD), F32)
        dk2 = jnp.zeros((rows, 2 * HD), F32)
        dqs = []
        for h in range(2):
            live = head_lanes(q2.shape, h)
            zero = jnp.zeros_like(q2)
            qm = jnp.where(live, q2, zero)
            s = nt(k2, qm) + dead
            head = 2 * (first + i) + h
            p = jnp.exp(s - max_ref[head])
            dp = nn(jnp.where(live, v2, zero), dst)
            dsc = (p * (dp - delta_ref[head])).astype(BF)
            dv2 = dv2 + nn(p.astype(BF), jnp.where(live, ds2, zero))
            dk2 = dk2 + nn(dsc, qm)
            dqs.append(nn(k2t[h * HD:(h + 1) * HD], dsc))
        dq[:, own] = (jnp.concatenate(dqs, axis=0) * SCALE).astype(BF).T
        dk[:, own] = dk2.astype(BF)
        dv[:, own] = dv2.astype(BF)
        return carry

    lax.fori_loop(0, dq.shape[1] // (2 * HD), pair, 0)
    for i, part in enumerate((dq, dk, dv)):
        g_ref[i] = nn(x_t_ref[...], part[...]).astype(BF)
    vsum = vin_ref[:, first * 2 * HD:first * 2 * HD + dq.shape[1]]
    row = lax.broadcasted_iota(jnp.int32, vsum.shape, 0)
    vsum = vsum + jnp.where(row == B_QUERY, colsum(dq[...].astype(F32)), 0.0) + jnp.where(row == B_VALUE, colsum(dv[...].astype(F32)), 0.0)
    high = vsum.astype(BF)
    low = (vsum - high.astype(F32)).astype(BF)
    shares = 2 * keep.shape[1]
    unit = x_t_ref.shape[0] // shares
    tall = keep.shape[2]

    def deal(c, *pieces):
        for z in range(shares // 2):
            for i in range(3):
                for j in range(unit // GROUP):
                    at, src = i * unit + j * GROUP, (2 * z + c) * unit + j * GROUP
                    pieces[at // tall][z, at % tall:at % tall + GROUP] = g_ref[i, src:src + GROUP]
            pieces[3][z, tall - 2 * GROUP:tall - GROUP] = high
            pieces[3][z, tall - GROUP:tall] = low

    per = 4 // len(sends)
    by_core(own_core(), deal, [keep.at[p] for p in range(4)], [sends[p // per].at[p % per] for p in range(4)])


def inputs_kernel(groups, hit_ref, out_page, dr_ref, wq_ref, wk_ref, wv_ref, *refs):
    parts = [refs[3 * g:3 * g + 3] for g in range(groups)]
    din_ref, *outs = refs[3 * groups:]
    total = dr_ref[...]
    for i, w in enumerate((wq_ref, wk_ref, wv_ref)):
        at = 0
        for part in parts:
            wide = part[i].shape[1]
            total = total + nt(part[i][...], w[:, at:at + wide])
            at += wide
    din_ref[...] = jnp.where(hit_ref[:, 0:1] > 0.5, 0.0, total).astype(BF)
    span = outs[0].shape[1]
    for i, out in enumerate(outs):
        rows = block(own_blk() ^ (i + 1), span)
        out[0] = out_page[rows, :]
        out[1] = din_ref[rows, :]


def added(a, b):
    return (a.astype(F32) + b.astype(F32)).astype(BF)


def halves_kernel(bit, came_parts, own, *refs):
    came, (*sends, keep) = refs[:came_parts], refs[came_parts:]
    rest = own.shape[1]
    per_came, per_send = 2 * rest // came_parts, rest // len(sends)
    mine = bit()
    for half in range(2):
        for keeps in (False, True):

            @pl.when((mine == half) == keeps)
            def _():
                for r in range(rest):
                    flat = half * rest + r
                    value = added(own[half, r], came[flat // per_came][flat % per_came])
                    if keeps:
                        keep[r] = value
                    else:
                        sends[r // per_send][r % per_send] = value


def joined_halves_kernel(bit, axis, cuts, *refs):
    owns, rest = refs[:len(cuts)], refs[len(cuts):]
    cames = []
    for n in cuts:
        cames.append(rest[:n])
        rest = rest[n:]
    send, keep = rest
    mine = bit()
    for half in range(2):
        for keeps, out in ((False, send), (True, keep)):

            @pl.when((mine == half) == keeps)
            def _():
                for r in range(out.shape[0]):
                    at = 0
                    for own, came in zip(owns, cames):
                        size = own.shape[1 + axis]
                        cut = slice(at, at + size)
                        index = (r, cut) if axis == 1 else (r, slice(None), cut)
                        out[index] = added(own[half, r], came[0][half, r] if len(came) == 1 else came[half][0, r])
                        at += size


def z_halves_kernel(came_parts, own, *refs):
    came, (*sends, keep) = refs[:came_parts], refs[came_parts:]
    pieces, depth = own.shape[:2]
    rest = depth // 2
    per_came, per_send = pieces * depth // came_parts, pieces * rest // len(sends)
    low, high = z_bits()
    core = own_core()
    for c in range(2):
        mine = low if (c == 0) == (depth == 4) else high
        for half in range(2):

            @pl.when((core == c) & (mine == half))
            def _():
                for p in range(pieces):
                    for r in range(rest):
                        for keeps in (False, True):
                            h = half if keeps else 1 - half
                            z = h if depth == 2 else 2 * r + h if c == 0 else 2 * h + r
                            flat = p * depth + z
                            value = added(own[p, z], came[flat // per_came][flat % per_came])
                            out = p * rest + r
                            if keeps:
                                keep[out] = value
                            else:
                                sends[out // per_send][out % per_send] = value


def sum_kernel(own, came, out):
    out[...] = added(own[...].reshape(out.shape), came[...].reshape(out.shape))


def pair_kernel(own, came, out):
    lo = second_bit()
    out[lo] = own[...]
    out[1 - lo] = came[...]


def last_kernel(place, own, came, *refs):
    mine = first_bit()
    for half in range(2):
        @pl.when(mine == half)
        def _():
            for j in range(2):
                place(2 * half + j, own, j, *refs)
                place(2 * (1 - half) + j, came, j, *refs)


def place_up(p, ref, j, up, out):
    unit, width = out.shape
    up[:, p * width:(p + 1) * width] = ref[j, 0:unit].astype(F32)
    for g, (piece, at) in enumerate(OUT_GROUPS):
        if piece == p:
            out[g * GROUP:(g + 1) * GROUP] = ref[j, unit + at * GROUP:unit + (at + 1) * GROUP].astype(F32)


def place_down(p, ref, j, down):
    unit = down.shape[0] // 4
    down[p * unit:(p + 1) * unit] = ref[j].astype(F32)


def place_rows(p, ref, j, query, key, value, vectors):
    unit = query.shape[0]
    tall = ref.shape[1]
    for g in range(tall // GROUP):
        at = p * tall + g * GROUP
        part = ref[j, g * GROUP:(g + 1) * GROUP].astype(F32)
        if at < 3 * unit:
            (query, key, value)[at // unit][at % unit:at % unit + GROUP] = part
        elif at == 3 * unit:
            vectors[...] = part + ref[j, (g + 1) * GROUP:(g + 2) * GROUP].astype(F32)


def page_rows_kernel(out_page, d_page, *refs):
    *came, out_rows, d_rows = refs
    span = out_rows.shape[1]
    me = own_blk()
    for which, (page, out) in enumerate(((out_page, out_rows), (d_page, d_rows))):
        out[me] = page[block(me, span), :]
        for i, part in enumerate(came):
            out[me ^ (i + 1)] = part[which]


VM = pl.BlockSpec(memory_space=pltpu.VMEM)
SM = pl.BlockSpec(memory_space=pltpu.SMEM)
HB = pl.BlockSpec(memory_space=pl.ANY)


def call(kernel, args, places, outs, scratch, limit):
    return pl.pallas_call(
        kernel,
        out_shape=[jax.ShapeDtypeStruct(s, d) for s, d in outs],
        in_specs=places,
        out_specs=[VM] * len(outs),
        scratch_shapes=[s if not isinstance(s, tuple) else pltpu.VMEM(*s) for s in scratch],
        compiler_params=pltpu.CompilerParams(vmem_limit_bytes=limit * MIB),
        cost_estimate=pl.CostEstimate(flops=1024, bytes_accessed=1024, transcendentals=0),
    )(*args)


def fetch(ids, counts, spots, table, rows):
    width = table.shape[1]
    slots = ids.shape[1]
    return call(
        fetch_kernel, (ids, counts, spots, table), [SM, SM, VM, HB], [((rows, width), BF), ((rows, 128), F32)],
        [((slots * GROUP, width), BF), ((slots * GROUP, width), F32), ((slots, width), F32), pltpu.SemaphoreType.DMA], LIMITS[0],
    )


LIMITS = [44, 16, 20, 8, 16, 10, 4]


def attend(lengths, inputs, pieces, placed, hit, biases, wq, wk, wv, wo):
    span, width = pieces[0].shape
    rows = 4 * span
    args = (lengths, inputs, *pieces, placed, hit, *biases, wq, wk, wv, wo)
    outs = [((width, rows), BF)] + [((rows, width), BF)] * 3 + [((width, rows), BF), ((HEADS, 1, rows), F32), ((HEADS, 1, rows), F32), ((rows, width), F32), ((rows, 128), F32)]
    return call(attend_kernel, args, [SM] + [VM] * 13, outs, [((rows, width), BF)] * 2, LIMITS[1])


def feed(n, cotangent, pieces, vecs, wu, wd):
    rows, width = n.shape
    ff = wu.shape[1]
    args = (n, cotangent, *pieces, *vecs, wu, wd)
    group = ((4, PARTS // 2, width // PARTS, width), BF)
    outs = [((rows, width), BF)] + [group] * 4 + [((rows, ff), BF), ((rows, width), F32), ((16, width), F32)]
    scratch = [((rows, ff), BF)] + [((rows, width), BF)] * 2 + [((width, rows), BF), ((rows, width), BF)] + [((width, width), BF)] * 2
    return call(ff_kernel, args, [VM] * len(args), outs, scratch, LIMITS[2])


def mixed_back(n, rstd, att, dh, dfirst, vsum, gain, wu):
    rows, width = n.shape
    args = (n, rstd, att, dh, dfirst, vsum, gain, wu)
    group = ((4, PARTS // 2, 2 * GROUP, width), BF)
    outs = [group] * 2 + [((rows, width), F32), ((rows, width), BF), (vsum.shape, F32)]
    return call(mixed_kernel, args, [VM] * len(args), outs, [((width, width), BF)], LIMITS[5])


def attended_back(att, sums, dd, wo):
    rows, width = dd.shape
    outs = [((width, rows), BF), ((HEADS, 1, rows), F32)]
    return call(attended_kernel, (att, sums, dd, wo), [VM] * 4, outs, [((width, rows), F32)], LIMITS[5])


def heads(first, count, cuts, lengths, x_t, vsum, q, k, v, dst, delta, tops):
    width, rows = x_t.shape
    wide = count * HD
    tall = (3 * (width // PARTS) + 2 * GROUP) // 4
    args = (lengths, x_t, vsum, q, k, v, dst, delta, tops)
    outs = [((rows, wide), BF)] * 3 + [((4, PARTS // 2, tall, wide), BF)] + [((4 // cuts, PARTS // 2, tall, wide), BF)] * cuts
    return call(functools.partial(heads_kernel, first // 2), args, [SM] + [VM] * 8, outs, [((3, width, wide), BF)], LIMITS[3])


def inputs_grad(span, hit, out_page, dr, wq, wk, wv, parts):
    rows, width = dr.shape
    args = (hit, out_page, dr, wq, wk, wv) + tuple(t for part in parts for t in part)
    outs = [(dr.shape, BF)] + [((2, span, width), BF)] * (rows // span - 1)
    return call(functools.partial(inputs_kernel, len(parts)), args, [VM] * len(args), outs, [], LIMITS[5])


def pick(array, index, axis=0):
    return lax.dynamic_index_in_dim(array, index, axis, keepdims=False)


def swap(array, bit):
    return lax.ppermute(array, "blk", [(i, i ^ bit) for i in range(lax.axis_size("blk"))])


def swap_first(array, first):
    blks, shares = lax.axis_size("blk"), lax.axis_size("batch")
    perm = []
    for b in range(blks):
        for s in range(shares):
            bit = 1 if (s % 2 == 0) == first else 2
            perm.append((b * shares + s, (b ^ bit) * shares + s))
    return lax.ppermute(array, ("blk", "batch"), perm)


def swap_batch(array, bit):
    return lax.ppermute(array, "batch", [(i, i ^ bit) for i in range(lax.axis_size("batch"))])


def swap_z(array, first):
    shares = lax.axis_size("batch")
    return lax.ppermute(array, "batch", [(i, i ^ (2 if (i % 2 == 0) == first else 4)) for i in range(shares)])


class Cell:
    def __init__(self, *values):
        self.values = values


class Order:
    def __init__(self):
        self.last = Cell()

    def enter(self, *arrays):
        tied = lax.optimization_barrier((*arrays, *self.last.values))
        self.last.values = tied[len(arrays):]
        return tied[:len(arrays)]

    def leave(self, cell):
        self.last = cell


class Chain:
    def __init__(self, order, cell, send):
        self.order = order
        self.own, self.came = cell, tuple(swap_batch(s, 1) for s in send)

    @classmethod
    def joined(cls, order, axis, cells, cames):
        chain = cls(order, None, ())
        groups = len(cells)
        tied = order.enter(*(c.values[0] for c in cells), *(t for came in cames for t in came))
        shape = tied[0].shape
        flat = [shape[0] * shape[1] // 2, shape[2], shape[3]]
        flat[axis] = sum(t.shape[axis + 1] for t in tied[:groups])
        args = [t.reshape((-1, flat[0]) + t.shape[2:]) for t in tied]
        kernel = functools.partial(joined_halves_kernel, first_bit, axis, [len(came) for came in cames])
        send, keep = call(kernel, args, [VM] * len(args), [(tuple(flat), BF)] * 2, [], LIMITS[6])
        chain.came = [swap_first(send, True)]
        chain.own = Cell(keep.reshape((shape[0] // 2, shape[1], flat[1], flat[2])))
        order.leave(chain.own)
        return chain

    def halve(self, axis, bit, move, cuts):
        own, *came = self.order.enter(self.own.values[0], *self.came)
        shape = own.shape
        after = shape[:axis] + (shape[axis] // 2,) + shape[axis + 1:]
        flat = (after[0] * after[1],) + shape[2:]
        if axis == 0:
            own = own.reshape((2,) + flat)
            kernel = functools.partial(halves_kernel, bit, len(came))
        else:
            kernel = functools.partial(z_halves_kernel, len(came))
        came = [c.reshape((-1,) + shape[2:]) for c in came]
        outs = [((flat[0] // cuts,) + shape[2:], BF)] * cuts + [(flat, BF)]
        *sends, keep = call(kernel, (own, *came), [VM] * (1 + len(came)), outs, [], LIMITS[6])
        self.came = [move(send) for send in sends]
        self.own = Cell(keep.reshape(after))
        self.order.leave(self.own)

    def first(self, cuts=1):
        self.halve(0, first_bit, lambda v: swap_first(v, True), cuts)

    def second(self, cuts=1):
        self.halve(0, second_bit, lambda v: swap_first(v, False), cuts)

    def z_first(self, cuts=1):
        self.halve(1, None, lambda v: swap_z(v, True), cuts)

    def z_second(self, cuts=1):
        self.halve(1, None, lambda v: swap_z(v, False), cuts)

    def gather_second(self):
        own, came = self.order.enter(self.own.values[0], *self.came)
        out, = call(sum_kernel, (own, came), [VM] * 2, [(own.shape[2:], BF)], [], LIMITS[6])
        self.own = Cell(out)
        self.came = (swap_first(out, False),)
        self.order.leave(self.own)

    def gather_first(self):
        own, came = self.order.enter(self.own.values[0], *self.came)
        out, = call(pair_kernel, (own, came), [VM] * 2, [((2,) + own.shape, BF)], [], LIMITS[6])
        self.own = Cell(out)
        self.came = (swap_first(out, True),)
        self.order.leave(self.own)

    def result(self, place, shapes, *others):
        own, came = self.order.enter(self.own.values[0], *self.came)
        args = (own, came, *others)
        return call(functools.partial(last_kernel, place), args, [VM] * len(args), [(s, F32) for s in shapes], [], LIMITS[6])


def own_vectors(vec, share, shares):
    width = vec.shape[-1]
    n = width // shares
    cut = lax.dynamic_slice_in_dim(vec, share * n, n, 1)
    flat = vec[B_UP:B_UP + 4].reshape(-1)
    return [cut[i] for i in range(B_UP)] + [lax.dynamic_slice_in_dim(flat, share * 4 * n, 4 * n, 0)]


def body(
    inputs, lengths, positions, counts, token_ids, table,
    w_query, b_query, w_key, w_value, b_value, w_out, b_out, gain_one, shift_one,
    w_up, b_up, w_down, b_down, gain_two, shift_two, cotangent,
):
    blk, share = lax.axis_index("blk"), lax.axis_index("batch")
    shares = lax.axis_size("batch")
    core = share % 2
    pages, span, width = inputs.shape
    ff = w_up.shape[1]
    unit = width // PARTS
    rows_in = [swap(pick(inputs, blk ^ i), i) for i in range(1, pages)]
    back_in = [swap(pick(cotangent, blk ^ i), i) for i in range(1, pages)]
    placed, hit = fetch(token_ids, counts, positions, table, pages * span)
    x_t, q, k, v, att, tops, sums, n1, rstd = attend(
        lengths, inputs, rows_in, placed, hit, (b_query, b_value, b_out), w_query, w_key, w_value, w_out
    )
    out_page, d_keep, d_send, u_keep, u_send, dh, dfirst, vsum = feed(
        n1, cotangent, back_in, (b_up, b_down, gain_one, shift_one, gain_two, shift_two), w_up, w_down
    )

    def to_mixed(n1, vsum):
        return mixed_back(n1, rstd, att, dh, dfirst, vsum, gain_one, w_up)

    order = Order()

    def attention_back(first, count, vsum, dst, delta, cuts=1):
        delta, = order.enter(delta)
        dq, dk, dv, keep, *send = heads(first, count, cuts, lengths, x_t, vsum, q, k, v, dst, delta, tops)
        parts = [dq, dk, dv]
        grads = Cell(keep)
        order.leave(grads)
        return parts, grads, send

    def page_rows(out_page, d_page, came):
        return call(page_rows_kernel, (out_page, d_page, *came), [VM] * (pages + 1), [(inputs.shape, BF)] * 2, [], LIMITS[6])

    if shares == PARTS and lax.axis_size("blk") == 4:
        d = Chain(order, Cell(d_keep), [d_send])
        u_came = swap_batch(u_send, 1)
        n_now, = order.enter(n1)
        o_keep, o_send, d_r1, d_branch, vsum = to_mixed(n_now, vsum)
        o_cell = Cell(o_keep)
        order.leave(o_cell)
        o_came = swap_batch(o_send, 1)
        att_now, = order.enter(att)
        sums_cell = Cell(*attended_back(att_now, sums, d_branch, w_out))
        order.leave(sums_cell)
        d.z_first()
        u = Chain.joined(order, 1, [Cell(u_keep), o_cell], [[u_came], [o_came]])
        groups = [attention_back(0, 8, vsum, *sums_cell.values, cuts=2)]
        groups.append(attention_back(8, 4, vsum, *sums_cell.values))
        parts = [g[0] for g in groups]
        a = Chain.joined(order, 2, [g[1] for g in groups], [[swap_batch(t, 1) for t in g[2]] for g in groups])
        d.z_second()
        u.second()
        hit_now, = order.enter(hit)
        d_page, *page_parts = inputs_grad(span, hit_now, out_page, d_r1, w_query, w_key, w_value, parts)
        d_cell = Cell(d_page)
        order.leave(d_cell)
        page_parts = [swap(part, i + 1) for i, part in enumerate(page_parts)]
        a.second()
        u.z_first()
        d.first()
        a.z_first()
        u.z_second()
        d.second()
        a.z_second()
        u.gather_second()
        d.gather_second()
        d_page, *came = order.enter(*d_cell.values, *page_parts)
        rows_cell = Cell(*page_rows(out_page, d_page, came))
        order.leave(rows_cell)
        a.gather_second()
        a.gather_first()
        u.gather_first()
        d.gather_first()
        grad_query, grad_key, grad_value, vectors = a.result(place_rows, [(unit, width)] * 3 + [(GROUP, width)])
        grad_up, grad_out = u.result(place_up, [(unit, ff), (unit, width)])
        grad_down, = d.result(place_down, [(ff // PARTS, width)])
        outputs, d_inputs = rows_cell.values
    else:
        o_keep, o_send, d_r1, d_branch, vsum = to_mixed(n1, vsum)
        attended = attended_back(att, sums, d_branch, w_out)
        groups = [attention_back(i, 4, vsum, *attended) for i in range(0, HEADS, 4)]
        a_keep = jnp.concatenate([g[1].values[0] for g in groups], axis=-1)
        a_send = jnp.concatenate([g[2][0] for g in groups], axis=-1)
        d_page, *page_parts = inputs_grad(span, hit, out_page, d_r1, w_query, w_key, w_value, [g[0] for g in groups])
        came = [swap(part, i + 1) for i, part in enumerate(page_parts)]
        outputs, d_inputs = page_rows(out_page, d_page, came)

        def parity(keep, send):
            packed = jnp.where(core == 0, jnp.stack([keep, send]), jnp.stack([send, keep]))
            return packed.transpose(1, 2, 0, 3, 4)

        def over(grad):
            part = lax.psum_scatter(grad.astype(F32), "batch", scatter_dimension=0, tiled=True)
            return lax.psum(part.astype(BF), "blk").astype(F32)

        out = parity(o_keep, o_send)
        out = jnp.concatenate([out[p][..., at * GROUP:(at + 1) * GROUP, :] for p, at in OUT_GROUPS], axis=-2)
        out = out.reshape(width, width)
        down = parity(d_keep, d_send).transpose(1, 2, 0, 3, 4).reshape(ff, width)
        up = parity(u_keep, u_send).transpose(1, 2, 3, 0, 4).reshape(width, ff)
        rows = parity(a_keep, a_send).transpose(1, 2, 0, 3, 4).reshape(PARTS, -1, width)
        mats = [rows[:, i * unit:(i + 1) * unit].reshape(width, width) for i in range(3)]
        vectors = rows[0, 3 * unit:3 * unit + GROUP].astype(F32) + rows[0, 3 * unit + GROUP:].astype(F32)
        vectors = lax.psum(vectors, ("blk", "batch"))
        grad_down, grad_up, grad_out = over(down), over(up), over(out)
        grad_query, grad_key, grad_value = (over(m) for m in mats)
    r = own_vectors(vectors, share, shares)
    return (
        outputs, d_inputs, grad_query, r[B_QUERY], grad_key, grad_value, r[B_VALUE], grad_out, r[B_OUT],
        r[GAIN_ONE], r[SHIFT_ONE], grad_up, r[B_UP], grad_down, r[B_DOWN], r[GAIN_TWO], r[SHIFT_TWO],
    )


def solution(mesh):
    split, whole = P("batch", "blk", None), P()
    rows, vec = P("batch", None), P("batch")
    in_specs = (split, vec, rows, vec, rows) + (whole,) * 16 + (split,)
    out_specs = (split, split, rows, vec, rows, rows, vec, rows, vec, vec, vec, rows, vec, rows, vec, vec, vec)
    return jax.shard_map(body, mesh=mesh, in_specs=in_specs, out_specs=out_specs, check_vma=False)
```

```python
import functools

import jax
import jax.numpy as jnp
from jax import lax
from jax.experimental import pallas as pl
from jax.experimental.pallas import tpu as pltpu
from jax.sharding import PartitionSpec as P

HEADS = 12
HD = 64
SCALE = 0.125
NEGATIVE = -1e30
EPSILON = 1e-12
BF = jnp.bfloat16
F32 = jnp.float32
MIB = 1024 * 1024
GROUP = 16
PARTS = 8
DOWN_Z = 80
B_QUERY, B_VALUE, B_OUT, B_DOWN, GAIN_ONE, SHIFT_ONE, GAIN_TWO, SHIFT_TWO, B_UP = range(9)


def nn(a, b):
    return lax.dot_general(a, b, (((1,), (0,)), ((), ())), preferred_element_type=F32)


def nt(a, b):
    return lax.dot_general(a, b, (((1,), (1,)), ((), ())), preferred_element_type=F32)


def tn(a, b):
    return lax.dot_general(a, b, (((0,), (0,)), ((), ())), preferred_element_type=F32)


def head_lanes(shape, which):
    lane = lax.broadcasted_iota(jnp.int32, shape, 1)
    return (lane >= HD) if which else (lane < HD)


def norm_parts(v):
    width = v.shape[-1]
    centre = jnp.sum(v, axis=-1, keepdims=True) * (1.0 / width)
    centred = v - centre
    spread = jnp.sum(centred * centred, axis=-1, keepdims=True) * (1.0 / width)
    rstd = lax.rsqrt(spread + EPSILON)
    return centred * rstd, rstd


def norm_back(c2, n, rstd):
    width = c2.shape[-1]
    a = jnp.sum(c2, axis=-1, keepdims=True) * (1.0 / width)
    b = jnp.sum(c2 * n, axis=-1, keepdims=True) * (1.0 / width)
    return (c2 - a - n * b) * rstd


def colsum(v):
    return jnp.sum(v, axis=0, keepdims=True)


def wide_row(ref):
    return ref[...].astype(F32).reshape(1, ref.shape[0])


def block(i, size):
    return pl.ds(pl.multiple_of(i * size, size), size)


def own_blk():
    return lax.axis_index("blk")


def own_core():
    return lax.rem(lax.axis_index("batch"), 2)


def first_bit():
    return jnp.where(own_core() == 0, lax.rem(own_blk(), 2), lax.div(own_blk(), 2))


def second_bit():
    return jnp.where(own_core() == 0, lax.div(own_blk(), 2), lax.rem(own_blk(), 2))


def z_bits():
    z = lax.div(lax.axis_index("batch"), 2)
    return lax.rem(z, 2), lax.div(z, 2)


def fetch_kernel(ids_ref, counts_ref, spots_ref, table_ref, placed_ref, hit_ref, rows_ref, wide_ref, sel_ref, sem):
    slots = ids_ref.shape[1]
    me = own_blk()

    def start(j, carry):
        group = pl.multiple_of((ids_ref[me, j] // GROUP) * GROUP, GROUP)
        pltpu.make_async_copy(table_ref.at[pl.ds(group, GROUP), :], rows_ref.at[block(j, GROUP), :], sem).start()
        return carry

    lax.fori_loop(0, slots, start, 0, unroll=8)
    total = placed_ref.shape[0]
    spot = lax.broadcasted_iota(jnp.int32, (total, slots), 0)
    slot = lax.broadcasted_iota(jnp.int32, (total, slots), 1)
    hits = ((spots_ref[pl.ds(me, 1), :] == spot) & (slot < counts_ref[me])).astype(F32)
    hit_ref[...] = jnp.broadcast_to(jnp.sum(hits, axis=1, keepdims=True), hit_ref.shape)
    pltpu.make_async_copy(table_ref.at[pl.ds(0, slots * GROUP), :], rows_ref, sem).wait()
    wide_ref[...] = rows_ref[...].astype(F32)
    for j in range(slots):
        at = j * GROUP + lax.rem(ids_ref[me, j], GROUP)
        sel_ref[pl.ds(j, 1), :] = wide_ref[pl.ds(at, 1), :]
    placed_ref[...] = nn(hits.astype(BF), sel_ref[...].astype(BF)).astype(BF)


def attend_kernel(
    lengths_ref, inputs_ref, p1_ref, p2_ref, p3_ref, placed_ref, hit_ref, bq_ref, bv_ref, bo_ref,
    wq_ref, wk_ref, wv_ref, wo_ref,
    x_t_ref, q_ref, k_ref, v_ref, att_ref, max_ref, sum_ref, n_ref, rstd_ref,
    x_ref, att_rows,
):
    me = own_blk()
    length = lengths_ref[me]
    rows, width = x_ref.shape
    span = p1_ref.shape[0]
    for step, piece in enumerate((inputs_ref[me], p1_ref[...], p2_ref[...], p3_ref[...])):
        at = block(me ^ step, span)
        x_ref[at, :] = jnp.where(hit_ref[at, 0:1] > 0.5, placed_ref[at, :], piece)
    x_t_ref[...] = x_ref[...].T
    q = (nn(x_ref[...], wq_ref[...]) + wide_row(bq_ref)).astype(BF)
    q_ref[...] = (q.astype(F32) * SCALE).astype(BF)
    k_ref[...] = nn(x_ref[...], wk_ref[...]).astype(BF)
    v_ref[...] = (nn(x_ref[...], wv_ref[...]) + wide_row(bv_ref)).astype(BF)
    dead = jnp.where(lax.broadcasted_iota(jnp.int32, (rows, 1), 0) < length, 0.0, NEGATIVE)

    def pair(i, carry):
        lanes = block(i, 2 * HD)
        q2, k2 = q_ref[:, lanes], k_ref[:, lanes]
        v2t = v_ref[:, lanes].T
        for h in range(2):
            qm = jnp.where(head_lanes(q2.shape, h), q2, jnp.zeros_like(q2))
            s = nt(k2, qm) + dead
            top = jnp.max(s, axis=0, keepdims=True)
            p = jnp.exp(s - top)
            total = jnp.sum(p, axis=0, keepdims=True)
            o = nn(v2t[h * HD:(h + 1) * HD], p.astype(BF)) / total
            max_ref[2 * i + h] = top
            sum_ref[2 * i + h] = total
            att_ref[block(2 * i + h, HD), :] = o.astype(BF)
        att_rows[:, lanes] = att_ref[lanes, :].T
        return carry

    lax.fori_loop(0, HEADS // 2, pair, 0, unroll=True)
    branch = nn(att_rows[...], wo_ref[...]) + wide_row(bo_ref)
    n, rstd = norm_parts(x_ref[...].astype(F32) + branch)
    n_ref[...] = n
    rstd_ref[...] = jnp.broadcast_to(rstd, rstd_ref.shape)


def gelu_both(v):
    e = jnp.exp(v * v * -0.5)
    t = 1.0 / (1.0 + (0.3275911 * 0.7071067811865476) * jnp.abs(v))
    poly = t * (0.5 * 0.254829592 + t * (0.5 * -0.284496736 + t * (0.5 * 1.421413741 + t * (0.5 * -1.453152027 + t * (0.5 * 1.061405429)))))
    tail = poly * e
    phi = jnp.where(v >= 0, 1.0 - tail, tail)
    return v * phi, phi + v * (e * 0.3989422804014327)


def by_core(core, deal, keep, send):
    for c in range(2):

        @pl.when(core == c)
        def _():
            deal(c, *keep)
            deal(1 - c, *send)


OUT_GROUPS = [(0, 0), (0, 1), (1, 0), (1, 1), (2, 0), (3, 0)]


def ff_kernel(
    n_ref, cot_ref, c1_ref, c2_ref, c3_ref,
    bu_ref, bd_ref, g1_ref, s1_ref, g2_ref, s2_ref, wu_ref, wd_ref,
    out_ref, dkeep, dsend, ukeep, usend, dh_ref, dfirst_ref, vsum_ref,
    act, cot, nlow, nlow_t, dd, g_down, g_up,
):
    width = n_ref.shape[1]
    ff = wu_ref.shape[1]
    parts = ff // width
    shares = 2 * dkeep.shape[1]
    unit = width // shares
    span = c1_ref.shape[0]
    me, core = own_blk(), own_core()
    for hop, piece in enumerate((cot_ref[me], c1_ref[...], c2_ref[...], c3_ref[...])):
        cot[block(me ^ hop, span), :] = piece
    normed = n_ref[...] * wide_row(g1_ref) + wide_row(s1_ref)
    nlow[...] = normed.astype(BF)
    nlow_t[...] = nlow[...].T
    for i in range(parts):
        lanes = slice(i * width, (i + 1) * width)
        a, b = gelu_both(nn(nlow[...], wu_ref[:, lanes]) + wide_row(bu_ref)[:, lanes])
        act[:, lanes] = a.astype(BF)
        dh_ref[:, lanes] = b.astype(BF)
    normed = n_ref[...] * wide_row(g1_ref) + wide_row(s1_ref)
    resid = normed + nn(act[...], wd_ref[...]) + wide_row(bd_ref)
    n2, rstd2 = norm_parts(resid)
    out_ref[...] = (n2 * wide_row(g2_ref) + wide_row(s2_ref)).astype(BF)
    c = cot[...].astype(F32)
    vsum_ref[...] = jnp.zeros_like(vsum_ref)
    vsum_ref[GAIN_TWO:GAIN_TWO + 1] = colsum(c * n2)
    vsum_ref[SHIFT_TWO:SHIFT_TWO + 1] = colsum(c)
    d_r2 = norm_back(c * wide_row(g2_ref), n2, rstd2)
    dfirst_ref[...] = d_r2
    dd[...] = d_r2.astype(BF)
    vsum_ref[B_DOWN:B_DOWN + 1] = colsum(dd[...].astype(F32))

    def back(i, carry):
        lanes = block(i, width)
        g_down[...] = tn(act[:, lanes], dd[...]).astype(BF)
        dhc = (nt(dd[...], wd_ref[lanes, :]) * dh_ref[:, lanes].astype(F32)).astype(BF)
        dh_ref[:, lanes] = dhc
        vsum_ref[pl.ds(B_UP + i, 1)] = colsum(dhc.astype(F32))
        g_up[...] = nn(nlow_t[...], dhc).astype(BF)

        def deal(c, down, up):
            for p in range(4):
                at = (c * 4 + p) * unit
                down[p, i] = g_down[at:at + DOWN_Z]
                up[p, i, unit:] = g_down[at + DOWN_Z:at + unit]
            for z in range(shares // 2):
                at = (2 * z + c) * unit
                up[i, z, 0:unit] = g_up[at:at + unit]

        by_core(core, deal, (dkeep, ukeep), (dsend, usend))
        return carry

    lax.fori_loop(0, parts, back, 0)


def mixed_kernel(
    n_ref, rstd_ref, att_ref, dh_ref, dfirst_ref, vin_ref, g1_ref, wu_ref,
    okeep, osend, dr_ref, dd, vsum_ref,
    g_out,
):
    width = n_ref.shape[1]
    shares = 2 * okeep.shape[1]
    unit = width // shares
    d_f = dfirst_ref[...] + nt(dh_ref[...], wu_ref[...])
    n1 = n_ref[...]
    vsum_ref[...] = vin_ref[...]
    vsum_ref[GAIN_ONE:GAIN_ONE + 1] = colsum(d_f * n1)
    vsum_ref[SHIFT_ONE:SHIFT_ONE + 1] = colsum(d_f)
    d_r1 = norm_back(d_f * wide_row(g1_ref), n1, rstd_ref[:, 0:1])
    dr_ref[...] = d_r1
    db = d_r1.astype(BF)
    dd[...] = db
    vsum_ref[B_OUT:B_OUT + 1] = colsum(db.astype(F32))
    g_out[...] = nn(att_ref[...], dd[...]).astype(BF)

    def deal(c, out):
        for z in range(shares // 2):
            for g in range(unit // GROUP):
                p, at = OUT_GROUPS[g]
                src = (2 * z + c) * unit + g * GROUP
                out[p, z, at * GROUP:(at + 1) * GROUP] = g_out[src:src + GROUP]
            for p in (2, 3):
                out[p, z, GROUP:2 * GROUP] = jnp.zeros((GROUP, width), BF)

    by_core(own_core(), deal, (okeep,), (osend,))


def attended_kernel(att_ref, sum_ref, dd_ref, wo_ref, dst_ref, delta_ref, dm_ref):
    dm_ref[...] = nt(wo_ref[...], dd_ref[...])
    for i in range(HEADS):
        at = slice(i * HD, (i + 1) * HD)
        inv = 1.0 / sum_ref[i]
        delta_ref[i] = colsum(dm_ref[at, :] * att_ref[at, :].astype(F32)) * inv
        dst_ref[at, :] = (dm_ref[at, :] * inv).astype(BF)


def heads_kernel(first, lengths_ref, x_t_ref, vin_ref, q_ref, k_ref, v_ref, dst_ref, delta_ref, max_ref, dq, dk, dv, keep, *sends):
    *sends, g_ref = sends
    length = lengths_ref[own_blk()]
    rows = q_ref.shape[0]
    dead = jnp.where(lax.broadcasted_iota(jnp.int32, (rows, 1), 0) < length, 0.0, NEGATIVE)

    def pair(i, carry):
        lanes, own = block(first + i, 2 * HD), block(i, 2 * HD)
        q2, k2, v2 = q_ref[:, lanes], k_ref[:, lanes], v_ref[:, lanes]
        dst = dst_ref[lanes, :]
        ds2 = dst.T
        k2t = k2.T
        dv2 = jnp.zeros((rows, 2 * HD), F32)
        dk2 = jnp.zeros((rows, 2 * HD), F32)
        dqs = []
        for h in range(2):
            live = head_lanes(q2.shape, h)
            zero = jnp.zeros_like(q2)
            qm = jnp.where(live, q2, zero)
            s = nt(k2, qm) + dead
            head = 2 * (first + i) + h
            p = jnp.exp(s - max_ref[head])
            dp = nn(jnp.where(live, v2, zero), dst)
            dsc = (p * (dp - delta_ref[head])).astype(BF)
            dv2 = dv2 + nn(p.astype(BF), jnp.where(live, ds2, zero))
            dk2 = dk2 + nn(dsc, qm)
            dqs.append(nn(k2t[h * HD:(h + 1) * HD], dsc))
        dq[:, own] = (jnp.concatenate(dqs, axis=0) * SCALE).astype(BF).T
        dk[:, own] = dk2.astype(BF)
        dv[:, own] = dv2.astype(BF)
        return carry

    lax.fori_loop(0, dq.shape[1] // (2 * HD), pair, 0, unroll=True)
    for i, part in enumerate((dq, dk, dv)):
        g_ref[i] = nn(x_t_ref[...], part[...]).astype(BF)
    vsum = vin_ref[:, first * 2 * HD:first * 2 * HD + dq.shape[1]]
    row = lax.broadcasted_iota(jnp.int32, vsum.shape, 0)
    vsum = vsum + jnp.where(row == B_QUERY, colsum(dq[...].astype(F32)), 0.0) + jnp.where(row == B_VALUE, colsum(dv[...].astype(F32)), 0.0)
    high = vsum.astype(BF)
    low = (vsum - high.astype(F32)).astype(BF)
    shares = 2 * keep.shape[1]
    unit = x_t_ref.shape[0] // shares
    tall = keep.shape[2]

    def deal(c, *pieces):
        for z in range(shares // 2):
            for i in range(3):
                for j in range(unit // GROUP):
                    at, src = i * unit + j * GROUP, (2 * z + c) * unit + j * GROUP
                    pieces[at // tall][z, at % tall:at % tall + GROUP] = g_ref[i, src:src + GROUP]
            pieces[3][z, tall - 2 * GROUP:tall - GROUP] = high
            pieces[3][z, tall - GROUP:tall] = low

    per = 4 // len(sends)
    by_core(own_core(), deal, [keep.at[p] for p in range(4)], [sends[p // per].at[p % per] for p in range(4)])


def inputs_kernel(groups, hit_ref, out_page, dr_ref, wq_ref, wk_ref, wv_ref, *refs):
    parts = [refs[3 * g:3 * g + 3] for g in range(groups)]
    din_ref, *outs = refs[3 * groups:]
    total = dr_ref[...]
    for i, w in enumerate((wq_ref, wk_ref, wv_ref)):
        at = 0
        for part in parts:
            wide = part[i].shape[1]
            total = total + nt(part[i][...], w[:, at:at + wide])
            at += wide
    din_ref[...] = jnp.where(hit_ref[:, 0:1] > 0.5, 0.0, total).astype(BF)
    span = outs[0].shape[1]
    for i, out in enumerate(outs):
        rows = block(own_blk() ^ (i + 1), span)
        out[0] = out_page[rows, :]
        out[1] = din_ref[rows, :]


def added(a, b):
    return (a.astype(F32) + b.astype(F32)).astype(BF)


def halves_kernel(bit, came_parts, own, *refs):
    came, (*sends, keep) = refs[:came_parts], refs[came_parts:]
    rest = own.shape[1]
    per_came, per_send = 2 * rest // came_parts, rest // len(sends)
    mine = bit()
    for half in range(2):
        for keeps in (False, True):

            @pl.when((mine == half) == keeps)
            def _():
                for r in range(rest):
                    flat = half * rest + r
                    value = added(own[half, r], came[flat // per_came][flat % per_came])
                    if keeps:
                        keep[r] = value
                    else:
                        sends[r // per_send][r % per_send] = value


def joined_halves_kernel(bit, axis, cuts, *refs):
    owns, rest = refs[:len(cuts)], refs[len(cuts):]
    cames = []
    for n in cuts:
        cames.append(rest[:n])
        rest = rest[n:]
    send, keep = rest
    mine = bit()
    for half in range(2):
        for keeps, out in ((False, send), (True, keep)):

            @pl.when((mine == half) == keeps)
            def _():
                for r in range(out.shape[0]):
                    at = 0
                    for own, came in zip(owns, cames):
                        size = own.shape[1 + axis]
                        cut = slice(at, at + size)
                        index = (r, cut) if axis == 1 else (r, slice(None), cut)
                        out[index] = added(own[half, r], came[0][half, r] if len(came) == 1 else came[half][0, r])
                        at += size


def z_halves_kernel(came_parts, own, *refs):
    came, (*sends, keep) = refs[:came_parts], refs[came_parts:]
    pieces, depth = own.shape[:2]
    rest = depth // 2
    per_came, per_send = pieces * depth // came_parts, pieces * rest // len(sends)
    low, high = z_bits()
    core = own_core()
    for c in range(2):
        mine = low if (c == 0) == (depth == 4) else high
        for half in range(2):

            @pl.when((core == c) & (mine == half))
            def _():
                for p in range(pieces):
                    for r in range(rest):
                        for keeps in (False, True):
                            h = half if keeps else 1 - half
                            z = h if depth == 2 else 2 * r + h if c == 0 else 2 * h + r
                            flat = p * depth + z
                            value = added(own[p, z], came[flat // per_came][flat % per_came])
                            out = p * rest + r
                            if keeps:
                                keep[out] = value
                            else:
                                sends[out // per_send][out % per_send] = value


def sum_kernel(own, came, out):
    out[...] = added(own[...].reshape(out.shape), came[...].reshape(out.shape))


def pair_kernel(own, came, out):
    lo = second_bit()
    out[lo] = own[...]
    out[1 - lo] = came[...]


def last_kernel(place, own, came, *refs):
    mine = first_bit()
    for half in range(2):
        @pl.when(mine == half)
        def _():
            for j in range(2):
                place(2 * half + j, own, j, *refs)
                place(2 * (1 - half) + j, came, j, *refs)


def place_up(p, ref, j, up, out, tail):
    unit, width = out.shape
    end = unit + tail.shape[1]
    up[:, p * width:(p + 1) * width] = ref[j, 0:unit].astype(F32)
    tail[p] = ref[j, unit:end].astype(F32)
    for g, (piece, at) in enumerate(OUT_GROUPS):
        if piece == p:
            out[g * GROUP:(g + 1) * GROUP] = ref[j, end + at * GROUP:end + (at + 1) * GROUP].astype(F32)


def place_down(p, ref, j, tail, down):
    unit = down.shape[0] // 4
    down[p * unit:p * unit + DOWN_Z] = ref[j].astype(F32)
    down[p * unit + DOWN_Z:(p + 1) * unit] = tail[p]


def place_rows(p, ref, j, query, key, value, vectors):
    unit = query.shape[0]
    tall = ref.shape[1]
    for g in range(tall // GROUP):
        at = p * tall + g * GROUP
        part = ref[j, g * GROUP:(g + 1) * GROUP].astype(F32)
        if at < 3 * unit:
            (query, key, value)[at // unit][at % unit:at % unit + GROUP] = part
        elif at == 3 * unit:
            vectors[...] = part + ref[j, (g + 1) * GROUP:(g + 2) * GROUP].astype(F32)


def page_rows_kernel(out_page, d_page, *refs):
    *came, out_rows, d_rows = refs
    span = out_rows.shape[1]
    me = own_blk()
    for which, (page, out) in enumerate(((out_page, out_rows), (d_page, d_rows))):
        out[me] = page[block(me, span), :]
        for i, part in enumerate(came):
            out[me ^ (i + 1)] = part[which]


VM = pl.BlockSpec(memory_space=pltpu.VMEM)
SM = pl.BlockSpec(memory_space=pltpu.SMEM)
HB = pl.BlockSpec(memory_space=pl.ANY)


def call(kernel, args, places, outs, scratch, limit):
    return pl.pallas_call(
        kernel,
        out_shape=[jax.ShapeDtypeStruct(s, d) for s, d in outs],
        in_specs=places,
        out_specs=[VM] * len(outs),
        scratch_shapes=[s if not isinstance(s, tuple) else pltpu.VMEM(*s) for s in scratch],
        compiler_params=pltpu.CompilerParams(vmem_limit_bytes=limit * MIB),
        cost_estimate=pl.CostEstimate(flops=1024, bytes_accessed=1024, transcendentals=0),
    )(*args)


def fetch(ids, counts, spots, table, rows):
    width = table.shape[1]
    slots = ids.shape[1]
    return call(
        fetch_kernel, (ids, counts, spots, table), [SM, SM, VM, HB], [((rows, width), BF), ((rows, 128), F32)],
        [((slots * GROUP, width), BF), ((slots * GROUP, width), F32), ((slots, width), F32), pltpu.SemaphoreType.DMA], LIMITS[0],
    )


LIMITS = [44, 16, 20, 8, 16, 10, 4]


def attend(lengths, inputs, pieces, placed, hit, biases, wq, wk, wv, wo):
    span, width = pieces[0].shape
    rows = 4 * span
    args = (lengths, inputs, *pieces, placed, hit, *biases, wq, wk, wv, wo)
    outs = [((width, rows), BF)] + [((rows, width), BF)] * 3 + [((width, rows), BF), ((HEADS, 1, rows), F32), ((HEADS, 1, rows), F32), ((rows, width), F32), ((rows, 128), F32)]
    return call(attend_kernel, args, [SM] + [VM] * 13, outs, [((rows, width), BF)] * 2, LIMITS[1])


def feed(n, cotangent, pieces, vecs, wu, wd):
    rows, width = n.shape
    ff = wu.shape[1]
    args = (n, cotangent, *pieces, *vecs, wu, wd)
    unit = width // PARTS
    groups = [((4, PARTS // 2, tall, width), BF) for tall in (DOWN_Z, 2 * unit - DOWN_Z)]
    outs = [((rows, width), BF)] + [groups[0]] * 2 + [groups[1]] * 2 + [((rows, ff), BF), ((rows, width), F32), ((16, width), F32)]
    scratch = [((rows, ff), BF)] + [((rows, width), BF)] * 2 + [((width, rows), BF), ((rows, width), BF)] + [((width, width), BF)] * 2
    return call(ff_kernel, args, [VM] * len(args), outs, scratch, LIMITS[2])


def mixed_back(n, rstd, att, dh, dfirst, vsum, gain, wu):
    rows, width = n.shape
    args = (n, rstd, att, dh, dfirst, vsum, gain, wu)
    group = ((4, PARTS // 2, 2 * GROUP, width), BF)
    outs = [group] * 2 + [((rows, width), F32), ((rows, width), BF), (vsum.shape, F32)]
    return call(mixed_kernel, args, [VM] * len(args), outs, [((width, width), BF)], LIMITS[5])


def attended_back(att, sums, dd, wo):
    rows, width = dd.shape
    outs = [((width, rows), BF), ((HEADS, 1, rows), F32)]
    return call(attended_kernel, (att, sums, dd, wo), [VM] * 4, outs, [((width, rows), F32)], LIMITS[5])


def heads(first, count, cuts, lengths, x_t, vsum, q, k, v, dst, delta, tops):
    width, rows = x_t.shape
    wide = count * HD
    tall = (3 * (width // PARTS) + 2 * GROUP) // 4
    args = (lengths, x_t, vsum, q, k, v, dst, delta, tops)
    outs = [((rows, wide), BF)] * 3 + [((4, PARTS // 2, tall, wide), BF)] + [((4 // cuts, PARTS // 2, tall, wide), BF)] * cuts
    return call(functools.partial(heads_kernel, first // 2), args, [SM] + [VM] * 8, outs, [((3, width, wide), BF)], LIMITS[3])


def inputs_grad(span, hit, out_page, dr, wq, wk, wv, parts):
    rows, width = dr.shape
    args = (hit, out_page, dr, wq, wk, wv) + tuple(t for part in parts for t in part)
    outs = [(dr.shape, BF)] + [((2, span, width), BF)] * (rows // span - 1)
    return call(functools.partial(inputs_kernel, len(parts)), args, [VM] * len(args), outs, [], LIMITS[5])


def pick(array, index, axis=0):
    return lax.dynamic_index_in_dim(array, index, axis, keepdims=False)


def swap(array, bit):
    return lax.ppermute(array, "blk", [(i, i ^ bit) for i in range(lax.axis_size("blk"))])


def swap_first(array, first):
    blks, shares = lax.axis_size("blk"), lax.axis_size("batch")
    perm = []
    for b in range(blks):
        for s in range(shares):
            bit = 1 if (s % 2 == 0) == first else 2
            perm.append((b * shares + s, (b ^ bit) * shares + s))
    return lax.ppermute(array, ("blk", "batch"), perm)


def swap_batch(array, bit):
    return lax.ppermute(array, "batch", [(i, i ^ bit) for i in range(lax.axis_size("batch"))])


def swap_z(array, first):
    shares = lax.axis_size("batch")
    return lax.ppermute(array, "batch", [(i, i ^ (2 if (i % 2 == 0) == first else 4)) for i in range(shares)])


class Cell:
    def __init__(self, *values):
        self.values = values


class Order:
    def __init__(self):
        self.last = Cell()

    def enter(self, *arrays):
        tied = lax.optimization_barrier((*arrays, *self.last.values))
        self.last.values = tied[len(arrays):]
        return tied[:len(arrays)]

    def leave(self, cell):
        self.last = cell


class Chain:
    def __init__(self, order, cell, send):
        self.order = order
        self.own, self.came = cell, tuple(swap_batch(s, 1) for s in send)

    @classmethod
    def joined(cls, order, axis, cells, cames):
        chain = cls(order, None, ())
        groups = len(cells)
        tied = order.enter(*(c.values[0] for c in cells), *(t for came in cames for t in came))
        shape = tied[0].shape
        flat = [shape[0] * shape[1] // 2, shape[2], shape[3]]
        flat[axis] = sum(t.shape[axis + 1] for t in tied[:groups])
        args = [t.reshape((-1, flat[0]) + t.shape[2:]) for t in tied]
        kernel = functools.partial(joined_halves_kernel, first_bit, axis, [len(came) for came in cames])
        send, keep = call(kernel, args, [VM] * len(args), [(tuple(flat), BF)] * 2, [], LIMITS[6])
        chain.came = [swap_first(send, True)]
        chain.own = Cell(keep.reshape((shape[0] // 2, shape[1], flat[1], flat[2])))
        order.leave(chain.own)
        return chain

    def halve(self, axis, bit, move, cuts):
        own, *came = self.order.enter(self.own.values[0], *self.came)
        shape = own.shape
        after = shape[:axis] + (shape[axis] // 2,) + shape[axis + 1:]
        flat = (after[0] * after[1],) + shape[2:]
        if axis == 0:
            own = own.reshape((2,) + flat)
            kernel = functools.partial(halves_kernel, bit, len(came))
        else:
            kernel = functools.partial(z_halves_kernel, len(came))
        came = [c.reshape((-1,) + shape[2:]) for c in came]
        outs = [((flat[0] // cuts,) + shape[2:], BF)] * cuts + [(flat, BF)]
        *sends, keep = call(kernel, (own, *came), [VM] * (1 + len(came)), outs, [], LIMITS[6])
        self.came = [move(send) for send in sends]
        self.own = Cell(keep.reshape(after))
        self.order.leave(self.own)

    def first(self, cuts=1):
        self.halve(0, first_bit, lambda v: swap_first(v, True), cuts)

    def second(self, cuts=1):
        self.halve(0, second_bit, lambda v: swap_first(v, False), cuts)

    def z_first(self, cuts=1):
        self.halve(1, None, lambda v: swap_z(v, True), cuts)

    def z_second(self, cuts=1):
        self.halve(1, None, lambda v: swap_z(v, False), cuts)

    def gather_second(self):
        own, came = self.order.enter(self.own.values[0], *self.came)
        out, = call(sum_kernel, (own, came), [VM] * 2, [(own.shape[2:], BF)], [], LIMITS[6])
        self.own = Cell(out)
        self.came = (swap_first(out, False),)
        self.order.leave(self.own)

    def gather_first(self):
        own, came = self.order.enter(self.own.values[0], *self.came)
        out, = call(pair_kernel, (own, came), [VM] * 2, [((2,) + own.shape, BF)], [], LIMITS[6])
        self.own = Cell(out)
        self.came = (swap_first(out, True),)
        self.order.leave(self.own)

    def result(self, place, shapes, *others):
        own, came = self.order.enter(self.own.values[0], *self.came)
        args = (own, came, *others)
        return call(functools.partial(last_kernel, place), args, [VM] * len(args), [(s, F32) for s in shapes], [], LIMITS[6])


def own_vectors(vec, share, shares):
    width = vec.shape[-1]
    n = width // shares
    cut = lax.dynamic_slice_in_dim(vec, share * n, n, 1)
    flat = vec[B_UP:B_UP + 4].reshape(-1)
    return [cut[i] for i in range(B_UP)] + [lax.dynamic_slice_in_dim(flat, share * 4 * n, 4 * n, 0)]


def body(
    inputs, lengths, positions, counts, token_ids, table,
    w_query, b_query, w_key, w_value, b_value, w_out, b_out, gain_one, shift_one,
    w_up, b_up, w_down, b_down, gain_two, shift_two, cotangent,
):
    blk, share = lax.axis_index("blk"), lax.axis_index("batch")
    shares = lax.axis_size("batch")
    core = share % 2
    pages, span, width = inputs.shape
    ff = w_up.shape[1]
    unit = width // PARTS
    rows_in = [swap(pick(inputs, blk ^ i), i) for i in range(1, pages)]
    placed, hit = fetch(token_ids, counts, positions, table, pages * span)
    back, hit = lax.optimization_barrier((cotangent, hit))
    back_in = [swap(pick(back, blk ^ i), i) for i in range(1, pages)]
    x_t, q, k, v, att, tops, sums, n1, rstd = attend(
        lengths, inputs, rows_in, placed, hit, (b_query, b_value, b_out), w_query, w_key, w_value, w_out
    )
    out_page, d_keep, d_send, u_keep, u_send, dh, dfirst, vsum = feed(
        n1, cotangent, back_in, (b_up, b_down, gain_one, shift_one, gain_two, shift_two), w_up, w_down
    )

    def to_mixed(n1, vsum):
        return mixed_back(n1, rstd, att, dh, dfirst, vsum, gain_one, w_up)

    order = Order()

    def attention_back(first, count, vsum, dst, delta, cuts=1):
        delta, = order.enter(delta)
        dq, dk, dv, keep, *send = heads(first, count, cuts, lengths, x_t, vsum, q, k, v, dst, delta, tops)
        parts = [dq, dk, dv]
        grads = Cell(keep)
        order.leave(grads)
        return parts, grads, send

    def page_rows(out_page, d_page, came):
        return call(page_rows_kernel, (out_page, d_page, *came), [VM] * (pages + 1), [(inputs.shape, BF)] * 2, [], LIMITS[6])

    if shares == PARTS and lax.axis_size("blk") == 4:
        d = Chain(order, Cell(d_keep), [d_send])
        u_came = swap_batch(u_send, 1)
        n_now, = order.enter(n1)
        o_keep, o_send, d_r1, d_branch, vsum = to_mixed(n_now, vsum)
        o_cell = Cell(o_keep)
        order.leave(o_cell)
        o_came = swap_batch(o_send, 1)
        att_now, = order.enter(att)
        sums_cell = Cell(*attended_back(att_now, sums, d_branch, w_out))
        order.leave(sums_cell)
        d.z_first()
        u = Chain.joined(order, 1, [Cell(u_keep), o_cell], [[u_came], [o_came]])
        groups = [attention_back(0, 8, vsum, *sums_cell.values, cuts=2)]
        groups.append(attention_back(8, 4, vsum, *sums_cell.values))
        parts = [g[0] for g in groups]
        a = Chain.joined(order, 2, [g[1] for g in groups], [[swap_batch(t, 1) for t in g[2]] for g in groups])
        d.z_second()
        u.second()
        hit_now, = order.enter(hit)
        d_page, *page_parts = inputs_grad(span, hit_now, out_page, d_r1, w_query, w_key, w_value, parts)
        d_cell = Cell(d_page)
        order.leave(d_cell)
        page_parts = [swap(part, i + 1) for i, part in enumerate(page_parts)]
        a.second()
        u.z_first()
        d.first()
        a.z_first()
        u.z_second()
        d.second()
        a.z_second()
        u.gather_second()
        d.gather_second()
        d_page, *came = order.enter(*d_cell.values, *page_parts)
        rows_cell = Cell(*page_rows(out_page, d_page, came))
        order.leave(rows_cell)
        a.gather_second()
        a.gather_first()
        u.gather_first()
        d.gather_first()
        grad_up, grad_out, tail = u.result(place_up, [(unit, ff), (unit, width), (4, unit - DOWN_Z, width)])
        grad_down, = d.result(place_down, [(ff // PARTS, width)], tail)
        grad_query, grad_key, grad_value, vectors = a.result(place_rows, [(unit, width)] * 3 + [(GROUP, width)])
        outputs, d_inputs = rows_cell.values
    else:
        o_keep, o_send, d_r1, d_branch, vsum = to_mixed(n1, vsum)
        attended = attended_back(att, sums, d_branch, w_out)
        groups = [attention_back(i, 4, vsum, *attended) for i in range(0, HEADS, 4)]
        a_keep = jnp.concatenate([g[1].values[0] for g in groups], axis=-1)
        a_send = jnp.concatenate([g[2][0] for g in groups], axis=-1)
        d_page, *page_parts = inputs_grad(span, hit, out_page, d_r1, w_query, w_key, w_value, [g[0] for g in groups])
        came = [swap(part, i + 1) for i, part in enumerate(page_parts)]
        outputs, d_inputs = page_rows(out_page, d_page, came)

        def parity(keep, send):
            packed = jnp.where(core == 0, jnp.stack([keep, send]), jnp.stack([send, keep]))
            return packed.transpose(1, 2, 0, 3, 4)

        def over(grad):
            part = lax.psum_scatter(grad.astype(F32), "batch", scatter_dimension=0, tiled=True)
            return lax.psum(part.astype(BF), "blk").astype(F32)

        out = parity(o_keep, o_send)
        out = jnp.concatenate([out[p][..., at * GROUP:(at + 1) * GROUP, :] for p, at in OUT_GROUPS], axis=-2)
        out = out.reshape(width, width)
        up = parity(u_keep, u_send)
        down = jnp.concatenate([parity(d_keep, d_send), up[..., unit:, :]], axis=-2)
        down = down.transpose(1, 2, 0, 3, 4).reshape(ff, width)
        up = up[..., :unit, :].transpose(1, 2, 3, 0, 4).reshape(width, ff)
        rows = parity(a_keep, a_send).transpose(1, 2, 0, 3, 4).reshape(PARTS, -1, width)
        mats = [rows[:, i * unit:(i + 1) * unit].reshape(width, width) for i in range(3)]
        vectors = rows[0, 3 * unit:3 * unit + GROUP].astype(F32) + rows[0, 3 * unit + GROUP:].astype(F32)
        vectors = lax.psum(vectors, ("blk", "batch"))
        grad_down, grad_up, grad_out = over(down), over(up), over(out)
        grad_query, grad_key, grad_value = (over(m) for m in mats)
    r = own_vectors(vectors, share, shares)
    return (
        outputs, d_inputs, grad_query, r[B_QUERY], grad_key, grad_value, r[B_VALUE], grad_out, r[B_OUT],
        r[GAIN_ONE], r[SHIFT_ONE], grad_up, r[B_UP], grad_down, r[B_DOWN], r[GAIN_TWO], r[SHIFT_TWO],
    )


def solution(mesh):
    split, whole = P("batch", "blk", None), P()
    rows, vec = P("batch", None), P("batch")
    in_specs = (split, vec, rows, vec, rows) + (whole,) * 16 + (split,)
    out_specs = (split, split, rows, vec, rows, rows, vec, rows, vec, vec, vec, rows, vec, rows, vec, vec, vec)
    return jax.shard_map(body, mesh=mesh, in_specs=in_specs, out_specs=out_specs, check_vma=False)
```

```python
import functools

import jax
import jax.numpy as jnp
from jax import lax
from jax.experimental import pallas as pl
from jax.experimental.pallas import tpu as pltpu
from jax.sharding import PartitionSpec as P

HEADS = 12
HD = 64
SCALE = 0.125
NEGATIVE = -1e30
EPSILON = 1e-12
BF = jnp.bfloat16
F32 = jnp.float32
MIB = 1024 * 1024
GROUP = 16
PARTS = 8
DOWN_Z = 80
B_QUERY, B_VALUE, B_OUT, B_DOWN, GAIN_ONE, SHIFT_ONE, GAIN_TWO, SHIFT_TWO, B_UP = range(9)


def nn(a, b):
    return lax.dot_general(a, b, (((1,), (0,)), ((), ())), preferred_element_type=F32)


def nt(a, b):
    return lax.dot_general(a, b, (((1,), (1,)), ((), ())), preferred_element_type=F32)


def tn(a, b):
    return lax.dot_general(a, b, (((0,), (0,)), ((), ())), preferred_element_type=F32)


def head_lanes(shape, which):
    lane = lax.broadcasted_iota(jnp.int32, shape, 1)
    return (lane >= HD) if which else (lane < HD)


def norm_parts(v):
    width = v.shape[-1]
    centre = jnp.sum(v, axis=-1, keepdims=True) * (1.0 / width)
    centred = v - centre
    spread = jnp.sum(centred * centred, axis=-1, keepdims=True) * (1.0 / width)
    rstd = lax.rsqrt(spread + EPSILON)
    return centred * rstd, rstd


def norm_back(c2, n, rstd):
    width = c2.shape[-1]
    a = jnp.sum(c2, axis=-1, keepdims=True) * (1.0 / width)
    b = jnp.sum(c2 * n, axis=-1, keepdims=True) * (1.0 / width)
    return (c2 - a - n * b) * rstd


def colsum(v):
    return jnp.sum(v, axis=0, keepdims=True)


def wide_row(ref):
    return ref[...].astype(F32).reshape(1, ref.shape[0])


def block(i, size):
    return pl.ds(pl.multiple_of(i * size, size), size)


def own_blk():
    return lax.axis_index("blk")


def own_core():
    return lax.rem(lax.axis_index("batch"), 2)


def first_bit():
    return jnp.where(own_core() == 0, lax.rem(own_blk(), 2), lax.div(own_blk(), 2))


def second_bit():
    return jnp.where(own_core() == 0, lax.div(own_blk(), 2), lax.rem(own_blk(), 2))


def z_bits():
    z = lax.div(lax.axis_index("batch"), 2)
    return lax.rem(z, 2), lax.div(z, 2)


def fetch_kernel(ids_ref, counts_ref, spots_ref, table_ref, placed_ref, hit_ref, rows_ref, wide_ref, sel_ref, sem):
    slots = ids_ref.shape[1]
    me = own_blk()

    def start(j, carry):
        group = pl.multiple_of((ids_ref[me, j] // GROUP) * GROUP, GROUP)
        pltpu.make_async_copy(table_ref.at[pl.ds(group, GROUP), :], rows_ref.at[block(j, GROUP), :], sem).start()
        return carry

    lax.fori_loop(0, slots, start, 0, unroll=8)
    total = placed_ref.shape[0]
    spot = lax.broadcasted_iota(jnp.int32, (total, slots), 0)
    slot = lax.broadcasted_iota(jnp.int32, (total, slots), 1)
    hits = ((spots_ref[pl.ds(me, 1), :] == spot) & (slot < counts_ref[me])).astype(F32)
    hit_ref[...] = jnp.broadcast_to(jnp.sum(hits, axis=1, keepdims=True), hit_ref.shape)
    pltpu.make_async_copy(table_ref.at[pl.ds(0, slots * GROUP), :], rows_ref, sem).wait()
    wide_ref[...] = rows_ref[...].astype(F32)

    def select(j, carry):
        at = j * GROUP + lax.rem(ids_ref[me, j], GROUP)
        sel_ref[pl.ds(j, 1), :] = wide_ref[pl.ds(at, 1), :]
        return carry

    lax.fori_loop(0, slots, select, 0, unroll=8)
    placed_ref[...] = nn(hits.astype(BF), sel_ref[...].astype(BF)).astype(BF)


def attend_kernel(
    lengths_ref, inputs_ref, p1_ref, p2_ref, p3_ref, placed_ref, hit_ref, bq_ref, bv_ref, bo_ref,
    wq_ref, wk_ref, wv_ref, wo_ref,
    x_t_ref, q_ref, k_ref, v_ref, att_ref, max_ref, sum_ref, n_ref, rstd_ref,
    x_ref, att_rows,
):
    me = own_blk()
    length = lengths_ref[me]
    rows, width = x_ref.shape
    span = p1_ref.shape[0]
    for step, piece in enumerate((inputs_ref[me], p1_ref[...], p2_ref[...], p3_ref[...])):
        at = block(me ^ step, span)
        x_ref[at, :] = jnp.where(hit_ref[at, 0:1] > 0.5, placed_ref[at, :], piece)
    x_t_ref[...] = x_ref[...].T
    q = (nn(x_ref[...], wq_ref[...]) + wide_row(bq_ref)).astype(BF)
    q_ref[...] = (q.astype(F32) * SCALE).astype(BF)
    k_ref[...] = nn(x_ref[...], wk_ref[...]).astype(BF)
    v_ref[...] = (nn(x_ref[...], wv_ref[...]) + wide_row(bv_ref)).astype(BF)
    dead = jnp.where(lax.broadcasted_iota(jnp.int32, (rows, 1), 0) < length, 0.0, NEGATIVE)

    def pair(i, carry):
        lanes = block(i, 2 * HD)
        q2, k2 = q_ref[:, lanes], k_ref[:, lanes]
        v2t = v_ref[:, lanes].T
        for h in range(2):
            qm = jnp.where(head_lanes(q2.shape, h), q2, jnp.zeros_like(q2))
            s = nt(k2, qm) + dead
            top = jnp.max(s, axis=0, keepdims=True)
            p = jnp.exp(s - top)
            total = jnp.sum(p, axis=0, keepdims=True)
            o = nn(v2t[h * HD:(h + 1) * HD], p.astype(BF)) / total
            max_ref[2 * i + h] = top
            sum_ref[2 * i + h] = total
            att_ref[block(2 * i + h, HD), :] = o.astype(BF)
        att_rows[:, lanes] = att_ref[lanes, :].T
        return carry

    lax.fori_loop(0, HEADS // 2, pair, 0, unroll=True)
    branch = nn(att_rows[...], wo_ref[...]) + wide_row(bo_ref)
    n, rstd = norm_parts(x_ref[...].astype(F32) + branch)
    n_ref[...] = n
    rstd_ref[...] = jnp.broadcast_to(rstd, rstd_ref.shape)


def gelu_both(v):
    e = jnp.exp(v * v * -0.5)
    t = 1.0 / (1.0 + (0.3275911 * 0.7071067811865476) * jnp.abs(v))
    poly = t * (0.5 * 0.254829592 + t * (0.5 * -0.284496736 + t * (0.5 * 1.421413741 + t * (0.5 * -1.453152027 + t * (0.5 * 1.061405429)))))
    tail = poly * e
    phi = jnp.where(v >= 0, 1.0 - tail, tail)
    return v * phi, phi + v * (e * 0.3989422804014327)


def by_core(core, deal, keep, send):
    for c in range(2):

        @pl.when(core == c)
        def _():
            deal(c, *keep)
            deal(1 - c, *send)


OUT_GROUPS = [(0, 0), (0, 1), (1, 0), (1, 1), (2, 0), (3, 0)]


def ff_kernel(
    n_ref, cot_ref, c1_ref, c2_ref, c3_ref,
    bu_ref, bd_ref, g1_ref, s1_ref, g2_ref, s2_ref, wu_ref, wd_ref,
    out_ref, dkeep, dsend, ukeep, usend, dh_ref, dfirst_ref, vsum_ref,
    act, cot, nlow, nlow_t, dd, g_down, g_up,
):
    width = n_ref.shape[1]
    ff = wu_ref.shape[1]
    parts = ff // width
    shares = 2 * dkeep.shape[1]
    unit = width // shares
    span = c1_ref.shape[0]
    me, core = own_blk(), own_core()
    for hop, piece in enumerate((cot_ref[me], c1_ref[...], c2_ref[...], c3_ref[...])):
        cot[block(me ^ hop, span), :] = piece
    normed = n_ref[...] * wide_row(g1_ref) + wide_row(s1_ref)
    nlow[...] = normed.astype(BF)
    nlow_t[...] = nlow[...].T
    for i in range(parts):
        lanes = slice(i * width, (i + 1) * width)
        a, b = gelu_both(nn(nlow[...], wu_ref[:, lanes]) + wide_row(bu_ref)[:, lanes])
        act[:, lanes] = a.astype(BF)
        dh_ref[:, lanes] = b.astype(BF)
    normed = n_ref[...] * wide_row(g1_ref) + wide_row(s1_ref)
    resid = normed + nn(act[...], wd_ref[...]) + wide_row(bd_ref)
    n2, rstd2 = norm_parts(resid)
    out_ref[...] = (n2 * wide_row(g2_ref) + wide_row(s2_ref)).astype(BF)
    c = cot[...].astype(F32)
    vsum_ref[...] = jnp.zeros_like(vsum_ref)
    vsum_ref[GAIN_TWO:GAIN_TWO + 1] = colsum(c * n2)
    vsum_ref[SHIFT_TWO:SHIFT_TWO + 1] = colsum(c)
    d_r2 = norm_back(c * wide_row(g2_ref), n2, rstd2)
    dfirst_ref[...] = d_r2
    dd[...] = d_r2.astype(BF)
    vsum_ref[B_DOWN:B_DOWN + 1] = colsum(dd[...].astype(F32))

    def back(i, carry):
        lanes = block(i, width)
        g_down[...] = tn(act[:, lanes], dd[...]).astype(BF)
        dhc = (nt(dd[...], wd_ref[lanes, :]) * dh_ref[:, lanes].astype(F32)).astype(BF)
        dh_ref[:, lanes] = dhc
        vsum_ref[pl.ds(B_UP + i, 1)] = colsum(dhc.astype(F32))
        g_up[...] = nn(nlow_t[...], dhc).astype(BF)

        def deal(c, down, up):
            for p in range(4):
                at = (c * 4 + p) * unit
                down[p, i] = g_down[at:at + DOWN_Z]
                up[p, i, unit:] = g_down[at + DOWN_Z:at + unit]
            for z in range(shares // 2):
                at = (2 * z + c) * unit
                up[i, z, 0:unit] = g_up[at:at + unit]

        by_core(core, deal, (dkeep, ukeep), (dsend, usend))
        return carry

    lax.fori_loop(0, parts, back, 0)


def mixed_kernel(
    n_ref, rstd_ref, att_ref, dh_ref, dfirst_ref, vin_ref, g1_ref, wu_ref,
    okeep, osend, dr_ref, dd, vsum_ref,
    g_out,
):
    width = n_ref.shape[1]
    shares = 2 * okeep.shape[1]
    unit = width // shares

    def first(i, carry):
        lanes = block(i, width // 3)
        dr_ref[:, lanes] = dfirst_ref[:, lanes] + nt(dh_ref[...], wu_ref[lanes, :])
        return carry

    lax.fori_loop(0, 3, first, 0)
    d_f = dr_ref[...]
    n1 = n_ref[...]
    vsum_ref[...] = vin_ref[...]
    vsum_ref[GAIN_ONE:GAIN_ONE + 1] = colsum(d_f * n1)
    vsum_ref[SHIFT_ONE:SHIFT_ONE + 1] = colsum(d_f)
    d_r1 = norm_back(d_f * wide_row(g1_ref), n1, rstd_ref[:, 0:1])
    dr_ref[...] = d_r1
    db = d_r1.astype(BF)
    dd[...] = db
    vsum_ref[B_OUT:B_OUT + 1] = colsum(db.astype(F32))
    g_out[...] = nn(att_ref[...], dd[...]).astype(BF)

    def deal(c, out):
        for z in range(shares // 2):
            for g in range(unit // GROUP):
                p, at = OUT_GROUPS[g]
                src = (2 * z + c) * unit + g * GROUP
                out[p, z, at * GROUP:(at + 1) * GROUP] = g_out[src:src + GROUP]
            for p in (2, 3):
                out[p, z, GROUP:2 * GROUP] = jnp.zeros((GROUP, width), BF)

    by_core(own_core(), deal, (okeep,), (osend,))


def attended_kernel(att_ref, sum_ref, dd_ref, wo_ref, dst_ref, delta_ref, dm_ref):
    dm_ref[...] = nt(wo_ref[...], dd_ref[...])
    for i in range(HEADS):
        at = slice(i * HD, (i + 1) * HD)
        inv = 1.0 / sum_ref[i]
        delta_ref[i] = colsum(dm_ref[at, :] * att_ref[at, :].astype(F32)) * inv
        dst_ref[at, :] = (dm_ref[at, :] * inv).astype(BF)


def heads_kernel(first, lengths_ref, x_t_ref, vin_ref, q_ref, k_ref, v_ref, dst_ref, delta_ref, max_ref, dq, dk, dv, keep, *sends):
    *sends, g_ref = sends
    length = lengths_ref[own_blk()]
    rows = q_ref.shape[0]
    dead = jnp.where(lax.broadcasted_iota(jnp.int32, (rows, 1), 0) < length, 0.0, NEGATIVE)

    def pair(i, carry):
        lanes, own = block(first + i, 2 * HD), block(i, 2 * HD)
        q2, k2, v2 = q_ref[:, lanes], k_ref[:, lanes], v_ref[:, lanes]
        dst = dst_ref[lanes, :]
        ds2 = dst.T
        k2t = k2.T
        dv2 = jnp.zeros((rows, 2 * HD), F32)
        dk2 = jnp.zeros((rows, 2 * HD), F32)
        dqs = []
        for h in range(2):
            live = head_lanes(q2.shape, h)
            zero = jnp.zeros_like(q2)
            qm = jnp.where(live, q2, zero)
            s = nt(k2, qm) + dead
            head = 2 * (first + i) + h
            p = jnp.exp(s - max_ref[head])
            dp = nn(jnp.where(live, v2, zero), dst)
            dsc = (p * (dp - delta_ref[head])).astype(BF)
            dv2 = dv2 + nn(p.astype(BF), jnp.where(live, ds2, zero))
            dk2 = dk2 + nn(dsc, qm)
            dqs.append(nn(k2t[h * HD:(h + 1) * HD], dsc))
        dq[:, own] = (jnp.concatenate(dqs, axis=0) * SCALE).astype(BF).T
        dk[:, own] = dk2.astype(BF)
        dv[:, own] = dv2.astype(BF)
        return carry

    lax.fori_loop(0, dq.shape[1] // (2 * HD), pair, 0)
    for i, part in enumerate((dq, dk, dv)):
        g_ref[i] = nn(x_t_ref[...], part[...]).astype(BF)
    vsum = vin_ref[:, first * 2 * HD:first * 2 * HD + dq.shape[1]]
    row = lax.broadcasted_iota(jnp.int32, vsum.shape, 0)
    vsum = vsum + jnp.where(row == B_QUERY, colsum(dq[...].astype(F32)), 0.0) + jnp.where(row == B_VALUE, colsum(dv[...].astype(F32)), 0.0)
    high = vsum.astype(BF)
    low = (vsum - high.astype(F32)).astype(BF)
    shares = 2 * keep.shape[1]
    unit = x_t_ref.shape[0] // shares
    tall = keep.shape[2]

    def deal(c, *pieces):
        def one(z, carry):
            for i in range(3):
                for j in range(unit // GROUP):
                    at = i * unit + j * GROUP
                    src = pl.ds(pl.multiple_of((2 * z + c) * unit + j * GROUP, GROUP), GROUP)
                    pieces[at // tall][z, at % tall:at % tall + GROUP] = g_ref[i, src]
            pieces[3][z, tall - 2 * GROUP:tall - GROUP] = high
            pieces[3][z, tall - GROUP:tall] = low
            return carry

        lax.fori_loop(0, shares // 2, one, 0)

    per = 4 // len(sends)
    by_core(own_core(), deal, [keep.at[p] for p in range(4)], [sends[p // per].at[p % per] for p in range(4)])


def inputs_kernel(groups, hit_ref, out_page, dr_ref, wq_ref, wk_ref, wv_ref, *refs):
    parts = [refs[3 * g:3 * g + 3] for g in range(groups)]
    din_ref, *outs = refs[3 * groups:]
    total = dr_ref[...]
    for i, w in enumerate((wq_ref, wk_ref, wv_ref)):
        at = 0
        for part in parts:
            wide = part[i].shape[1]
            total = total + nt(part[i][...], w[:, at:at + wide])
            at += wide
    din_ref[...] = jnp.where(hit_ref[:, 0:1] > 0.5, 0.0, total).astype(BF)
    span = outs[0].shape[1]
    for i, out in enumerate(outs):
        rows = block(own_blk() ^ (i + 1), span)
        out[0] = out_page[rows, :]
        out[1] = din_ref[rows, :]


def added(a, b):
    return (a.astype(F32) + b.astype(F32)).astype(BF)


def halves_kernel(bit, came_parts, own, came, send, keep):
    mine = bit()

    def one(r, carry):
        send[r] = added(own[1 - mine, r], came[1 - mine, r])
        keep[r] = added(own[mine, r], came[mine, r])
        return carry

    lax.fori_loop(0, own.shape[1], one, 0)


def joined_halves_kernel(bit, axis, cuts, *refs):
    owns, rest = refs[:len(cuts)], refs[len(cuts):]
    cames = []
    for n in cuts:
        cames.append(rest[:n])
        rest = rest[n:]
    send, keep = rest
    mine = bit()

    def half_of(half, out, came_half):
        def one(r, carry):
            at = 0
            for own, came in zip(owns, cames):
                size = own.shape[1 + axis]
                cut = slice(at, at + size)
                index = (r, cut) if axis == 1 else (r, slice(None), cut)
                out[index] = added(own[half, r], came[0][half, r] if len(came) == 1 else came[came_half][0, r])
                at += size
            return carry

        lax.fori_loop(0, out.shape[0], one, 0)

    if max(cuts) == 1:
        half_of(1 - mine, send, None)
        half_of(mine, keep, None)
        return
    for half in range(2):

        @pl.when(mine == half)
        def _():
            half_of(1 - half, send, 1 - half)
            half_of(half, keep, half)


def z_halves_kernel(came_parts, own, came, send, keep):
    pieces, depth = own.shape[:2]
    rest = depth // 2
    low, high = z_bits()
    core = own_core()
    if depth == 4:
        mine = jnp.where(core == 0, low, high)
        by_half, by_rest = jnp.where(core == 0, 1, 2), jnp.where(core == 0, 2, 1)
    else:
        mine = jnp.where(core == 0, high, low)
        by_half, by_rest = 1, 0

    def one(j, carry):
        p, r = lax.div(j, rest), lax.rem(j, rest)
        theirs, ours = (1 - mine) * by_half + r * by_rest, mine * by_half + r * by_rest
        send[j] = added(own[p, theirs], came[p, theirs])
        keep[j] = added(own[p, ours], came[p, ours])
        return carry

    lax.fori_loop(0, pieces * rest, one, 0)


def sum_kernel(own, came, out):
    out[...] = added(own[...].reshape(out.shape), came[...].reshape(out.shape))


def pair_kernel(own, came, out):
    lo = second_bit()
    out[lo] = own[...]
    out[1 - lo] = came[...]


def last_kernel(place, own, came, *refs):
    mine = first_bit()
    for half in range(2):
        @pl.when(mine == half)
        def _():
            for j in range(2):
                place(2 * half + j, own, j, *refs)
                place(2 * (1 - half) + j, came, j, *refs)


def place_up(p, ref, j, up, out, tail):
    unit, width = out.shape
    end = unit + tail.shape[1]
    up[:, p * width:(p + 1) * width] = ref[j, 0:unit].astype(F32)
    tail[p] = ref[j, unit:end].astype(F32)
    for g, (piece, at) in enumerate(OUT_GROUPS):
        if piece == p:
            out[g * GROUP:(g + 1) * GROUP] = ref[j, end + at * GROUP:end + (at + 1) * GROUP].astype(F32)


def place_down(p, ref, j, tail, down):
    unit = down.shape[0] // 4
    down[p * unit:p * unit + DOWN_Z] = ref[j].astype(F32)
    down[p * unit + DOWN_Z:(p + 1) * unit] = tail[p]


def place_rows(p, ref, j, query, key, value, vectors):
    unit = query.shape[0]
    tall = ref.shape[1]
    for g in range(tall // GROUP):
        at = p * tall + g * GROUP
        part = ref[j, g * GROUP:(g + 1) * GROUP].astype(F32)
        if at < 3 * unit:
            (query, key, value)[at // unit][at % unit:at % unit + GROUP] = part
        elif at == 3 * unit:
            vectors[...] = part + ref[j, (g + 1) * GROUP:(g + 2) * GROUP].astype(F32)


def page_rows_kernel(out_page, d_page, *refs):
    *came, out_rows, d_rows = refs
    span = out_rows.shape[1]
    me = own_blk()
    for which, (page, out) in enumerate(((out_page, out_rows), (d_page, d_rows))):
        out[me] = page[block(me, span), :]
        for i, part in enumerate(came):
            out[me ^ (i + 1)] = part[which]


VM = pl.BlockSpec(memory_space=pltpu.VMEM)
SM = pl.BlockSpec(memory_space=pltpu.SMEM)
HB = pl.BlockSpec(memory_space=pl.ANY)


def call(kernel, args, places, outs, scratch, limit):
    return pl.pallas_call(
        kernel,
        out_shape=[jax.ShapeDtypeStruct(s, d) for s, d in outs],
        in_specs=places,
        out_specs=[VM] * len(outs),
        scratch_shapes=[s if not isinstance(s, tuple) else pltpu.VMEM(*s) for s in scratch],
        compiler_params=pltpu.CompilerParams(vmem_limit_bytes=limit * MIB),
        cost_estimate=pl.CostEstimate(flops=1024, bytes_accessed=1024, transcendentals=0),
    )(*args)


def fetch(ids, counts, spots, table, rows):
    width = table.shape[1]
    slots = ids.shape[1]
    return call(
        fetch_kernel, (ids, counts, spots, table), [SM, SM, VM, HB], [((rows, width), BF), ((rows, 128), F32)],
        [((slots * GROUP, width), BF), ((slots * GROUP, width), F32), ((slots, width), F32), pltpu.SemaphoreType.DMA], LIMITS[0],
    )


LIMITS = [44, 16, 20, 8, 16, 10, 4]


def attend(lengths, inputs, pieces, placed, hit, biases, wq, wk, wv, wo):
    span, width = pieces[0].shape
    rows = 4 * span
    args = (lengths, inputs, *pieces, placed, hit, *biases, wq, wk, wv, wo)
    outs = [((width, rows), BF)] + [((rows, width), BF)] * 3 + [((width, rows), BF), ((HEADS, 1, rows), F32), ((HEADS, 1, rows), F32), ((rows, width), F32), ((rows, 128), F32)]
    return call(attend_kernel, args, [SM] + [VM] * 13, outs, [((rows, width), BF)] * 2, LIMITS[1])


def feed(n, cotangent, pieces, vecs, wu, wd):
    rows, width = n.shape
    ff = wu.shape[1]
    args = (n, cotangent, *pieces, *vecs, wu, wd)
    unit = width // PARTS
    groups = [((4, PARTS // 2, tall, width), BF) for tall in (DOWN_Z, 2 * unit - DOWN_Z)]
    outs = [((rows, width), BF)] + [groups[0]] * 2 + [groups[1]] * 2 + [((rows, ff), BF), ((rows, width), F32), ((16, width), F32)]
    scratch = [((rows, ff), BF)] + [((rows, width), BF)] * 2 + [((width, rows), BF), ((rows, width), BF)] + [((width, width), BF)] * 2
    return call(ff_kernel, args, [VM] * len(args), outs, scratch, LIMITS[2])


def mixed_back(n, rstd, att, dh, dfirst, vsum, gain, wu):
    rows, width = n.shape
    args = (n, rstd, att, dh, dfirst, vsum, gain, wu)
    group = ((4, PARTS // 2, 2 * GROUP, width), BF)
    outs = [group] * 2 + [((rows, width), F32), ((rows, width), BF), (vsum.shape, F32)]
    return call(mixed_kernel, args, [VM] * len(args), outs, [((width, width), BF)], LIMITS[5])


def attended_back(att, sums, dd, wo):
    rows, width = dd.shape
    outs = [((width, rows), BF), ((HEADS, 1, rows), F32)]
    return call(attended_kernel, (att, sums, dd, wo), [VM] * 4, outs, [((width, rows), F32)], LIMITS[5])


def heads(first, count, cuts, lengths, x_t, vsum, q, k, v, dst, delta, tops):
    width, rows = x_t.shape
    wide = count * HD
    tall = (3 * (width // PARTS) + 2 * GROUP) // 4
    args = (lengths, x_t, vsum, q, k, v, dst, delta, tops)
    outs = [((rows, wide), BF)] * 3 + [((4, PARTS // 2, tall, wide), BF)] + [((4 // cuts, PARTS // 2, tall, wide), BF)] * cuts
    return call(functools.partial(heads_kernel, first // 2), args, [SM] + [VM] * 8, outs, [((3, width, wide), BF)], LIMITS[3])


def inputs_grad(span, hit, out_page, dr, wq, wk, wv, parts):
    rows, width = dr.shape
    args = (hit, out_page, dr, wq, wk, wv) + tuple(t for part in parts for t in part)
    outs = [(dr.shape, BF)] + [((2, span, width), BF)] * (rows // span - 1)
    return call(functools.partial(inputs_kernel, len(parts)), args, [VM] * len(args), outs, [], LIMITS[5])


def pick(array, index, axis=0):
    return lax.dynamic_index_in_dim(array, index, axis, keepdims=False)


def swap(array, bit):
    return lax.ppermute(array, "blk", [(i, i ^ bit) for i in range(lax.axis_size("blk"))])


def swap_first(array, first):
    blks, shares = lax.axis_size("blk"), lax.axis_size("batch")
    perm = []
    for b in range(blks):
        for s in range(shares):
            bit = 1 if (s % 2 == 0) == first else 2
            perm.append((b * shares + s, (b ^ bit) * shares + s))
    return lax.ppermute(array, ("blk", "batch"), perm)


def swap_batch(array, bit):
    return lax.ppermute(array, "batch", [(i, i ^ bit) for i in range(lax.axis_size("batch"))])


def swap_z(array, first):
    shares = lax.axis_size("batch")
    return lax.ppermute(array, "batch", [(i, i ^ (2 if (i % 2 == 0) == first else 4)) for i in range(shares)])


class Cell:
    def __init__(self, *values):
        self.values = values


class Order:
    def __init__(self):
        self.last = Cell()

    def enter(self, *arrays):
        tied = lax.optimization_barrier((*arrays, *self.last.values))
        self.last.values = tied[len(arrays):]
        return tied[:len(arrays)]

    def leave(self, cell):
        self.last = cell


class Chain:
    def __init__(self, order, cell, send):
        self.order = order
        self.own, self.came = cell, tuple(swap_batch(s, 1) for s in send)

    @classmethod
    def joined(cls, order, axis, cells, cames):
        chain = cls(order, None, ())
        groups = len(cells)
        tied = order.enter(*(c.values[0] for c in cells), *(t for came in cames for t in came))
        shape = tied[0].shape
        flat = [shape[0] * shape[1] // 2, shape[2], shape[3]]
        flat[axis] = sum(t.shape[axis + 1] for t in tied[:groups])
        args = [t.reshape((-1, flat[0]) + t.shape[2:]) for t in tied]
        kernel = functools.partial(joined_halves_kernel, first_bit, axis, [len(came) for came in cames])
        send, keep = call(kernel, args, [VM] * len(args), [(tuple(flat), BF)] * 2, [], LIMITS[6])
        chain.came = [swap_first(send, True)]
        chain.own = Cell(keep.reshape((shape[0] // 2, shape[1], flat[1], flat[2])))
        order.leave(chain.own)
        return chain

    def halve(self, axis, bit, move, cuts):
        own, *came = self.order.enter(self.own.values[0], *self.came)
        shape = own.shape
        after = shape[:axis] + (shape[axis] // 2,) + shape[axis + 1:]
        flat = (after[0] * after[1],) + shape[2:]
        if axis == 0:
            own = own.reshape((2,) + flat)
            kernel = functools.partial(halves_kernel, bit, len(came))
        else:
            kernel = functools.partial(z_halves_kernel, len(came))
        came = [came[0].reshape(own.shape)]
        outs = [((flat[0] // cuts,) + shape[2:], BF)] * cuts + [(flat, BF)]
        *sends, keep = call(kernel, (own, *came), [VM] * (1 + len(came)), outs, [], LIMITS[6])
        self.came = [move(send) for send in sends]
        self.own = Cell(keep.reshape(after))
        self.order.leave(self.own)

    def first(self, cuts=1):
        self.halve(0, first_bit, lambda v: swap_first(v, True), cuts)

    def second(self, cuts=1):
        self.halve(0, second_bit, lambda v: swap_first(v, False), cuts)

    def z_first(self, cuts=1):
        self.halve(1, None, lambda v: swap_z(v, True), cuts)

    def z_second(self, cuts=1):
        self.halve(1, None, lambda v: swap_z(v, False), cuts)

    def gather_second(self):
        own, came = self.order.enter(self.own.values[0], *self.came)
        out, = call(sum_kernel, (own, came), [VM] * 2, [(own.shape[2:], BF)], [], LIMITS[6])
        self.own = Cell(out)
        self.came = (swap_first(out, False),)
        self.order.leave(self.own)

    def gather_first(self):
        own, came = self.order.enter(self.own.values[0], *self.came)
        out, = call(pair_kernel, (own, came), [VM] * 2, [((2,) + own.shape, BF)], [], LIMITS[6])
        self.own = Cell(out)
        self.came = (swap_first(out, True),)
        self.order.leave(self.own)

    def result(self, place, shapes, *others):
        own, came = self.order.enter(self.own.values[0], *self.came)
        args = (own, came, *others)
        return call(functools.partial(last_kernel, place), args, [VM] * len(args), [(s, F32) for s in shapes], [], LIMITS[6])


def own_vectors(vec, share, shares):
    width = vec.shape[-1]
    n = width // shares
    cut = lax.dynamic_slice_in_dim(vec, share * n, n, 1)
    flat = vec[B_UP:B_UP + 4].reshape(-1)
    return [cut[i] for i in range(B_UP)] + [lax.dynamic_slice_in_dim(flat, share * 4 * n, 4 * n, 0)]


def body(
    inputs, lengths, positions, counts, token_ids, table,
    w_query, b_query, w_key, w_value, b_value, w_out, b_out, gain_one, shift_one,
    w_up, b_up, w_down, b_down, gain_two, shift_two, cotangent,
):
    blk, share = lax.axis_index("blk"), lax.axis_index("batch")
    shares = lax.axis_size("batch")
    core = share % 2
    pages, span, width = inputs.shape
    ff = w_up.shape[1]
    unit = width // PARTS
    rows_in = [swap(pick(inputs, blk ^ i), i) for i in range(1, pages)]
    placed, hit = fetch(token_ids, counts, positions, table, pages * span)
    back, hit = lax.optimization_barrier((cotangent, hit))
    back_in = [swap(pick(back, blk ^ i), i) for i in range(1, pages)]
    x_t, q, k, v, att, tops, sums, n1, rstd = attend(
        lengths, inputs, rows_in, placed, hit, (b_query, b_value, b_out), w_query, w_key, w_value, w_out
    )
    out_page, d_keep, d_send, u_keep, u_send, dh, dfirst, vsum = feed(
        n1, cotangent, back_in, (b_up, b_down, gain_one, shift_one, gain_two, shift_two), w_up, w_down
    )

    def to_mixed(n1, vsum):
        return mixed_back(n1, rstd, att, dh, dfirst, vsum, gain_one, w_up)

    order = Order()

    def attention_back(first, count, vsum, dst, delta, cuts=1):
        delta, = order.enter(delta)
        dq, dk, dv, keep, *send = heads(first, count, cuts, lengths, x_t, vsum, q, k, v, dst, delta, tops)
        parts = [dq, dk, dv]
        grads = Cell(keep)
        order.leave(grads)
        return parts, grads, send

    def page_rows(out_page, d_page, came):
        return call(page_rows_kernel, (out_page, d_page, *came), [VM] * (pages + 1), [(inputs.shape, BF)] * 2, [], LIMITS[6])

    if shares == PARTS and lax.axis_size("blk") == 4:
        d = Chain(order, Cell(d_keep), [d_send])
        u_came = swap_batch(u_send, 1)
        n_now, = order.enter(n1)
        o_keep, o_send, d_r1, d_branch, vsum = to_mixed(n_now, vsum)
        o_cell = Cell(o_keep)
        order.leave(o_cell)
        o_came = swap_batch(o_send, 1)
        att_now, = order.enter(att)
        sums_cell = Cell(*attended_back(att_now, sums, d_branch, w_out))
        order.leave(sums_cell)
        d.z_first()
        u = Chain.joined(order, 1, [Cell(u_keep), o_cell], [[u_came], [o_came]])
        groups = [attention_back(0, 8, vsum, *sums_cell.values, cuts=2)]
        groups.append(attention_back(8, 4, vsum, *sums_cell.values))
        parts = [g[0] for g in groups]
        a = Chain.joined(order, 2, [g[1] for g in groups], [[swap_batch(t, 1) for t in g[2]] for g in groups])
        d.z_second()
        u.second()
        hit_now, = order.enter(hit)
        d_page, *page_parts = inputs_grad(span, hit_now, out_page, d_r1, w_query, w_key, w_value, parts)
        d_cell = Cell(d_page)
        order.leave(d_cell)
        page_parts = [swap(part, i + 1) for i, part in enumerate(page_parts)]
        a.second()
        u.z_first()
        d.first()
        a.z_first()
        u.z_second()
        d.second()
        a.z_second()
        u.gather_second()
        d.gather_second()
        d_page, *came = order.enter(*d_cell.values, *page_parts)
        rows_cell = Cell(*page_rows(out_page, d_page, came))
        order.leave(rows_cell)
        a.gather_second()
        a.gather_first()
        u.gather_first()
        d.gather_first()
        grad_up, grad_out, tail = u.result(place_up, [(unit, ff), (unit, width), (4, unit - DOWN_Z, width)])
        grad_down, = d.result(place_down, [(ff // PARTS, width)], tail)
        grad_query, grad_key, grad_value, vectors = a.result(place_rows, [(unit, width)] * 3 + [(GROUP, width)])
        outputs, d_inputs = rows_cell.values
    else:
        o_keep, o_send, d_r1, d_branch, vsum = to_mixed(n1, vsum)
        attended = attended_back(att, sums, d_branch, w_out)
        groups = [attention_back(i, 4, vsum, *attended) for i in range(0, HEADS, 4)]
        a_keep = jnp.concatenate([g[1].values[0] for g in groups], axis=-1)
        a_send = jnp.concatenate([g[2][0] for g in groups], axis=-1)
        d_page, *page_parts = inputs_grad(span, hit, out_page, d_r1, w_query, w_key, w_value, [g[0] for g in groups])
        came = [swap(part, i + 1) for i, part in enumerate(page_parts)]
        outputs, d_inputs = page_rows(out_page, d_page, came)

        def parity(keep, send):
            packed = jnp.where(core == 0, jnp.stack([keep, send]), jnp.stack([send, keep]))
            return packed.transpose(1, 2, 0, 3, 4)

        def over(grad):
            part = lax.psum_scatter(grad.astype(F32), "batch", scatter_dimension=0, tiled=True)
            return lax.psum(part.astype(BF), "blk").astype(F32)

        out = parity(o_keep, o_send)
        out = jnp.concatenate([out[p][..., at * GROUP:(at + 1) * GROUP, :] for p, at in OUT_GROUPS], axis=-2)
        out = out.reshape(width, width)
        up = parity(u_keep, u_send)
        down = jnp.concatenate([parity(d_keep, d_send), up[..., unit:, :]], axis=-2)
        down = down.transpose(1, 2, 0, 3, 4).reshape(ff, width)
        up = up[..., :unit, :].transpose(1, 2, 3, 0, 4).reshape(width, ff)
        rows = parity(a_keep, a_send).transpose(1, 2, 0, 3, 4).reshape(PARTS, -1, width)
        mats = [rows[:, i * unit:(i + 1) * unit].reshape(width, width) for i in range(3)]
        vectors = rows[0, 3 * unit:3 * unit + GROUP].astype(F32) + rows[0, 3 * unit + GROUP:].astype(F32)
        vectors = lax.psum(vectors, ("blk", "batch"))
        grad_down, grad_up, grad_out = over(down), over(up), over(out)
        grad_query, grad_key, grad_value = (over(m) for m in mats)
    r = own_vectors(vectors, share, shares)
    return (
        outputs, d_inputs, grad_query, r[B_QUERY], grad_key, grad_value, r[B_VALUE], grad_out, r[B_OUT],
        r[GAIN_ONE], r[SHIFT_ONE], grad_up, r[B_UP], grad_down, r[B_DOWN], r[GAIN_TWO], r[SHIFT_TWO],
    )


def solution(mesh):
    split, whole = P("batch", "blk", None), P()
    rows, vec = P("batch", None), P("batch")
    in_specs = (split, vec, rows, vec, rows) + (whole,) * 16 + (split,)
    out_specs = (split, split, rows, vec, rows, rows, vec, rows, vec, vec, vec, rows, vec, rows, vec, vec, vec)
    return jax.shard_map(body, mesh=mesh, in_specs=in_specs, out_specs=out_specs, check_vma=False)
```

```python
import functools

import jax
import jax.numpy as jnp
from jax import lax
from jax.experimental import pallas as pl
from jax.experimental.pallas import tpu as pltpu
from jax.sharding import PartitionSpec as P

HEADS = 12
HD = 64
SCALE = 0.125
NEGATIVE = -1e30
EPSILON = 1e-12
BF = jnp.bfloat16
F32 = jnp.float32
MIB = 1024 * 1024
GROUP = 16
PARTS = 8
DOWN_Z = 80
B_QUERY, B_VALUE, B_OUT, B_DOWN, GAIN_ONE, SHIFT_ONE, GAIN_TWO, SHIFT_TWO, B_UP = range(9)


def nn(a, b):
    return lax.dot_general(a, b, (((1,), (0,)), ((), ())), preferred_element_type=F32)


def nt(a, b):
    return lax.dot_general(a, b, (((1,), (1,)), ((), ())), preferred_element_type=F32)


def tn(a, b):
    return lax.dot_general(a, b, (((0,), (0,)), ((), ())), preferred_element_type=F32)


def head_lanes(shape, which):
    lane = lax.broadcasted_iota(jnp.int32, shape, 1)
    return (lane >= HD) if which else (lane < HD)


def norm_parts(v):
    width = v.shape[-1]
    centre = jnp.sum(v, axis=-1, keepdims=True) * (1.0 / width)
    centred = v - centre
    spread = jnp.sum(centred * centred, axis=-1, keepdims=True) * (1.0 / width)
    rstd = lax.rsqrt(spread + EPSILON)
    return centred * rstd, rstd


def norm_back(c2, n, rstd):
    width = c2.shape[-1]
    a = jnp.sum(c2, axis=-1, keepdims=True) * (1.0 / width)
    b = jnp.sum(c2 * n, axis=-1, keepdims=True) * (1.0 / width)
    return (c2 - a - n * b) * rstd


def colsum(v):
    return jnp.sum(v, axis=0, keepdims=True)


def wide_row(ref):
    return ref[...].astype(F32).reshape(1, ref.shape[0])


def block(i, size):
    return pl.ds(pl.multiple_of(i * size, size), size)


def own_blk():
    return lax.axis_index("blk")


def own_core():
    return lax.rem(lax.axis_index("batch"), 2)


def first_bit():
    return jnp.where(own_core() == 0, lax.rem(own_blk(), 2), lax.div(own_blk(), 2))


def second_bit():
    return jnp.where(own_core() == 0, lax.div(own_blk(), 2), lax.rem(own_blk(), 2))


def z_bits():
    z = lax.div(lax.axis_index("batch"), 2)
    return lax.rem(z, 2), lax.div(z, 2)


def fetch_kernel(ids_ref, counts_ref, spots_ref, table_ref, placed_ref, hit_ref, rows_ref, wide_ref, sel_ref, sem):
    slots = ids_ref.shape[1]
    me = own_blk()

    def start(j, carry):
        group = pl.multiple_of((ids_ref[me, j] // GROUP) * GROUP, GROUP)
        pltpu.make_async_copy(table_ref.at[pl.ds(group, GROUP), :], rows_ref.at[block(j, GROUP), :], sem).start()
        return carry

    lax.fori_loop(0, slots, start, 0, unroll=8)
    total = placed_ref.shape[0]
    spot = lax.broadcasted_iota(jnp.int32, (total, slots), 0)
    slot = lax.broadcasted_iota(jnp.int32, (total, slots), 1)
    hits = ((spots_ref[pl.ds(me, 1), :] == spot) & (slot < counts_ref[me])).astype(F32)
    hit_ref[...] = jnp.broadcast_to(jnp.sum(hits, axis=1, keepdims=True), hit_ref.shape)
    pltpu.make_async_copy(table_ref.at[pl.ds(0, slots * GROUP), :], rows_ref, sem).wait()
    wide_ref[...] = rows_ref[...].astype(F32)

    def select(j, carry):
        at = j * GROUP + lax.rem(ids_ref[me, j], GROUP)
        sel_ref[pl.ds(j, 1), :] = wide_ref[pl.ds(at, 1), :]
        return carry

    lax.fori_loop(0, slots, select, 0, unroll=8)
    placed_ref[...] = nn(hits.astype(BF), sel_ref[...].astype(BF)).astype(BF)


def attend_kernel(
    lengths_ref, inputs_ref, p1_ref, p2_ref, p3_ref, placed_ref, hit_ref, bq_ref, bv_ref, bo_ref,
    wq_ref, wk_ref, wv_ref, wo_ref,
    x_t_ref, q_ref, k_ref, v_ref, att_ref, max_ref, sum_ref, n_ref, rstd_ref,
    x_ref, att_rows,
):
    me = own_blk()
    length = lengths_ref[me]
    rows, width = x_ref.shape
    span = p1_ref.shape[0]
    for step, piece in enumerate((inputs_ref[me], p1_ref[...], p2_ref[...], p3_ref[...])):
        at = block(me ^ step, span)
        x_ref[at, :] = jnp.where(hit_ref[at, 0:1] > 0.5, placed_ref[at, :], piece)
    x_t_ref[...] = x_ref[...].T
    q = (nn(x_ref[...], wq_ref[...]) + wide_row(bq_ref)).astype(BF)
    q_ref[...] = (q.astype(F32) * SCALE).astype(BF)
    k_ref[...] = nn(x_ref[...], wk_ref[...]).astype(BF)
    v_ref[...] = (nn(x_ref[...], wv_ref[...]) + wide_row(bv_ref)).astype(BF)
    dead = jnp.where(lax.broadcasted_iota(jnp.int32, (rows, 1), 0) < length, 0.0, NEGATIVE)

    def pair(i, carry):
        lanes = block(i, 2 * HD)
        q2, k2 = q_ref[:, lanes], k_ref[:, lanes]
        v2t = v_ref[:, lanes].T
        for h in range(2):
            qm = jnp.where(head_lanes(q2.shape, h), q2, jnp.zeros_like(q2))
            s = nt(k2, qm) + dead
            top = jnp.max(s, axis=0, keepdims=True)
            p = jnp.exp(s - top)
            total = jnp.sum(p, axis=0, keepdims=True)
            o = nn(v2t[h * HD:(h + 1) * HD], p.astype(BF)) / total
            max_ref[2 * i + h] = top
            sum_ref[2 * i + h] = total
            att_ref[block(2 * i + h, HD), :] = o.astype(BF)
        att_rows[:, lanes] = att_ref[lanes, :].T
        return carry

    lax.fori_loop(0, HEADS // 2, pair, 0, unroll=True)
    branch = nn(att_rows[...], wo_ref[...]) + wide_row(bo_ref)
    n, rstd = norm_parts(x_ref[...].astype(F32) + branch)
    n_ref[...] = n
    rstd_ref[...] = jnp.broadcast_to(rstd, rstd_ref.shape)


def gelu_both(v):
    e = jnp.exp2(v * v * -0.7213475204444817)
    t = pl.reciprocal(1.0 + (0.3275911 * 0.7071067811865476) * jnp.abs(v))
    poly = t * (0.5 * 0.254829592 + t * (0.5 * -0.284496736 + t * (0.5 * 1.421413741 + t * (0.5 * -1.453152027 + t * (0.5 * 1.061405429)))))
    tail = poly * e
    phi = jnp.where(v >= 0, 1.0 - tail, tail)
    return v * phi, phi + v * (e * 0.3989422804014327)


def by_core(core, deal, keep, send):
    for c in range(2):

        @pl.when(core == c)
        def _():
            deal(c, *keep)
            deal(1 - c, *send)


OUT_GROUPS = [(0, 0), (0, 1), (1, 0), (1, 1), (2, 0), (3, 0)]


def ff_kernel(
    n_ref, cot_ref, c1_ref, c2_ref, c3_ref,
    bu_ref, bd_ref, g1_ref, s1_ref, g2_ref, s2_ref, wu_ref, wd_ref,
    out_ref, dkeep, dsend, ukeep, usend, dh_ref, dfirst_ref, vsum_ref,
    act, cot, nlow, nlow_t, dd, g_down, g_up,
):
    width = n_ref.shape[1]
    ff = wu_ref.shape[1]
    parts = ff // width
    shares = 2 * dkeep.shape[1]
    unit = width // shares
    span = c1_ref.shape[0]
    me, core = own_blk(), own_core()
    for hop, piece in enumerate((cot_ref[me], c1_ref[...], c2_ref[...], c3_ref[...])):
        cot[block(me ^ hop, span), :] = piece
    normed = n_ref[...] * wide_row(g1_ref) + wide_row(s1_ref)
    nlow[...] = normed.astype(BF)
    nlow_t[...] = nlow[...].T
    for i in range(parts):
        lanes = slice(i * width, (i + 1) * width)
        a, b = gelu_both(nn(nlow[...], wu_ref[:, lanes]) + wide_row(bu_ref)[:, lanes])
        act[:, lanes] = a.astype(BF)
        dh_ref[:, lanes] = b.astype(BF)
    normed = n_ref[...] * wide_row(g1_ref) + wide_row(s1_ref)
    resid = normed + nn(act[...], wd_ref[...]) + wide_row(bd_ref)
    n2, rstd2 = norm_parts(resid)
    out_ref[...] = (n2 * wide_row(g2_ref) + wide_row(s2_ref)).astype(BF)
    c = cot[...].astype(F32)
    vsum_ref[...] = jnp.zeros_like(vsum_ref)
    vsum_ref[GAIN_TWO:GAIN_TWO + 1] = colsum(c * n2)
    vsum_ref[SHIFT_TWO:SHIFT_TWO + 1] = colsum(c)
    d_r2 = norm_back(c * wide_row(g2_ref), n2, rstd2)
    dfirst_ref[...] = d_r2
    dd[...] = d_r2.astype(BF)
    vsum_ref[B_DOWN:B_DOWN + 1] = colsum(dd[...].astype(F32))

    def back(i, carry):
        lanes = block(i, width)
        g_down[...] = tn(act[:, lanes], dd[...]).astype(BF)
        dhc = (nt(dd[...], wd_ref[lanes, :]) * dh_ref[:, lanes].astype(F32)).astype(BF)
        dh_ref[:, lanes] = dhc
        vsum_ref[pl.ds(B_UP + i, 1)] = colsum(dhc.astype(F32))
        g_up[...] = nn(nlow_t[...], dhc).astype(BF)

        def deal(c, down, up):
            for p in range(4):
                at = (c * 4 + p) * unit
                down[p, i] = g_down[at:at + DOWN_Z]
                up[p, i, unit:] = g_down[at + DOWN_Z:at + unit]
            for z in range(shares // 2):
                at = (2 * z + c) * unit
                up[i, z, 0:unit] = g_up[at:at + unit]

        by_core(core, deal, (dkeep, ukeep), (dsend, usend))
        return carry

    lax.fori_loop(0, parts, back, 0)


def mixed_kernel(
    n_ref, rstd_ref, att_ref, dh_ref, dfirst_ref, vin_ref, g1_ref, wu_ref,
    okeep, osend, dr_ref, dd, vsum_ref,
    g_out,
):
    width = n_ref.shape[1]
    shares = 2 * okeep.shape[1]
    unit = width // shares

    def first(i, carry):
        lanes = block(i, width // 3)
        dr_ref[:, lanes] = dfirst_ref[:, lanes] + nt(dh_ref[...], wu_ref[lanes, :])
        return carry

    lax.fori_loop(0, 3, first, 0)
    d_f = dr_ref[...]
    n1 = n_ref[...]
    vsum_ref[...] = vin_ref[...]
    vsum_ref[GAIN_ONE:GAIN_ONE + 1] = colsum(d_f * n1)
    vsum_ref[SHIFT_ONE:SHIFT_ONE + 1] = colsum(d_f)
    d_r1 = norm_back(d_f * wide_row(g1_ref), n1, rstd_ref[:, 0:1])
    dr_ref[...] = d_r1
    db = d_r1.astype(BF)
    dd[...] = db
    vsum_ref[B_OUT:B_OUT + 1] = colsum(db.astype(F32))
    g_out[...] = nn(att_ref[...], dd[...]).astype(BF)

    def deal(c, out):
        for z in range(shares // 2):
            for g in range(unit // GROUP):
                p, at = OUT_GROUPS[g]
                src = (2 * z + c) * unit + g * GROUP
                out[p, z, at * GROUP:(at + 1) * GROUP] = g_out[src:src + GROUP]
            for p in (2, 3):
                out[p, z, GROUP:2 * GROUP] = jnp.zeros((GROUP, width), BF)

    by_core(own_core(), deal, (okeep,), (osend,))


def attended_kernel(att_ref, sum_ref, dd_ref, wo_ref, dst_ref, delta_ref, dm_ref):
    dm_ref[...] = nt(wo_ref[...], dd_ref[...])
    for i in range(HEADS):
        at = slice(i * HD, (i + 1) * HD)
        inv = 1.0 / sum_ref[i]
        delta_ref[i] = colsum(dm_ref[at, :] * att_ref[at, :].astype(F32)) * inv
        dst_ref[at, :] = (dm_ref[at, :] * inv).astype(BF)


def heads_kernel(first, lengths_ref, x_t_ref, vin_ref, q_ref, k_ref, v_ref, dst_ref, delta_ref, max_ref, dq, dk, dv, keep, *sends):
    *sends, g_ref = sends
    length = lengths_ref[own_blk()]
    rows = q_ref.shape[0]
    dead = jnp.where(lax.broadcasted_iota(jnp.int32, (rows, 1), 0) < length, 0.0, NEGATIVE)

    def pair(i, carry):
        lanes, own = block(first + i, 2 * HD), block(i, 2 * HD)
        q2, k2, v2 = q_ref[:, lanes], k_ref[:, lanes], v_ref[:, lanes]
        dst = dst_ref[lanes, :]
        ds2 = dst.T
        k2t = k2.T
        dv2 = jnp.zeros((rows, 2 * HD), F32)
        dk2 = jnp.zeros((rows, 2 * HD), F32)
        dqs = []
        for h in range(2):
            live = head_lanes(q2.shape, h)
            zero = jnp.zeros_like(q2)
            qm = jnp.where(live, q2, zero)
            s = nt(k2, qm) + dead
            head = 2 * (first + i) + h
            p = jnp.exp(s - max_ref[head])
            dp = nn(jnp.where(live, v2, zero), dst)
            dsc = (p * (dp - delta_ref[head])).astype(BF)
            dv2 = dv2 + nn(p.astype(BF), jnp.where(live, ds2, zero))
            dk2 = dk2 + nn(dsc, qm)
            dqs.append(nn(k2t[h * HD:(h + 1) * HD], dsc))
        dq[:, own] = (jnp.concatenate(dqs, axis=0) * SCALE).astype(BF).T
        dk[:, own] = dk2.astype(BF)
        dv[:, own] = dv2.astype(BF)
        return carry

    lax.fori_loop(0, dq.shape[1] // (2 * HD), pair, 0)
    for i, part in enumerate((dq, dk, dv)):
        g_ref[i] = nn(x_t_ref[...], part[...]).astype(BF)
    vsum = vin_ref[:, first * 2 * HD:first * 2 * HD + dq.shape[1]]
    row = lax.broadcasted_iota(jnp.int32, vsum.shape, 0)
    vsum = vsum + jnp.where(row == B_QUERY, colsum(dq[...].astype(F32)), 0.0) + jnp.where(row == B_VALUE, colsum(dv[...].astype(F32)), 0.0)
    high = vsum.astype(BF)
    low = (vsum - high.astype(F32)).astype(BF)
    shares = 2 * keep.shape[1]
    unit = x_t_ref.shape[0] // shares
    tall = keep.shape[2]

    def deal(c, *pieces):
        def one(z, carry):
            for i in range(3):
                for j in range(unit // GROUP):
                    at = i * unit + j * GROUP
                    src = pl.ds(pl.multiple_of((2 * z + c) * unit + j * GROUP, GROUP), GROUP)
                    pieces[at // tall][z, at % tall:at % tall + GROUP] = g_ref[i, src]
            pieces[3][z, tall - 2 * GROUP:tall - GROUP] = high
            pieces[3][z, tall - GROUP:tall] = low
            return carry

        lax.fori_loop(0, shares // 2, one, 0)

    per = 4 // len(sends)
    by_core(own_core(), deal, [keep.at[p] for p in range(4)], [sends[p // per].at[p % per] for p in range(4)])


def inputs_kernel(groups, hit_ref, out_page, dr_ref, wq_ref, wk_ref, wv_ref, *refs):
    parts = [refs[3 * g:3 * g + 3] for g in range(groups)]
    din_ref, *outs = refs[3 * groups:]
    total = dr_ref[...]
    for i, w in enumerate((wq_ref, wk_ref, wv_ref)):
        at = 0
        for part in parts:
            wide = part[i].shape[1]
            total = total + nt(part[i][...], w[:, at:at + wide])
            at += wide
    din_ref[...] = jnp.where(hit_ref[:, 0:1] > 0.5, 0.0, total).astype(BF)
    span = outs[0].shape[1]
    for i, out in enumerate(outs):
        rows = block(own_blk() ^ (i + 1), span)
        out[0] = out_page[rows, :]
        out[1] = din_ref[rows, :]


def added(a, b):
    return (a.astype(F32) + b.astype(F32)).astype(BF)


def halves_kernel(bit, came_parts, own, came, send, keep):
    mine = bit()

    def one(r, carry):
        send[r] = added(own[1 - mine, r], came[1 - mine, r])
        keep[r] = added(own[mine, r], came[mine, r])
        return carry

    lax.fori_loop(0, own.shape[1], one, 0)


def joined_halves_kernel(bit, axis, cuts, *refs):
    owns, rest = refs[:len(cuts)], refs[len(cuts):]
    cames = []
    for n in cuts:
        cames.append(rest[:n])
        rest = rest[n:]
    send, keep = rest
    mine = bit()

    def half_of(half, out, came_half):
        def one(r, carry):
            at = 0
            for own, came in zip(owns, cames):
                size = own.shape[1 + axis]
                cut = slice(at, at + size)
                index = (r, cut) if axis == 1 else (r, slice(None), cut)
                out[index] = added(own[half, r], came[0][half, r] if len(came) == 1 else came[came_half][0, r])
                at += size
            return carry

        lax.fori_loop(0, out.shape[0], one, 0)

    if max(cuts) == 1:
        half_of(1 - mine, send, None)
        half_of(mine, keep, None)
        return
    for half in range(2):

        @pl.when(mine == half)
        def _():
            half_of(1 - half, send, 1 - half)
            half_of(half, keep, half)


def z_halves_kernel(came_parts, own, came, send, keep):
    pieces, depth = own.shape[:2]
    rest = depth // 2
    low, high = z_bits()
    core = own_core()
    if depth == 4:
        mine = jnp.where(core == 0, low, high)
        by_half, by_rest = jnp.where(core == 0, 1, 2), jnp.where(core == 0, 2, 1)
    else:
        mine = jnp.where(core == 0, high, low)
        by_half, by_rest = 1, 0

    def one(j, carry):
        p, r = lax.div(j, rest), lax.rem(j, rest)
        theirs, ours = (1 - mine) * by_half + r * by_rest, mine * by_half + r * by_rest
        send[j] = added(own[p, theirs], came[p, theirs])
        keep[j] = added(own[p, ours], came[p, ours])
        return carry

    lax.fori_loop(0, pieces * rest, one, 0)


def sum_kernel(own, came, out):
    out[...] = added(own[...].reshape(out.shape), came[...].reshape(out.shape))


def pair_kernel(own, came, out):
    lo = second_bit()
    out[lo] = own[...]
    out[1 - lo] = came[...]


def last_kernel(place, own, came, *refs):
    mine = first_bit()
    for half in range(2):
        @pl.when(mine == half)
        def _():
            for j in range(2):
                place(2 * half + j, own, j, *refs)
                place(2 * (1 - half) + j, came, j, *refs)


def place_up(p, ref, j, up, out, tail):
    unit, width = out.shape
    end = unit + tail.shape[1]
    up[:, p * width:(p + 1) * width] = ref[j, 0:unit].astype(F32)
    tail[p] = ref[j, unit:end].astype(F32)
    for g, (piece, at) in enumerate(OUT_GROUPS):
        if piece == p:
            out[g * GROUP:(g + 1) * GROUP] = ref[j, end + at * GROUP:end + (at + 1) * GROUP].astype(F32)


def place_down(p, ref, j, tail, down):
    unit = down.shape[0] // 4
    down[p * unit:p * unit + DOWN_Z] = ref[j].astype(F32)
    down[p * unit + DOWN_Z:(p + 1) * unit] = tail[p]


def place_rows(p, ref, j, query, key, value, vectors):
    unit = query.shape[0]
    tall = ref.shape[1]
    for g in range(tall // GROUP):
        at = p * tall + g * GROUP
        part = ref[j, g * GROUP:(g + 1) * GROUP].astype(F32)
        if at < 3 * unit:
            (query, key, value)[at // unit][at % unit:at % unit + GROUP] = part
        elif at == 3 * unit:
            vectors[...] = part + ref[j, (g + 1) * GROUP:(g + 2) * GROUP].astype(F32)


def page_rows_kernel(out_page, d_page, *refs):
    *came, out_rows, d_rows = refs
    span = out_rows.shape[1]
    me = own_blk()
    for which, (page, out) in enumerate(((out_page, out_rows), (d_page, d_rows))):
        out[me] = page[block(me, span), :]
        for i, part in enumerate(came):
            out[me ^ (i + 1)] = part[which]


VM = pl.BlockSpec(memory_space=pltpu.VMEM)
SM = pl.BlockSpec(memory_space=pltpu.SMEM)
HB = pl.BlockSpec(memory_space=pl.ANY)


def call(kernel, args, places, outs, scratch, limit):
    return pl.pallas_call(
        kernel,
        out_shape=[jax.ShapeDtypeStruct(s, d) for s, d in outs],
        in_specs=places,
        out_specs=[VM] * len(outs),
        scratch_shapes=[s if not isinstance(s, tuple) else pltpu.VMEM(*s) for s in scratch],
        compiler_params=pltpu.CompilerParams(vmem_limit_bytes=limit * MIB),
        cost_estimate=pl.CostEstimate(flops=1024, bytes_accessed=1024, transcendentals=0),
    )(*args)


def fetch(ids, counts, spots, table, rows):
    width = table.shape[1]
    slots = ids.shape[1]
    return call(
        fetch_kernel, (ids, counts, spots, table), [SM, SM, VM, HB], [((rows, width), BF), ((rows, 128), F32)],
        [((slots * GROUP, width), BF), ((slots * GROUP, width), F32), ((slots, width), F32), pltpu.SemaphoreType.DMA], LIMITS[0],
    )


LIMITS = [44, 16, 20, 8, 16, 10, 4]


def attend(lengths, inputs, pieces, placed, hit, biases, wq, wk, wv, wo):
    span, width = pieces[0].shape
    rows = 4 * span
    args = (lengths, inputs, *pieces, placed, hit, *biases, wq, wk, wv, wo)
    outs = [((width, rows), BF)] + [((rows, width), BF)] * 3 + [((width, rows), BF), ((HEADS, 1, rows), F32), ((HEADS, 1, rows), F32), ((rows, width), F32), ((rows, 128), F32)]
    return call(attend_kernel, args, [SM] + [VM] * 13, outs, [((rows, width), BF)] * 2, LIMITS[1])


def feed(n, cotangent, pieces, vecs, wu, wd):
    rows, width = n.shape
    ff = wu.shape[1]
    args = (n, cotangent, *pieces, *vecs, wu, wd)
    unit = width // PARTS
    groups = [((4, PARTS // 2, tall, width), BF) for tall in (DOWN_Z, 2 * unit - DOWN_Z)]
    outs = [((rows, width), BF)] + [groups[0]] * 2 + [groups[1]] * 2 + [((rows, ff), BF), ((rows, width), F32), ((16, width), F32)]
    scratch = [((rows, ff), BF)] + [((rows, width), BF)] * 2 + [((width, rows), BF), ((rows, width), BF)] + [((width, width), BF)] * 2
    return call(ff_kernel, args, [VM] * len(args), outs, scratch, LIMITS[2])


def mixed_back(n, rstd, att, dh, dfirst, vsum, gain, wu):
    rows, width = n.shape
    args = (n, rstd, att, dh, dfirst, vsum, gain, wu)
    group = ((4, PARTS // 2, 2 * GROUP, width), BF)
    outs = [group] * 2 + [((rows, width), F32), ((rows, width), BF), (vsum.shape, F32)]
    return call(mixed_kernel, args, [VM] * len(args), outs, [((width, width), BF)], LIMITS[5])


def attended_back(att, sums, dd, wo):
    rows, width = dd.shape
    outs = [((width, rows), BF), ((HEADS, 1, rows), F32)]
    return call(attended_kernel, (att, sums, dd, wo), [VM] * 4, outs, [((width, rows), F32)], LIMITS[5])


def heads(first, count, cuts, lengths, x_t, vsum, q, k, v, dst, delta, tops):
    width, rows = x_t.shape
    wide = count * HD
    tall = (3 * (width // PARTS) + 2 * GROUP) // 4
    args = (lengths, x_t, vsum, q, k, v, dst, delta, tops)
    outs = [((rows, wide), BF)] * 3 + [((4, PARTS // 2, tall, wide), BF)] + [((4 // cuts, PARTS // 2, tall, wide), BF)] * cuts
    return call(functools.partial(heads_kernel, first // 2), args, [SM] + [VM] * 8, outs, [((3, width, wide), BF)], LIMITS[3])


def inputs_grad(span, hit, out_page, dr, wq, wk, wv, parts):
    rows, width = dr.shape
    args = (hit, out_page, dr, wq, wk, wv) + tuple(t for part in parts for t in part)
    outs = [(dr.shape, BF)] + [((2, span, width), BF)] * (rows // span - 1)
    return call(functools.partial(inputs_kernel, len(parts)), args, [VM] * len(args), outs, [], LIMITS[5])


def pick(array, index, axis=0):
    return lax.dynamic_index_in_dim(array, index, axis, keepdims=False)


def swap(array, bit):
    return lax.ppermute(array, "blk", [(i, i ^ bit) for i in range(lax.axis_size("blk"))])


def swap_first(array, first):
    blks, shares = lax.axis_size("blk"), lax.axis_size("batch")
    perm = []
    for b in range(blks):
        for s in range(shares):
            bit = 1 if (s % 2 == 0) == first else 2
            perm.append((b * shares + s, (b ^ bit) * shares + s))
    return lax.ppermute(array, ("blk", "batch"), perm)


def swap_batch(array, bit):
    return lax.ppermute(array, "batch", [(i, i ^ bit) for i in range(lax.axis_size("batch"))])


def swap_z(array, first):
    shares = lax.axis_size("batch")
    return lax.ppermute(array, "batch", [(i, i ^ (2 if (i % 2 == 0) == first else 4)) for i in range(shares)])


class Cell:
    def __init__(self, *values):
        self.values = values


class Order:
    def __init__(self):
        self.last = Cell()

    def enter(self, *arrays):
        tied = lax.optimization_barrier((*arrays, *self.last.values))
        self.last.values = tied[len(arrays):]
        return tied[:len(arrays)]

    def leave(self, cell):
        self.last = cell


class Chain:
    def __init__(self, order, cell, send):
        self.order = order
        self.own, self.came = cell, tuple(swap_batch(s, 1) for s in send)

    @classmethod
    def joined(cls, order, axis, cells, cames):
        chain = cls(order, None, ())
        groups = len(cells)
        tied = order.enter(*(c.values[0] for c in cells), *(t for came in cames for t in came))
        shape = tied[0].shape
        flat = [shape[0] * shape[1] // 2, shape[2], shape[3]]
        flat[axis] = sum(t.shape[axis + 1] for t in tied[:groups])
        args = [t.reshape((-1, flat[0]) + t.shape[2:]) for t in tied]
        kernel = functools.partial(joined_halves_kernel, first_bit, axis, [len(came) for came in cames])
        send, keep = call(kernel, args, [VM] * len(args), [(tuple(flat), BF)] * 2, [], LIMITS[6])
        chain.came = [swap_first(send, True)]
        chain.own = Cell(keep.reshape((shape[0] // 2, shape[1], flat[1], flat[2])))
        order.leave(chain.own)
        return chain

    def halve(self, axis, bit, move, cuts):
        own, *came = self.order.enter(self.own.values[0], *self.came)
        shape = own.shape
        after = shape[:axis] + (shape[axis] // 2,) + shape[axis + 1:]
        flat = (after[0] * after[1],) + shape[2:]
        if axis == 0:
            own = own.reshape((2,) + flat)
            kernel = functools.partial(halves_kernel, bit, len(came))
        else:
            kernel = functools.partial(z_halves_kernel, len(came))
        came = [came[0].reshape(own.shape)]
        outs = [((flat[0] // cuts,) + shape[2:], BF)] * cuts + [(flat, BF)]
        *sends, keep = call(kernel, (own, *came), [VM] * (1 + len(came)), outs, [], LIMITS[6])
        self.came = [move(send) for send in sends]
        self.own = Cell(keep.reshape(after))
        self.order.leave(self.own)

    def first(self, cuts=1):
        self.halve(0, first_bit, lambda v: swap_first(v, True), cuts)

    def second(self, cuts=1):
        self.halve(0, second_bit, lambda v: swap_first(v, False), cuts)

    def z_first(self, cuts=1):
        self.halve(1, None, lambda v: swap_z(v, True), cuts)

    def z_second(self, cuts=1):
        self.halve(1, None, lambda v: swap_z(v, False), cuts)

    def gather_second(self):
        own, came = self.order.enter(self.own.values[0], *self.came)
        out, = call(sum_kernel, (own, came), [VM] * 2, [(own.shape[2:], BF)], [], LIMITS[6])
        self.own = Cell(out)
        self.came = (swap_first(out, False),)
        self.order.leave(self.own)

    def gather_first(self):
        own, came = self.order.enter(self.own.values[0], *self.came)
        out, = call(pair_kernel, (own, came), [VM] * 2, [((2,) + own.shape, BF)], [], LIMITS[6])
        self.own = Cell(out)
        self.came = (swap_first(out, True),)
        self.order.leave(self.own)

    def result(self, place, shapes, *others):
        own, came = self.order.enter(self.own.values[0], *self.came)
        args = (own, came, *others)
        return call(functools.partial(last_kernel, place), args, [VM] * len(args), [(s, F32) for s in shapes], [], LIMITS[6])


def own_vectors(vec, share, shares):
    width = vec.shape[-1]
    n = width // shares
    cut = lax.dynamic_slice_in_dim(vec, share * n, n, 1)
    flat = vec[B_UP:B_UP + 4].reshape(-1)
    return [cut[i] for i in range(B_UP)] + [lax.dynamic_slice_in_dim(flat, share * 4 * n, 4 * n, 0)]


def body(
    inputs, lengths, positions, counts, token_ids, table,
    w_query, b_query, w_key, w_value, b_value, w_out, b_out, gain_one, shift_one,
    w_up, b_up, w_down, b_down, gain_two, shift_two, cotangent,
):
    blk, share = lax.axis_index("blk"), lax.axis_index("batch")
    shares = lax.axis_size("batch")
    core = share % 2
    pages, span, width = inputs.shape
    ff = w_up.shape[1]
    unit = width // PARTS
    rows_in = [swap(pick(inputs, blk ^ i), i) for i in range(1, pages)]
    placed, hit = fetch(token_ids, counts, positions, table, pages * span)
    back, hit = lax.optimization_barrier((cotangent, hit))
    back_in = [swap(pick(back, blk ^ i), i) for i in range(1, pages)]
    x_t, q, k, v, att, tops, sums, n1, rstd = attend(
        lengths, inputs, rows_in, placed, hit, (b_query, b_value, b_out), w_query, w_key, w_value, w_out
    )
    out_page, d_keep, d_send, u_keep, u_send, dh, dfirst, vsum = feed(
        n1, cotangent, back_in, (b_up, b_down, gain_one, shift_one, gain_two, shift_two), w_up, w_down
    )

    def to_mixed(n1, vsum):
        return mixed_back(n1, rstd, att, dh, dfirst, vsum, gain_one, w_up)

    order = Order()

    def attention_back(first, count, vsum, dst, delta, cuts=1):
        delta, = order.enter(delta)
        dq, dk, dv, keep, *send = heads(first, count, cuts, lengths, x_t, vsum, q, k, v, dst, delta, tops)
        parts = [dq, dk, dv]
        grads = Cell(keep)
        order.leave(grads)
        return parts, grads, send

    def page_rows(out_page, d_page, came):
        return call(page_rows_kernel, (out_page, d_page, *came), [VM] * (pages + 1), [(inputs.shape, BF)] * 2, [], LIMITS[6])

    if shares == PARTS and lax.axis_size("blk") == 4:
        d = Chain(order, Cell(d_keep), [d_send])
        u_came = swap_batch(u_send, 1)
        n_now, = order.enter(n1)
        o_keep, o_send, d_r1, d_branch, vsum = to_mixed(n_now, vsum)
        o_cell = Cell(o_keep)
        order.leave(o_cell)
        o_came = swap_batch(o_send, 1)
        att_now, = order.enter(att)
        sums_cell = Cell(*attended_back(att_now, sums, d_branch, w_out))
        order.leave(sums_cell)
        d.z_first()
        u = Chain.joined(order, 1, [Cell(u_keep), o_cell], [[u_came], [o_came]])
        groups = [attention_back(0, 8, vsum, *sums_cell.values, cuts=2)]
        groups.append(attention_back(8, 4, vsum, *sums_cell.values))
        parts = [g[0] for g in groups]
        a = Chain.joined(order, 2, [g[1] for g in groups], [[swap_batch(t, 1) for t in g[2]] for g in groups])
        d.z_second()
        u.second()
        hit_now, = order.enter(hit)
        d_page, *page_parts = inputs_grad(span, hit_now, out_page, d_r1, w_query, w_key, w_value, parts)
        d_cell = Cell(d_page)
        order.leave(d_cell)
        page_parts = [swap(part, i + 1) for i, part in enumerate(page_parts)]
        a.second()
        u.z_first()
        d.first()
        a.z_first()
        u.z_second()
        d.second()
        a.z_second()
        u.gather_second()
        d.gather_second()
        d_page, *came = order.enter(*d_cell.values, *page_parts)
        rows_cell = Cell(*page_rows(out_page, d_page, came))
        order.leave(rows_cell)
        a.gather_second()
        a.gather_first()
        u.gather_first()
        d.gather_first()
        grad_up, grad_out, tail = u.result(place_up, [(unit, ff), (unit, width), (4, unit - DOWN_Z, width)])
        grad_down, = d.result(place_down, [(ff // PARTS, width)], tail)
        grad_query, grad_key, grad_value, vectors = a.result(place_rows, [(unit, width)] * 3 + [(GROUP, width)])
        outputs, d_inputs = rows_cell.values
    else:
        o_keep, o_send, d_r1, d_branch, vsum = to_mixed(n1, vsum)
        attended = attended_back(att, sums, d_branch, w_out)
        groups = [attention_back(i, 4, vsum, *attended) for i in range(0, HEADS, 4)]
        a_keep = jnp.concatenate([g[1].values[0] for g in groups], axis=-1)
        a_send = jnp.concatenate([g[2][0] for g in groups], axis=-1)
        d_page, *page_parts = inputs_grad(span, hit, out_page, d_r1, w_query, w_key, w_value, [g[0] for g in groups])
        came = [swap(part, i + 1) for i, part in enumerate(page_parts)]
        outputs, d_inputs = page_rows(out_page, d_page, came)

        def parity(keep, send):
            packed = jnp.where(core == 0, jnp.stack([keep, send]), jnp.stack([send, keep]))
            return packed.transpose(1, 2, 0, 3, 4)

        def over(grad):
            part = lax.psum_scatter(grad.astype(F32), "batch", scatter_dimension=0, tiled=True)
            return lax.psum(part.astype(BF), "blk").astype(F32)

        out = parity(o_keep, o_send)
        out = jnp.concatenate([out[p][..., at * GROUP:(at + 1) * GROUP, :] for p, at in OUT_GROUPS], axis=-2)
        out = out.reshape(width, width)
        up = parity(u_keep, u_send)
        down = jnp.concatenate([parity(d_keep, d_send), up[..., unit:, :]], axis=-2)
        down = down.transpose(1, 2, 0, 3, 4).reshape(ff, width)
        up = up[..., :unit, :].transpose(1, 2, 3, 0, 4).reshape(width, ff)
        rows = parity(a_keep, a_send).transpose(1, 2, 0, 3, 4).reshape(PARTS, -1, width)
        mats = [rows[:, i * unit:(i + 1) * unit].reshape(width, width) for i in range(3)]
        vectors = rows[0, 3 * unit:3 * unit + GROUP].astype(F32) + rows[0, 3 * unit + GROUP:].astype(F32)
        vectors = lax.psum(vectors, ("blk", "batch"))
        grad_down, grad_up, grad_out = over(down), over(up), over(out)
        grad_query, grad_key, grad_value = (over(m) for m in mats)
    r = own_vectors(vectors, share, shares)
    return (
        outputs, d_inputs, grad_query, r[B_QUERY], grad_key, grad_value, r[B_VALUE], grad_out, r[B_OUT],
        r[GAIN_ONE], r[SHIFT_ONE], grad_up, r[B_UP], grad_down, r[B_DOWN], r[GAIN_TWO], r[SHIFT_TWO],
    )


def solution(mesh):
    split, whole = P("batch", "blk", None), P()
    rows, vec = P("batch", None), P("batch")
    in_specs = (split, vec, rows, vec, rows) + (whole,) * 16 + (split,)
    out_specs = (split, split, rows, vec, rows, rows, vec, rows, vec, vec, vec, rows, vec, rows, vec, vec, vec)
    return jax.shard_map(body, mesh=mesh, in_specs=in_specs, out_specs=out_specs, check_vma=False)
```

```python
import functools

import jax
import jax.numpy as jnp
from jax import lax
from jax.experimental import pallas as pl
from jax.experimental.pallas import tpu as pltpu
from jax.sharding import PartitionSpec as P

HEADS = 12
HD = 64
SCALE = 0.125
NEGATIVE = -1e30
EPSILON = 1e-12
BF = jnp.bfloat16
F32 = jnp.float32
MIB = 1024 * 1024
GROUP = 16
PARTS = 8
DOWN_Z = 80
B_QUERY, B_VALUE, B_OUT, B_DOWN, GAIN_ONE, SHIFT_ONE, GAIN_TWO, SHIFT_TWO, B_UP = range(9)


def nn(a, b):
    return lax.dot_general(a, b, (((1,), (0,)), ((), ())), preferred_element_type=F32)


def nt(a, b):
    return lax.dot_general(a, b, (((1,), (1,)), ((), ())), preferred_element_type=F32)


def tn(a, b):
    return lax.dot_general(a, b, (((0,), (0,)), ((), ())), preferred_element_type=F32)


def head_lanes(shape, which):
    lane = lax.broadcasted_iota(jnp.int32, shape, 1)
    return (lane >= HD) if which else (lane < HD)


def norm_parts(v):
    width = v.shape[-1]
    centre = jnp.sum(v, axis=-1, keepdims=True) * (1.0 / width)
    centred = v - centre
    spread = jnp.sum(centred * centred, axis=-1, keepdims=True) * (1.0 / width)
    rstd = lax.rsqrt(spread + EPSILON)
    return centred * rstd, rstd


def norm_back(c2, n, rstd):
    width = c2.shape[-1]
    a = jnp.sum(c2, axis=-1, keepdims=True) * (1.0 / width)
    b = jnp.sum(c2 * n, axis=-1, keepdims=True) * (1.0 / width)
    return (c2 - a - n * b) * rstd


def colsum(v):
    return jnp.sum(v, axis=0, keepdims=True)


def wide_row(ref):
    return ref[...].astype(F32).reshape(1, ref.shape[0])


def block(i, size):
    return pl.ds(pl.multiple_of(i * size, size), size)


def own_blk():
    return lax.axis_index("blk")


def own_core():
    return lax.rem(lax.axis_index("batch"), 2)


def first_bit():
    return jnp.where(own_core() == 0, lax.rem(own_blk(), 2), lax.div(own_blk(), 2))


def second_bit():
    return jnp.where(own_core() == 0, lax.div(own_blk(), 2), lax.rem(own_blk(), 2))


def z_bits():
    z = lax.div(lax.axis_index("batch"), 2)
    return lax.rem(z, 2), lax.div(z, 2)


def fetch_kernel(ids_ref, counts_ref, spots_ref, table_ref, placed_ref, hit_ref, rows_ref, wide_ref, sel_ref, sem):
    slots = ids_ref.shape[1]
    me = own_blk()

    def start(j, carry):
        group = pl.multiple_of((ids_ref[me, j] // GROUP) * GROUP, GROUP)
        pltpu.make_async_copy(table_ref.at[pl.ds(group, GROUP), :], rows_ref.at[block(j, GROUP), :], sem).start()
        return carry

    lax.fori_loop(0, slots, start, 0, unroll=8)
    total = placed_ref.shape[0]
    spot = lax.broadcasted_iota(jnp.int32, (total, slots), 0)
    slot = lax.broadcasted_iota(jnp.int32, (total, slots), 1)
    hits = ((spots_ref[pl.ds(me, 1), :] == spot) & (slot < counts_ref[me])).astype(F32)
    hit_ref[...] = jnp.broadcast_to(jnp.sum(hits, axis=1, keepdims=True), hit_ref.shape)
    pltpu.make_async_copy(table_ref.at[pl.ds(0, slots * GROUP), :], rows_ref, sem).wait()
    wide_ref[...] = rows_ref[...].astype(F32)

    def select(j, carry):
        at = j * GROUP + lax.rem(ids_ref[me, j], GROUP)
        sel_ref[pl.ds(j, 1), :] = wide_ref[pl.ds(at, 1), :]
        return carry

    lax.fori_loop(0, slots, select, 0, unroll=8)
    placed_ref[...] = nn(hits.astype(BF), sel_ref[...].astype(BF)).astype(BF)


def attend_kernel(
    lengths_ref, inputs_ref, p1_ref, p2_ref, p3_ref, placed_ref, hit_ref, bq_ref, bv_ref, bo_ref,
    wq_ref, wk_ref, wv_ref, wo_ref,
    x_t_ref, q_ref, k_ref, v_ref, att_ref, max_ref, sum_ref, n_ref, rstd_ref,
    x_ref, att_rows,
):
    me = own_blk()
    length = lengths_ref[me]
    rows, width = x_ref.shape
    span = p1_ref.shape[0]
    for step, piece in enumerate((inputs_ref[me], p1_ref[...], p2_ref[...], p3_ref[...])):
        at = block(me ^ step, span)
        x_ref[at, :] = jnp.where(hit_ref[at, 0:1] > 0.5, placed_ref[at, :], piece)
    x_t_ref[...] = x_ref[...].T
    q = (nn(x_ref[...], wq_ref[...]) + wide_row(bq_ref)).astype(BF)
    q_ref[...] = (q.astype(F32) * SCALE).astype(BF)
    k_ref[...] = nn(x_ref[...], wk_ref[...]).astype(BF)
    v_ref[...] = (nn(x_ref[...], wv_ref[...]) + wide_row(bv_ref)).astype(BF)
    dead = jnp.where(lax.broadcasted_iota(jnp.int32, (rows, 1), 0) < length, 0.0, NEGATIVE)

    def pair(i, carry):
        lanes = block(i, 2 * HD)
        q2, k2 = q_ref[:, lanes], k_ref[:, lanes]
        v2t = v_ref[:, lanes].T
        for h in range(2):
            qm = jnp.where(head_lanes(q2.shape, h), q2, jnp.zeros_like(q2))
            s = nt(k2, qm) + dead
            top = jnp.max(s, axis=0, keepdims=True)
            p = jnp.exp(s - top)
            total = jnp.sum(p, axis=0, keepdims=True)
            o = nn(v2t[h * HD:(h + 1) * HD], p.astype(BF)) / total
            max_ref[2 * i + h] = top
            sum_ref[2 * i + h] = total
            att_ref[block(2 * i + h, HD), :] = o.astype(BF)
        att_rows[:, lanes] = att_ref[lanes, :].T
        return carry

    lax.fori_loop(0, HEADS // 2, pair, 0, unroll=True)
    branch = nn(att_rows[...], wo_ref[...]) + wide_row(bo_ref)
    n, rstd = norm_parts(x_ref[...].astype(F32) + branch)
    n_ref[...] = n
    rstd_ref[...] = jnp.broadcast_to(rstd, rstd_ref.shape)


def gelu_both(v):
    e = jnp.exp2(v * v * -0.7213475204444817)
    t = pl.reciprocal(1.0 + (0.3275911 * 0.7071067811865476) * jnp.abs(v))
    poly = t * (0.5 * 0.254829592 + t * (0.5 * -0.284496736 + t * (0.5 * 1.421413741 + t * (0.5 * -1.453152027 + t * (0.5 * 1.061405429)))))
    tail = poly * e
    phi = jnp.where(v >= 0, 1.0 - tail, tail)
    return v * phi, phi + v * (e * 0.3989422804014327)


def by_core(core, deal, keep, send):
    for c in range(2):

        @pl.when(core == c)
        def _():
            deal(c, *keep)
            deal(1 - c, *send)


OUT_GROUPS = [(0, 0), (0, 1), (1, 0), (1, 1), (2, 0), (3, 0)]


def ff_kernel(
    n_ref, cot_ref, c1_ref, c2_ref, c3_ref,
    bu_ref, bd_ref, g1_ref, s1_ref, g2_ref, s2_ref, wu_ref, wd_ref,
    out_ref, dkeep, dsend, ukeep, usend, dh_ref, dfirst_ref, vsum_ref,
    act, cot, nlow, nlow_t, dd, g_down, g_up,
):
    width = n_ref.shape[1]
    ff = wu_ref.shape[1]
    parts = ff // width
    shares = 2 * dkeep.shape[1]
    unit = width // shares
    span = c1_ref.shape[0]
    me, core = own_blk(), own_core()
    for hop, piece in enumerate((cot_ref[me], c1_ref[...], c2_ref[...], c3_ref[...])):
        cot[block(me ^ hop, span), :] = piece
    normed = n_ref[...] * wide_row(g1_ref) + wide_row(s1_ref)
    nlow[...] = normed.astype(BF)
    nlow_t[...] = nlow[...].T
    for i in range(parts):
        lanes = slice(i * width, (i + 1) * width)
        a, b = gelu_both(nn(nlow[...], wu_ref[:, lanes]) + wide_row(bu_ref)[:, lanes])
        act[:, lanes] = a.astype(BF)
        dh_ref[:, lanes] = b.astype(BF)
    normed = n_ref[...] * wide_row(g1_ref) + wide_row(s1_ref)
    resid = normed + nn(act[...], wd_ref[...]) + wide_row(bd_ref)
    n2, rstd2 = norm_parts(resid)
    out_ref[...] = (n2 * wide_row(g2_ref) + wide_row(s2_ref)).astype(BF)
    c = cot[...].astype(F32)
    vsum_ref[...] = jnp.zeros_like(vsum_ref)
    vsum_ref[GAIN_TWO:GAIN_TWO + 1] = colsum(c * n2)
    vsum_ref[SHIFT_TWO:SHIFT_TWO + 1] = colsum(c)
    d_r2 = norm_back(c * wide_row(g2_ref), n2, rstd2)
    dfirst_ref[...] = d_r2
    dd[...] = d_r2.astype(BF)
    vsum_ref[B_DOWN:B_DOWN + 1] = colsum(dd[...].astype(F32))

    def back(i, carry):
        lanes = block(i, width)
        g_down[...] = tn(act[:, lanes], dd[...]).astype(BF)
        dhc = (nt(dd[...], wd_ref[lanes, :]) * dh_ref[:, lanes].astype(F32)).astype(BF)
        dh_ref[:, lanes] = dhc
        vsum_ref[pl.ds(B_UP + i, 1)] = colsum(dhc.astype(F32))
        g_up[...] = nn(nlow_t[...], dhc).astype(BF)

        def deal(c, down, up):
            for p in range(4):
                at = (c * 4 + p) * unit
                down[p, i] = g_down[at:at + DOWN_Z]
                up[p, i, unit:] = g_down[at + DOWN_Z:at + unit]
            for z in range(shares // 2):
                at = (2 * z + c) * unit
                up[i, z, 0:unit] = g_up[at:at + unit]

        by_core(core, deal, (dkeep, ukeep), (dsend, usend))
        return carry

    lax.fori_loop(0, parts, back, 0)


def mixed_kernel(
    n_ref, rstd_ref, att_ref, dh_ref, dfirst_ref, vin_ref, g1_ref, wu_ref,
    okeep, osend, dr_ref, dd, vsum_ref,
    g_out,
):
    width = n_ref.shape[1]
    shares = 2 * okeep.shape[1]
    unit = width // shares

    def first(i, carry):
        lanes = block(i, width // 3)
        dr_ref[:, lanes] = dfirst_ref[:, lanes] + nt(dh_ref[...], wu_ref[lanes, :])
        return carry

    lax.fori_loop(0, 3, first, 0)
    d_f = dr_ref[...]
    n1 = n_ref[...]
    vsum_ref[...] = vin_ref[...]
    vsum_ref[GAIN_ONE:GAIN_ONE + 1] = colsum(d_f * n1)
    vsum_ref[SHIFT_ONE:SHIFT_ONE + 1] = colsum(d_f)
    d_r1 = norm_back(d_f * wide_row(g1_ref), n1, rstd_ref[:, 0:1])
    dr_ref[...] = d_r1
    db = d_r1.astype(BF)
    dd[...] = db
    vsum_ref[B_OUT:B_OUT + 1] = colsum(db.astype(F32))
    g_out[...] = nn(att_ref[...], dd[...]).astype(BF)

    def deal(c, out):
        for z in range(shares // 2):
            for g in range(unit // GROUP):
                p, at = OUT_GROUPS[g]
                src = (2 * z + c) * unit + g * GROUP
                out[p, z, at * GROUP:(at + 1) * GROUP] = g_out[src:src + GROUP]
            for p in (2, 3):
                out[p, z, GROUP:2 * GROUP] = jnp.zeros((GROUP, width), BF)

    by_core(own_core(), deal, (okeep,), (osend,))


def attended_kernel(att_ref, sum_ref, dd_ref, wo_ref, dst_ref, delta_ref, dm_ref):
    dm_ref[...] = nt(wo_ref[...], dd_ref[...])
    for i in range(HEADS):
        at = slice(i * HD, (i + 1) * HD)
        inv = 1.0 / sum_ref[i]
        delta_ref[i] = colsum(dm_ref[at, :] * att_ref[at, :].astype(F32)) * inv
        dst_ref[at, :] = (dm_ref[at, :] * inv).astype(BF)


def heads_kernel(first, lengths_ref, x_t_ref, vin_ref, q_ref, k_ref, v_ref, dst_ref, delta_ref, max_ref, dq, dk, dv, keep, *sends):
    *sends, g_ref = sends
    length = lengths_ref[own_blk()]
    rows = q_ref.shape[0]
    dead = jnp.where(lax.broadcasted_iota(jnp.int32, (rows, 1), 0) < length, 0.0, NEGATIVE)

    def pair(i, carry):
        lanes, own = block(first + i, 2 * HD), block(i, 2 * HD)
        q2, k2, v2 = q_ref[:, lanes], k_ref[:, lanes], v_ref[:, lanes]
        dst = dst_ref[lanes, :]
        ds2 = dst.T
        k2t = k2.T
        dv2 = jnp.zeros((rows, 2 * HD), F32)
        dk2 = jnp.zeros((rows, 2 * HD), F32)
        dqs = []
        for h in range(2):
            live = head_lanes(q2.shape, h)
            zero = jnp.zeros_like(q2)
            qm = jnp.where(live, q2, zero)
            s = nt(k2, qm) + dead
            head = 2 * (first + i) + h
            p = jnp.exp(s - max_ref[head])
            dp = nn(jnp.where(live, v2, zero), dst)
            dsc = (p * (dp - delta_ref[head])).astype(BF)
            dv2 = dv2 + nn(p.astype(BF), jnp.where(live, ds2, zero))
            dk2 = dk2 + nn(dsc, qm)
            dqs.append(nn(k2t[h * HD:(h + 1) * HD], dsc))
        dq[:, own] = (jnp.concatenate(dqs, axis=0) * SCALE).astype(BF).T
        dk[:, own] = dk2.astype(BF)
        dv[:, own] = dv2.astype(BF)
        return carry

    lax.fori_loop(0, dq.shape[1] // (2 * HD), pair, 0)
    for i, part in enumerate((dq, dk, dv)):
        g_ref[i] = nn(x_t_ref[...], part[...]).astype(BF)
    vsum = vin_ref[:, first * 2 * HD:first * 2 * HD + dq.shape[1]]
    row = lax.broadcasted_iota(jnp.int32, vsum.shape, 0)
    vsum = vsum + jnp.where(row == B_QUERY, colsum(dq[...].astype(F32)), 0.0) + jnp.where(row == B_VALUE, colsum(dv[...].astype(F32)), 0.0)
    high = vsum.astype(BF)
    low = (vsum - high.astype(F32)).astype(BF)
    shares = 2 * keep.shape[1]
    unit = x_t_ref.shape[0] // shares
    tall = keep.shape[2]

    def deal(c, *pieces):
        def one(z, carry):
            for i in range(3):
                for j in range(unit // GROUP):
                    at = i * unit + j * GROUP
                    src = pl.ds(pl.multiple_of((2 * z + c) * unit + j * GROUP, GROUP), GROUP)
                    pieces[at // tall][z, at % tall:at % tall + GROUP] = g_ref[i, src]
            pieces[3][z, tall - 2 * GROUP:tall - GROUP] = high
            pieces[3][z, tall - GROUP:tall] = low
            return carry

        lax.fori_loop(0, shares // 2, one, 0)

    per = 4 // len(sends)
    by_core(own_core(), deal, [keep.at[p] for p in range(4)], [sends[p // per].at[p % per] for p in range(4)])


def inputs_kernel(groups, hit_ref, out_page, dr_ref, wq_ref, wk_ref, wv_ref, *refs):
    parts = [refs[3 * g:3 * g + 3] for g in range(groups)]
    din_ref, *outs = refs[3 * groups:]
    total = dr_ref[...]
    for i, w in enumerate((wq_ref, wk_ref, wv_ref)):
        at = 0
        for part in parts:
            wide = part[i].shape[1]
            total = total + nt(part[i][...], w[:, at:at + wide])
            at += wide
    din_ref[...] = jnp.where(hit_ref[:, 0:1] > 0.5, 0.0, total).astype(BF)
    span = outs[0].shape[1]
    for i, out in enumerate(outs):
        rows = block(own_blk() ^ (i + 1), span)
        out[0] = out_page[rows, :]
        out[1] = din_ref[rows, :]


def added(a, b):
    return (a.astype(F32) + b.astype(F32)).astype(BF)


def halves_kernel(bit, came_parts, own, came, send, keep):
    mine = bit()

    def one(r, carry):
        send[r] = added(own[1 - mine, r], came[1 - mine, r])
        keep[r] = added(own[mine, r], came[mine, r])
        return carry

    lax.fori_loop(0, own.shape[1], one, 0)


def joined_halves_kernel(bit, axis, cuts, *refs):
    owns, rest = refs[:len(cuts)], refs[len(cuts):]
    cames = []
    for n in cuts:
        cames.append(rest[:n])
        rest = rest[n:]
    send, keep = rest
    mine = bit()

    def half_of(half, out, came_half):
        def one(r, carry):
            at = 0
            for own, came in zip(owns, cames):
                size = own.shape[1 + axis]
                cut = slice(at, at + size)
                index = (r, cut) if axis == 1 else (r, slice(None), cut)
                out[index] = added(own[half, r], came[0][half, r] if len(came) == 1 else came[came_half][0, r])
                at += size
            return carry

        lax.fori_loop(0, out.shape[0], one, 0)

    if max(cuts) == 1:
        half_of(1 - mine, send, None)
        half_of(mine, keep, None)
        return
    for half in range(2):

        @pl.when(mine == half)
        def _():
            half_of(1 - half, send, 1 - half)
            half_of(half, keep, half)


def z_halves_kernel(came_parts, own, came, send, keep):
    pieces, depth = own.shape[:2]
    rest = depth // 2
    low, high = z_bits()
    core = own_core()
    if depth == 4:
        mine = jnp.where(core == 0, low, high)
        by_half, by_rest = jnp.where(core == 0, 1, 2), jnp.where(core == 0, 2, 1)
    else:
        mine = jnp.where(core == 0, high, low)
        by_half, by_rest = 1, 0

    def one(j, carry):
        p, r = lax.div(j, rest), lax.rem(j, rest)
        theirs, ours = (1 - mine) * by_half + r * by_rest, mine * by_half + r * by_rest
        send[j] = added(own[p, theirs], came[p, theirs])
        keep[j] = added(own[p, ours], came[p, ours])
        return carry

    lax.fori_loop(0, pieces * rest, one, 0)


def sum_kernel(own, came, out):
    out[...] = added(own[...].reshape(out.shape), came[...].reshape(out.shape))


def pair_kernel(own, came, out):
    lo = second_bit()
    out[lo] = own[...]
    out[1 - lo] = came[...]


def last_kernel(place, own, came, *refs):
    mine = first_bit()
    for half in range(2):
        @pl.when(mine == half)
        def _():
            for j in range(2):
                place(2 * half + j, own, j, *refs)
                place(2 * (1 - half) + j, came, j, *refs)


def place_up(p, ref, j, up, out, tail):
    unit, width = out.shape
    end = unit + tail.shape[1]
    up[:, p * width:(p + 1) * width] = ref[j, 0:unit].astype(F32)
    tail[p] = ref[j, unit:end].astype(F32)
    for g, (piece, at) in enumerate(OUT_GROUPS):
        if piece == p:
            out[g * GROUP:(g + 1) * GROUP] = ref[j, end + at * GROUP:end + (at + 1) * GROUP].astype(F32)


def place_down(p, ref, j, tail, down):
    unit = down.shape[0] // 4
    down[p * unit:p * unit + DOWN_Z] = ref[j].astype(F32)
    down[p * unit + DOWN_Z:(p + 1) * unit] = tail[p]


def last_two_kernel(up_own, up_came, down_own, down_came, up, out, down, tail):
    last_kernel(place_up, up_own, up_came, up, out, tail)
    last_kernel(place_down, down_own, down_came, tail, down)


def place_rows(p, ref, j, query, key, value, vectors):
    unit = query.shape[0]
    tall = ref.shape[1]
    for g in range(tall // GROUP):
        at = p * tall + g * GROUP
        part = ref[j, g * GROUP:(g + 1) * GROUP].astype(F32)
        if at < 3 * unit:
            (query, key, value)[at // unit][at % unit:at % unit + GROUP] = part
        elif at == 3 * unit:
            vectors[...] = part + ref[j, (g + 1) * GROUP:(g + 2) * GROUP].astype(F32)


def page_rows_kernel(out_page, d_page, *refs):
    *came, out_rows, d_rows = refs
    span = out_rows.shape[1]
    me = own_blk()
    for which, (page, out) in enumerate(((out_page, out_rows), (d_page, d_rows))):
        out[me] = page[block(me, span), :]
        for i, part in enumerate(came):
            out[me ^ (i + 1)] = part[which]


VM = pl.BlockSpec(memory_space=pltpu.VMEM)
SM = pl.BlockSpec(memory_space=pltpu.SMEM)
HB = pl.BlockSpec(memory_space=pl.ANY)


def call(kernel, args, places, outs, scratch, limit):
    return pl.pallas_call(
        kernel,
        out_shape=[jax.ShapeDtypeStruct(s, d) for s, d in outs],
        in_specs=places,
        out_specs=[VM] * len(outs),
        scratch_shapes=[s if not isinstance(s, tuple) else pltpu.VMEM(*s) for s in scratch],
        compiler_params=pltpu.CompilerParams(vmem_limit_bytes=limit * MIB),
        cost_estimate=pl.CostEstimate(flops=1024, bytes_accessed=1024, transcendentals=0),
    )(*args)


def fetch(ids, counts, spots, table, rows):
    width = table.shape[1]
    slots = ids.shape[1]
    return call(
        fetch_kernel, (ids, counts, spots, table), [SM, SM, VM, HB], [((rows, width), BF), ((rows, 128), F32)],
        [((slots * GROUP, width), BF), ((slots * GROUP, width), F32), ((slots, width), F32), pltpu.SemaphoreType.DMA], LIMITS[0],
    )


LIMITS = [44, 16, 20, 8, 16, 10, 4]


def attend(lengths, inputs, pieces, placed, hit, biases, wq, wk, wv, wo):
    span, width = pieces[0].shape
    rows = 4 * span
    args = (lengths, inputs, *pieces, placed, hit, *biases, wq, wk, wv, wo)
    outs = [((width, rows), BF)] + [((rows, width), BF)] * 3 + [((width, rows), BF), ((HEADS, 1, rows), F32), ((HEADS, 1, rows), F32), ((rows, width), F32), ((rows, 128), F32)]
    return call(attend_kernel, args, [SM] + [VM] * 13, outs, [((rows, width), BF)] * 2, LIMITS[1])


def feed(n, cotangent, pieces, vecs, wu, wd):
    rows, width = n.shape
    ff = wu.shape[1]
    args = (n, cotangent, *pieces, *vecs, wu, wd)
    unit = width // PARTS
    groups = [((4, PARTS // 2, tall, width), BF) for tall in (DOWN_Z, 2 * unit - DOWN_Z)]
    outs = [((rows, width), BF)] + [groups[0]] * 2 + [groups[1]] * 2 + [((rows, ff), BF), ((rows, width), F32), ((16, width), F32)]
    scratch = [((rows, ff), BF)] + [((rows, width), BF)] * 2 + [((width, rows), BF), ((rows, width), BF)] + [((width, width), BF)] * 2
    return call(ff_kernel, args, [VM] * len(args), outs, scratch, LIMITS[2])


def mixed_back(n, rstd, att, dh, dfirst, vsum, gain, wu):
    rows, width = n.shape
    args = (n, rstd, att, dh, dfirst, vsum, gain, wu)
    group = ((4, PARTS // 2, 2 * GROUP, width), BF)
    outs = [group] * 2 + [((rows, width), F32), ((rows, width), BF), (vsum.shape, F32)]
    return call(mixed_kernel, args, [VM] * len(args), outs, [((width, width), BF)], LIMITS[5])


def attended_back(att, sums, dd, wo):
    rows, width = dd.shape
    outs = [((width, rows), BF), ((HEADS, 1, rows), F32)]
    return call(attended_kernel, (att, sums, dd, wo), [VM] * 4, outs, [((width, rows), F32)], LIMITS[5])


def heads(first, count, cuts, lengths, x_t, vsum, q, k, v, dst, delta, tops):
    width, rows = x_t.shape
    wide = count * HD
    tall = (3 * (width // PARTS) + 2 * GROUP) // 4
    args = (lengths, x_t, vsum, q, k, v, dst, delta, tops)
    outs = [((rows, wide), BF)] * 3 + [((4, PARTS // 2, tall, wide), BF)] + [((4 // cuts, PARTS // 2, tall, wide), BF)] * cuts
    return call(functools.partial(heads_kernel, first // 2), args, [SM] + [VM] * 8, outs, [((3, width, wide), BF)], LIMITS[3])


def inputs_grad(span, hit, out_page, dr, wq, wk, wv, parts):
    rows, width = dr.shape
    args = (hit, out_page, dr, wq, wk, wv) + tuple(t for part in parts for t in part)
    outs = [(dr.shape, BF)] + [((2, span, width), BF)] * (rows // span - 1)
    return call(functools.partial(inputs_kernel, len(parts)), args, [VM] * len(args), outs, [], LIMITS[5])


def pick(array, index, axis=0):
    return lax.dynamic_index_in_dim(array, index, axis, keepdims=False)


def swap(array, bit):
    return lax.ppermute(array, "blk", [(i, i ^ bit) for i in range(lax.axis_size("blk"))])


def swap_first(array, first):
    blks, shares = lax.axis_size("blk"), lax.axis_size("batch")
    perm = []
    for b in range(blks):
        for s in range(shares):
            bit = 1 if (s % 2 == 0) == first else 2
            perm.append((b * shares + s, (b ^ bit) * shares + s))
    return lax.ppermute(array, ("blk", "batch"), perm)


def swap_batch(array, bit):
    return lax.ppermute(array, "batch", [(i, i ^ bit) for i in range(lax.axis_size("batch"))])


def swap_z(array, first):
    shares = lax.axis_size("batch")
    return lax.ppermute(array, "batch", [(i, i ^ (2 if (i % 2 == 0) == first else 4)) for i in range(shares)])


class Cell:
    def __init__(self, *values):
        self.values = values


class Order:
    def __init__(self):
        self.last = Cell()

    def enter(self, *arrays):
        tied = lax.optimization_barrier((*arrays, *self.last.values))
        self.last.values = tied[len(arrays):]
        return tied[:len(arrays)]

    def leave(self, cell):
        self.last = cell


class Chain:
    def __init__(self, order, cell, send):
        self.order = order
        self.own, self.came = cell, tuple(swap_batch(s, 1) for s in send)

    @classmethod
    def joined(cls, order, axis, cells, cames):
        chain = cls(order, None, ())
        groups = len(cells)
        tied = order.enter(*(c.values[0] for c in cells), *(t for came in cames for t in came))
        shape = tied[0].shape
        flat = [shape[0] * shape[1] // 2, shape[2], shape[3]]
        flat[axis] = sum(t.shape[axis + 1] for t in tied[:groups])
        args = [t.reshape((-1, flat[0]) + t.shape[2:]) for t in tied]
        kernel = functools.partial(joined_halves_kernel, first_bit, axis, [len(came) for came in cames])
        send, keep = call(kernel, args, [VM] * len(args), [(tuple(flat), BF)] * 2, [], LIMITS[6])
        chain.came = [swap_first(send, True)]
        chain.own = Cell(keep.reshape((shape[0] // 2, shape[1], flat[1], flat[2])))
        order.leave(chain.own)
        return chain

    def halve(self, axis, bit, move, cuts):
        own, *came = self.order.enter(self.own.values[0], *self.came)
        shape = own.shape
        after = shape[:axis] + (shape[axis] // 2,) + shape[axis + 1:]
        flat = (after[0] * after[1],) + shape[2:]
        if axis == 0:
            own = own.reshape((2,) + flat)
            kernel = functools.partial(halves_kernel, bit, len(came))
        else:
            kernel = functools.partial(z_halves_kernel, len(came))
        came = [came[0].reshape(own.shape)]
        outs = [((flat[0] // cuts,) + shape[2:], BF)] * cuts + [(flat, BF)]
        *sends, keep = call(kernel, (own, *came), [VM] * (1 + len(came)), outs, [], LIMITS[6])
        self.came = [move(send) for send in sends]
        self.own = Cell(keep.reshape(after))
        self.order.leave(self.own)

    def first(self, cuts=1):
        self.halve(0, first_bit, lambda v: swap_first(v, True), cuts)

    def second(self, cuts=1):
        self.halve(0, second_bit, lambda v: swap_first(v, False), cuts)

    def z_first(self, cuts=1):
        self.halve(1, None, lambda v: swap_z(v, True), cuts)

    def z_second(self, cuts=1):
        self.halve(1, None, lambda v: swap_z(v, False), cuts)

    def gather_second(self):
        own, came = self.order.enter(self.own.values[0], *self.came)
        out, = call(sum_kernel, (own, came), [VM] * 2, [(own.shape[2:], BF)], [], LIMITS[6])
        self.own = Cell(out)
        self.came = (swap_first(out, False),)
        self.order.leave(self.own)

    def gather_first(self):
        own, came = self.order.enter(self.own.values[0], *self.came)
        out, = call(pair_kernel, (own, came), [VM] * 2, [((2,) + own.shape, BF)], [], LIMITS[6])
        self.own = Cell(out)
        self.came = (swap_first(out, True),)
        self.order.leave(self.own)

    def result(self, place, shapes, *others):
        own, came = self.order.enter(self.own.values[0], *self.came)
        args = (own, came, *others)
        return call(functools.partial(last_kernel, place), args, [VM] * len(args), [(s, F32) for s in shapes], [], LIMITS[6])


def own_vectors(vec, share, shares):
    width = vec.shape[-1]
    n = width // shares
    cut = lax.dynamic_slice_in_dim(vec, share * n, n, 1)
    flat = vec[B_UP:B_UP + 4].reshape(-1)
    return [cut[i] for i in range(B_UP)] + [lax.dynamic_slice_in_dim(flat, share * 4 * n, 4 * n, 0)]


def body(
    inputs, lengths, positions, counts, token_ids, table,
    w_query, b_query, w_key, w_value, b_value, w_out, b_out, gain_one, shift_one,
    w_up, b_up, w_down, b_down, gain_two, shift_two, cotangent,
):
    blk, share = lax.axis_index("blk"), lax.axis_index("batch")
    shares = lax.axis_size("batch")
    core = share % 2
    pages, span, width = inputs.shape
    ff = w_up.shape[1]
    unit = width // PARTS
    rows_in = [swap(pick(inputs, blk ^ i), i) for i in range(1, pages)]
    placed, hit = fetch(token_ids, counts, positions, table, pages * span)
    back, hit = lax.optimization_barrier((cotangent, hit))
    back_in = [swap(pick(back, blk ^ i), i) for i in range(1, pages)]
    x_t, q, k, v, att, tops, sums, n1, rstd = attend(
        lengths, inputs, rows_in, placed, hit, (b_query, b_value, b_out), w_query, w_key, w_value, w_out
    )
    out_page, d_keep, d_send, u_keep, u_send, dh, dfirst, vsum = feed(
        n1, cotangent, back_in, (b_up, b_down, gain_one, shift_one, gain_two, shift_two), w_up, w_down
    )

    def to_mixed(n1, vsum):
        return mixed_back(n1, rstd, att, dh, dfirst, vsum, gain_one, w_up)

    order = Order()

    def attention_back(first, count, vsum, dst, delta, cuts=1):
        delta, = order.enter(delta)
        dq, dk, dv, keep, *send = heads(first, count, cuts, lengths, x_t, vsum, q, k, v, dst, delta, tops)
        parts = [dq, dk, dv]
        grads = Cell(keep)
        order.leave(grads)
        return parts, grads, send

    def page_rows(out_page, d_page, came):
        return call(page_rows_kernel, (out_page, d_page, *came), [VM] * (pages + 1), [(inputs.shape, BF)] * 2, [], LIMITS[6])

    if shares == PARTS and lax.axis_size("blk") == 4:
        d = Chain(order, Cell(d_keep), [d_send])
        u_came = swap_batch(u_send, 1)
        n_now, = order.enter(n1)
        o_keep, o_send, d_r1, d_branch, vsum = to_mixed(n_now, vsum)
        o_cell = Cell(o_keep)
        order.leave(o_cell)
        o_came = swap_batch(o_send, 1)
        att_now, = order.enter(att)
        sums_cell = Cell(*attended_back(att_now, sums, d_branch, w_out))
        order.leave(sums_cell)
        d.z_first()
        u = Chain.joined(order, 1, [Cell(u_keep), o_cell], [[u_came], [o_came]])
        groups = [attention_back(0, 8, vsum, *sums_cell.values, cuts=2)]
        groups.append(attention_back(8, 4, vsum, *sums_cell.values))
        parts = [g[0] for g in groups]
        a = Chain.joined(order, 2, [g[1] for g in groups], [[swap_batch(t, 1) for t in g[2]] for g in groups])
        d.z_second()
        u.second()
        hit_now, = order.enter(hit)
        d_page, *page_parts = inputs_grad(span, hit_now, out_page, d_r1, w_query, w_key, w_value, parts)
        d_cell = Cell(d_page)
        order.leave(d_cell)
        page_parts = [swap(part, i + 1) for i, part in enumerate(page_parts)]
        a.second()
        u.z_first()
        d.first()
        a.z_first()
        u.z_second()
        d.second()
        a.z_second()
        u.gather_second()
        d.gather_second()
        d_page, *came = order.enter(*d_cell.values, *page_parts)
        rows_cell = Cell(*page_rows(out_page, d_page, came))
        order.leave(rows_cell)
        a.gather_second()
        a.gather_first()
        u.gather_first()
        d.gather_first()
        args = order.enter(u.own.values[0], *u.came, d.own.values[0], *d.came)
        shapes = [(unit, ff), (unit, width), (ff // PARTS, width)]
        tail = ((4, unit - DOWN_Z, width), F32)
        grad_up, grad_out, grad_down = call(last_two_kernel, args, [VM] * 4, [(t, F32) for t in shapes], [tail], LIMITS[6])
        grad_query, grad_key, grad_value, vectors = a.result(place_rows, [(unit, width)] * 3 + [(GROUP, width)])
        outputs, d_inputs = rows_cell.values
    else:
        o_keep, o_send, d_r1, d_branch, vsum = to_mixed(n1, vsum)
        attended = attended_back(att, sums, d_branch, w_out)
        groups = [attention_back(i, 4, vsum, *attended) for i in range(0, HEADS, 4)]
        a_keep = jnp.concatenate([g[1].values[0] for g in groups], axis=-1)
        a_send = jnp.concatenate([g[2][0] for g in groups], axis=-1)
        d_page, *page_parts = inputs_grad(span, hit, out_page, d_r1, w_query, w_key, w_value, [g[0] for g in groups])
        came = [swap(part, i + 1) for i, part in enumerate(page_parts)]
        outputs, d_inputs = page_rows(out_page, d_page, came)

        def parity(keep, send):
            packed = jnp.where(core == 0, jnp.stack([keep, send]), jnp.stack([send, keep]))
            return packed.transpose(1, 2, 0, 3, 4)

        def over(grad):
            part = lax.psum_scatter(grad.astype(F32), "batch", scatter_dimension=0, tiled=True)
            return lax.psum(part.astype(BF), "blk").astype(F32)

        out = parity(o_keep, o_send)
        out = jnp.concatenate([out[p][..., at * GROUP:(at + 1) * GROUP, :] for p, at in OUT_GROUPS], axis=-2)
        out = out.reshape(width, width)
        up = parity(u_keep, u_send)
        down = jnp.concatenate([parity(d_keep, d_send), up[..., unit:, :]], axis=-2)
        down = down.transpose(1, 2, 0, 3, 4).reshape(ff, width)
        up = up[..., :unit, :].transpose(1, 2, 3, 0, 4).reshape(width, ff)
        rows = parity(a_keep, a_send).transpose(1, 2, 0, 3, 4).reshape(PARTS, -1, width)
        mats = [rows[:, i * unit:(i + 1) * unit].reshape(width, width) for i in range(3)]
        vectors = rows[0, 3 * unit:3 * unit + GROUP].astype(F32) + rows[0, 3 * unit + GROUP:].astype(F32)
        vectors = lax.psum(vectors, ("blk", "batch"))
        grad_down, grad_up, grad_out = over(down), over(up), over(out)
        grad_query, grad_key, grad_value = (over(m) for m in mats)
    r = own_vectors(vectors, share, shares)
    return (
        outputs, d_inputs, grad_query, r[B_QUERY], grad_key, grad_value, r[B_VALUE], grad_out, r[B_OUT],
        r[GAIN_ONE], r[SHIFT_ONE], grad_up, r[B_UP], grad_down, r[B_DOWN], r[GAIN_TWO], r[SHIFT_TWO],
    )


def solution(mesh):
    split, whole = P("batch", "blk", None), P()
    rows, vec = P("batch", None), P("batch")
    in_specs = (split, vec, rows, vec, rows) + (whole,) * 16 + (split,)
    out_specs = (split, split, rows, vec, rows, rows, vec, rows, vec, vec, vec, rows, vec, rows, vec, vec, vec)
    return jax.shard_map(body, mesh=mesh, in_specs=in_specs, out_specs=out_specs, check_vma=False)
```
